512 devices in a mesh: gx: 32 (over x, y, core), gy: 16 (over z).
Axes of the slice: x: 4, y: 4, z: 16, core: 2. Of those that a mesh axis runs over, the one named last changes fastest.
Arguments:
- iterate: float32 [512, 32, 2048], P('gx', None, 'gy'), may hold values from -6 to 6
- source: float32 [512, 32, 2048], P('gx', None, 'gy'), may hold values from -8 to 8
- labels: int32 [512, 32, 2048], P('gx', None, 'gy'), may hold values from 0 to 3
Outputs:
- corrected: float32 [512, 32, 2048], P('gx', None, 'gy')
- coarse_correction: float32 [256, 16, 1024], P('gx', 'gy')
The draws below stay inside these ranges and needn't reach their ends.
All inputs are finite; a program needn't handle non-finite values.
Results may differ from the reference program's by a relative error of at most 0.00002.
Values sent between devices are 32-bit elements; how exact they have to be, the bound alone decides.
No kernel may reach another device: no remote copies, remote signals or barrier semaphores. Data moves between devices by JAX's collectives and lax.ppermute only.
A program may use at most 128 MiB of HBM per device.

```python
import jax
import jax.numpy as jnp

NZ = 32
SWEEPS = 4
COARSE_SWEEPS = 16
NX = 512
NY = 2048


def plant(values, own_key, least, largest):
    index_at = [jax.random.randint(jax.random.fold_in(own_key, axis), (), 0, length) for axis, length in enumerate(values.shape)]
    widest = values.shape.index(max(values.shape))
    next_to = index_at[:widest] + [(index_at[widest] + 1) % values.shape[widest]] + index_at[widest + 1:]
    return values.at[tuple(index_at)].set(least).at[tuple(next_to)].set(largest)


def block_scale(key, extent, split, low, top_value):
    factor_of, own = 1.0, jax.random.fold_in(key, 6)
    for position, shards_of in split:
        steps = jnp.exp(jax.random.uniform(jax.random.fold_in(own, position), (shards_of,), jnp.float32, low / len(split), top_value / len(split)))
        factor_of = factor_of * jnp.repeat(steps, extent[position] // shards_of).reshape([-1 if axis == position else 1 for axis in range(len(extent))])
    return factor_of


def gaussian(key, extent, spread, reach, shards=(), held_as=jnp.bfloat16):
    values = spread * jax.random.normal(key, extent, jnp.float32)
    if shards:
        values = values * block_scale(key, extent, shards, -0.22, 0.18)
    return jnp.clip(values, -reach, reach).astype(held_as)


def setup_inputs(seed: int = 0) -> dict:
    arg_keys = jax.random.split(jax.random.key(seed), 4)
    iterate = gaussian(arg_keys[0], (NX, NZ, NY), 1.0, 6.0, ((0, 32), (2, 16)), jnp.float32)
    source = gaussian(arg_keys[1], (NX, NZ, NY), 1.0, 8.0, ((0, 32), (2, 16)), jnp.float32)
    labels = plant(jax.random.randint(arg_keys[2], (NX, NZ, NY), 0, 4), jax.random.fold_in(arg_keys[2], 1), 0, 3).astype(jnp.int32)
    return {"iterate": iterate, "source": source, "labels": labels}


TABLE = (0.5, 1.0, 2.5, 6.0)
LOWER = 0.25
UPPER = 2.0


def conduct(labels):
    total = jnp.zeros(labels.shape, jnp.float32)
    for label_id, value in enumerate(TABLE):
        total = total + jnp.where(labels == label_id, jnp.float32(value), jnp.float32(0.0))
    return total


def neighbours(padded):
    return [padded[2:, 1:-1, 1:-1], padded[:-2, 1:-1, 1:-1],
            padded[1:-1, 2:, 1:-1], padded[1:-1, :-2, 1:-1],
            padded[1:-1, 1:-1, 2:], padded[1:-1, 1:-1, :-2]]


def coefficients(conductance, padded, factor):
    face_coefs = [factor * (conductance + other) for other in neighbours(padded)]
    diagonal = face_coefs[0]
    for extra in face_coefs[1:]:
        diagonal = diagonal + extra
    return face_coefs, diagonal


def apply_op(field, padded, face_coefs):
    total = jnp.zeros(field.shape, jnp.float32)
    for coef, other in zip(face_coefs, neighbours(padded)):
        total = total + coef * (field - other)
    return total


def chebyshev(rhs, inverse, operate, sweeps):
    centre = (UPPER + LOWER) / 2.0
    radius = (UPPER - LOWER) / 2.0
    sigma = centre / radius
    weight = 1.0 / sigma
    remain = rhs
    step = inverse * remain / centre
    solution = step
    for sweep in range(1, sweeps):
        remain = remain - operate(step)
        weight_new = 1.0 / (2.0 * sigma - weight)
        step = (weight_new * weight) * step + (2.0 * weight_new / radius) * inverse * remain
        solution = solution + step
        weight = weight_new
    return solution


def restrict(field):
    shape_in = field.shape
    parts = field.reshape(shape_in[0] // 2, 2, shape_in[1] // 2, 2, shape_in[2] // 2, 2)
    return parts.sum(axis=(1, 3, 5))


def prolong(field):
    shape_in = field.shape
    wide = jnp.broadcast_to(field[:, None, :, None, :, None],
                            (shape_in[0], 2, shape_in[1], 2, shape_in[2], 2))
    return wide.reshape(shape_in[0] * 2, shape_in[1] * 2, shape_in[2] * 2)


def reference(iterate, source, labels):
    conductance = conduct(labels)
    face_coefs, diagonal = coefficients(conductance, jnp.pad(conductance, 1), 0.5)

    def fine_apply(field):
        return apply_op(field, jnp.pad(field, 1), face_coefs)

    residual = source - fine_apply(iterate)
    fine_correction = chebyshev(residual, 1.0 / diagonal, fine_apply, SWEEPS)
    coarse_rhs = restrict(residual)
    coarse_cond = restrict(conductance) / 8.0
    coarse_coefs, coarse_diag = coefficients(coarse_cond, jnp.pad(coarse_cond, 1), 2.0)

    def coarse_apply(field):
        return apply_op(field, jnp.pad(field, 1), coarse_coefs)

    coarse_correction = chebyshev(coarse_rhs, 1.0 / coarse_diag, coarse_apply, COARSE_SWEEPS)
    corrected = iterate + fine_correction + prolong(coarse_correction)
    return corrected, coarse_correction
```

```python
import jax
import jax.numpy as jnp
from jax import lax
from jax.experimental import pallas as pl
from jax.experimental.pallas import tpu as pltpu
from jax.sharding import PartitionSpec as P

SWEEPS = 4
COARSE_SWEEPS = 16
TABLE = (0.5, 1.0, 2.5, 6.0)
LOWER = 0.25
UPPER = 2.0
F32 = jnp.float32

ROWS, NZ, LANES = 16, 32, 128
CROWS, CZ, CLANES = 8, 16, 64
HALO = SWEEPS
EXT = ROWS + 2 * HALO
CEXT = CROWS + 2 * COARSE_SWEEPS


def weights(sweeps):
    centre = (UPPER + LOWER) / 2.0
    radius = (UPPER - LOWER) / 2.0
    sigma = centre / radius
    rho = 1.0 / sigma
    pairs = []
    for _ in range(1, sweeps):
        rho_new = 1.0 / (2.0 * sigma - rho)
        pairs.append((rho_new * rho, 2.0 * rho_new / radius))
        rho = rho_new
    return 1.0 / centre, pairs


def conduct(labels):
    total = jnp.zeros(labels.shape, F32)
    for label_id, value in enumerate(TABLE):
        total = jnp.where(labels == label_id, F32(value), total)
    return total


def roll(x, shift, axis):
    size = x.shape[axis]
    shift = shift % size
    return x if shift == 0 else pltpu.roll(x, shift, axis)


def iota(shape, axis):
    return lax.broadcasted_iota(jnp.int32, shape, axis)


def flux(k_a, k_b, v_a, v_b):
    return 0.5 * (k_a + k_b) * (v_a - v_b)


def dot(a, b):
    return jnp.dot(a, b, precision=lax.Precision.HIGHEST, preferred_element_type=F32)


def residual_kernel(flags, it, src, lab, sib, out, r_ref, k_ref, v_ref, c_ref, up_ref, dn_ref, pool):
    first = flags[0] == 0
    low, high = flags[1].astype(F32), flags[2].astype(F32)
    for i in range(HALO):
        v_ref[i] = jnp.where(first, out[0, i], sib[0, i]) * low
        v_ref[EXT - HALO + i] = jnp.where(first, sib[1, i], out[1, i]) * high
        k_ref[i] = jnp.where(first, out[0, 7 + i], sib[0, 7 + i]) * low
        k_ref[EXT - HALO + i] = jnp.where(first, sib[1, 7 + i], out[1, 7 + i]) * high
    for i in range(ROWS):
        v_ref[HALO + i] = it[i]
        k_ref[HALO + i] = conduct(lab[i])
    z, lane = iota((NZ, LANES), 0), iota((NZ, LANES), 1)
    zero = jnp.zeros((NZ, LANES), F32)
    r_ref[0] = zero
    r_ref[EXT - 1] = zero
    before = flux(k_ref[0], k_ref[1], v_ref[0], v_ref[1])
    for i in range(1, EXT - 1):
        k, v = k_ref[i], v_ref[i]
        if i < HALO:
            s = jnp.where(first, out[0, 3 + i], sib[0, 3 + i]) * low
        elif i < HALO + ROWS:
            s = src[i - HALO]
        else:
            j = 4 + i - HALO - ROWS
            s = jnp.where(first, sib[1, j], out[1, j]) * high
        after = flux(k, k_ref[i + 1], v, v_ref[i + 1])
        fy = jnp.where(lane < LANES - 1, flux(k, roll(k, -1, 1), v, roll(v, -1, 1)), 0.0)
        k_z = jnp.where(z < NZ - 1, roll(k, -1, 0), 0.0)
        v_z = jnp.where(z < NZ - 1, roll(v, -1, 0), 0.0)
        fz = flux(k, k_z, v, v_z)
        fz_in = jnp.where(z > 0, roll(fz, 1, 0), -0.5 * k * v)
        r = s - after + before - fy + roll(fy, 1, 1) - fz + fz_in
        r_ref[i] = r
        before = after
        if HALO <= i < HALO + ROWS:
            j = (i - HALO) // 2
            if i % 2 == 0:
                r_even, k_even = r, k
            else:
                pool[0, j] = r_even + r
                pool[1, j] = k_even + k
    tops = pool[:, :, pl.ds(0, CZ, stride=2), :] + pool[:, :, pl.ds(1, CZ, stride=2), :]
    child, parent = iota((LANES, LANES), 0) // 2, iota((LANES, LANES), 1)
    to_left = jnp.where(child == parent, F32(1.0), F32(0.0))
    to_right = jnp.where(child == parent - CLANES, F32(0.125), F32(0.0))
    coarse = dot(tops[0].reshape(CROWS * CZ, LANES), to_left) + dot(tops[1].reshape(CROWS * CZ, LANES), to_right)
    coarse = coarse.reshape(CROWS, CZ, LANES)
    c_ref[...] = coarse

    for t in range(2):
        up, dn = zero, zero
        for i in range(16 * t, min(16 * t + 16, EXT)):
            k, v, r = k_ref[i], v_ref[i], r_ref[i]
            off = (i % 16) * 8
            here = (lane >= off) & (lane < off + 8)
            top = jnp.where(lane >= 124, k, jnp.where(lane >= 121, roll(r, -4, 1), roll(v, -7, 1)))
            bottom = jnp.where(lane < 4, k, jnp.where(lane < 7, roll(r, 4, 1), roll(v, 7, 1)))
            up = jnp.where(here, roll(top, off - 120, 1), up)
            dn = jnp.where(here, roll(bottom, off, 1), dn)
        up_ref[NZ * t:NZ * (t + 1)] = up
        dn_ref[NZ * t:NZ * (t + 1)] = dn
    lane = iota((CZ, LANES), 1)
    for t in range(2):
        up = dn = jnp.zeros((CZ, LANES), F32)
        for j in range(4 * t, 4 * t + 4):
            row = coarse[j]
            off = (j % 4) * 32
            at_r = (lane >= off) & (lane < off + 16)
            at_k = (lane >= off + 16) & (lane < off + 32)
            up = jnp.where(at_r, roll(row, off - 48, 1), jnp.where(at_k, roll(row, off + 16 - 112, 1), up))
            dn = jnp.where(at_r, roll(row, off, 1), jnp.where(at_k, roll(row, off + 16 - 64, 1), dn))
        up_ref[2 * NZ + CZ * t:2 * NZ + CZ * (t + 1)] = up
        dn_ref[2 * NZ + CZ * t:2 * NZ + CZ * (t + 1)] = dn


def strip_flux(up, dn):
    lane = iota(up.shape, 1)
    face = flux(roll(up, -7, 1), dn, up, roll(dn, -7, 1))
    return jnp.where(lane % 8 == 0, face, 0.0)


def coarse_kernel(c_ref, ou, od, ru, rd, o_ref, pool):
    for n, (a, b) in enumerate(((ou, rd), (ru, od))):
        face = strip_flux(a[0:2 * NZ], b[0:2 * NZ])
        pool[n] = face + roll(face, -8, 1)
    sums = pool[:, pl.ds(0, NZ, stride=2), :] + pool[:, pl.ds(1, NZ, stride=2), :]
    lane = iota((CZ, LANES), 1)
    for j in range(CROWS):
        e = HALO + 2 * j
        rows = slice(CZ * (e // 16), CZ * (e // 16) + CZ)
        src = (e % 16) * 8
        right, left = sums[0, rows], sums[1, rows]
        own = c_ref[j]
        strip = slice(2 * NZ + CZ * (j // 4), 2 * NZ + CZ * (j // 4) + CZ)
        off = (j % 4) * 32
        up, dn = ru[strip], rd[strip]
        for n in range(2):
            value = jnp.where(lane < 64, roll(own, -64 * n, 1), 0.0)
            value = jnp.where((lane >= 64) & (lane < 80), roll(dn, 64 - off - 16 * n, 1), value)
            value = jnp.where(lane >= 112, roll(up, 112 - off - 16 * n, 1), value)
            if n == 0:
                value = value - jnp.where(lane == 63, roll(right, 63 - src, 1), 0.0)
                value = value + jnp.where(lane == 64, roll(right, 64 - src, 1), 0.0)
                value = value - jnp.where(lane == 127, roll(left, 127 - src, 1), 0.0)
                value = value + jnp.where(lane == 0, roll(left, -src, 1), 0.0)
            o_ref[n, j] = value


def coarse_solve_kernel(flags, pair, out, relay, o_ref, k_s, r_s, s_s, x_s, c_s):
    first = flags[0] == 0
    low, high = flags[3].astype(F32), flags[4].astype(F32)
    for n, dest in enumerate((r_s, k_s)):
        for j in range(CROWS):
            dest[j] = jnp.where(first, out[0, 0, n, j], relay[0, n, j]) * low
            dest[8 + j] = jnp.where(first, out[0, 1, n, j] * low, pair[0, n, j])
            dest[16 + j] = jnp.where(first, pair[0, n, j], pair[1, n, j])
            dest[24 + j] = jnp.where(first, pair[1, n, j], out[1, 0, n, j] * high)
            dest[32 + j] = jnp.where(first, relay[1, n, j], out[1, 1, n, j]) * high
    z = iota((CZ, LANES), 0)
    start, pairs = weights(COARSE_SWEEPS)
    zero = jnp.zeros((CZ, LANES), F32)
    s_s[0] = zero
    s_s[CEXT - 1] = zero
    below = 2.0 * (k_s[0] + k_s[1])
    for i in range(1, CEXT - 1):
        k = k_s[i]
        above = 2.0 * (k + k_s[i + 1])
        z_up = 2.0 * (k + jnp.where(z < CZ - 1, roll(k, -1, 0), 0.0))
        z_dn = 2.0 * (k + jnp.where(z > 0, roll(k, 1, 0), 0.0))
        y_up = 2.0 * (k + roll(k, -1, 1))
        y_dn = 2.0 * (k + roll(k, 1, 1))
        diagonal = above + below + z_up + z_dn + y_up + y_dn
        inverse = jnp.where(k > 0, 1.0 / jnp.where(k > 0, diagonal, 1.0), 0.0)
        c_s[0, i] = inverse * above
        c_s[1, i] = inverse * below
        c_s[2, i] = jnp.where(z < CZ - 1, inverse * z_up, 0.0)
        c_s[3, i] = jnp.where(z > 0, inverse * z_dn, 0.0)
        c_s[4, i] = inverse * y_up
        c_s[5, i] = inverse * y_dn
        r = inverse * r_s[i]
        r_s[i] = r
        s_s[i] = r * start
        if 16 <= i < 24:
            x_s[i - 16] = r * start
        below = above
    for n in range(1, COARSE_SWEEPS):
        keep, add = pairs[n - 1]
        prev, here = s_s[n], s_s[n + 1]
        for i in range(n + 1, CEXT - 1 - n):
            ahead = s_s[i + 1]
            total = c_s[0, i] * ahead + c_s[1, i] * prev
            total = total + c_s[2, i] * roll(here, -1, 0) + c_s[3, i] * roll(here, 1, 0)
            total = total + c_s[4, i] * roll(here, -1, 1) + c_s[5, i] * roll(here, 1, 1)
            r = r_s[i] - (here - total)
            step = keep * here + add * r
            r_s[i] = r
            s_s[i] = step
            if 16 <= i < 24:
                x_s[i - 16] = x_s[i - 16] + step
            prev, here = here, ahead
    o_ref[...] = x_s[...]


def fine_kernel(it, r_ref, k_ref, ou, od, ru, rd, x_ref, o_ref, k_s, r_s, s_s, x_s, c_s, p_s):
    lane = iota((NZ, LANES), 1)
    right = strip_flux(ou[0:2 * NZ], rd[0:2 * NZ])
    left = strip_flux(ru[0:2 * NZ], od[0:2 * NZ])
    dn = rd[0:2 * NZ] + roll(right, 4, 1)
    up = ru[0:2 * NZ] - roll(left, 3, 1)
    for i in range(EXT):
        t = slice(NZ * (i // 16), NZ * (i // 16) + NZ)
        off = (i % 16) * 8
        k_s[i, :, 0:LANES] = k_ref[i]
        k_s[i, :, LANES:] = jnp.where(lane < 4, roll(dn[t], -off, 1), jnp.where(lane >= 124, roll(up[t], 120 - off, 1), 0.0))
        r = r_ref[i] - jnp.where(lane == 127, roll(right[t], 127 - off, 1), 0.0)
        r_s[i, :, 0:LANES] = r + jnp.where(lane == 0, roll(left[t], -off, 1), 0.0)
        r_s[i, :, LANES:] = jnp.where(
            lane < 3, roll(dn[t], -off - 4, 1), jnp.where(lane >= 125, roll(up[t], 124 - off, 1), 0.0)
        )
    z = iota((NZ, 2 * LANES), 0)
    start, pairs = weights(SWEEPS)
    zero = jnp.zeros((NZ, 2 * LANES), F32)
    s_s[0] = zero
    s_s[EXT - 1] = zero
    below = 0.5 * (k_s[0] + k_s[1])
    for i in range(1, EXT - 1):
        k = k_s[i]
        above = 0.5 * (k + k_s[i + 1])
        z_up = 0.5 * (k + jnp.where(z < NZ - 1, roll(k, -1, 0), 0.0))
        z_dn = 0.5 * (k + jnp.where(z > 0, roll(k, 1, 0), 0.0))
        y_up = 0.5 * (k + roll(k, -1, 1))
        y_dn = 0.5 * (k + roll(k, 1, 1))
        diagonal = above + below + z_up + z_dn + y_up + y_dn
        inverse = jnp.where(k > 0, 1.0 / jnp.where(k > 0, diagonal, 1.0), 0.0)
        c_s[0, i] = inverse * above
        c_s[1, i] = inverse * below
        c_s[2, i] = jnp.where(z < NZ - 1, inverse * z_up, 0.0)
        c_s[3, i] = jnp.where(z > 0, inverse * z_dn, 0.0)
        c_s[4, i] = inverse * y_up
        c_s[5, i] = inverse * y_dn
        r = inverse * r_s[i]
        r_s[i] = r
        s_s[i] = r * start
        if HALO <= i < HALO + ROWS:
            x_s[i - HALO] = r[:, 0:LANES] * start
        below = above
    for n in range(1, SWEEPS):
        keep, add = pairs[n - 1]
        prev, here = s_s[n], s_s[n + 1]
        for i in range(n + 1, EXT - 1 - n):
            ahead = s_s[i + 1]
            total = c_s[0, i] * ahead + c_s[1, i] * prev
            total = total + c_s[2, i] * roll(here, -1, 0) + c_s[3, i] * roll(here, 1, 0)
            total = total + c_s[4, i] * roll(here, -1, 1) + c_s[5, i] * roll(here, 1, 1)
            r = r_s[i] - (here - total)
            step = keep * here + add * r
            r_s[i] = r
            s_s[i] = step
            if HALO <= i < HALO + ROWS:
                x_s[i - HALO] = x_s[i - HALO] + step[:, 0:LANES]
            prev, here = here, ahead
    child, parent = iota((LANES, LANES), 1) // 2, iota((LANES, LANES), 0)
    spread = jnp.where(child == parent, F32(1.0), F32(0.0))
    wide = dot(x_ref[...].reshape(CROWS * CZ, LANES), spread).reshape(CROWS, CZ, LANES)
    p_s[:, pl.ds(0, CZ, stride=2), :] = wide
    p_s[:, pl.ds(1, CZ, stride=2), :] = wide
    for i in range(ROWS):
        o_ref[i] = it[i] + x_s[i] + p_s[i // 2]


def call(kernel, outs, scratch, in_smem=False, operands=(), flops=1000000):
    vmem = pl.BlockSpec(memory_space=pltpu.VMEM)
    specs = [vmem] * len(operands)
    if in_smem:
        specs[0] = pl.BlockSpec(memory_space=pltpu.SMEM)
    size = sum(4 * x.size for x in operands) + sum(4 * o.size for o in outs)
    multiple = len(outs) > 1
    return pl.pallas_call(
        kernel,
        out_shape=outs if multiple else outs[0],
        in_specs=specs,
        out_specs=[vmem] * len(outs) if multiple else vmem,
        scratch_shapes=[pltpu.VMEM(s, F32) for s in scratch],
        compiler_params=pltpu.CompilerParams(vmem_limit_bytes=40 * 1024 * 1024),
        cost_estimate=pl.CostEstimate(flops=flops, bytes_accessed=size, transcendentals=0),
    )(*operands)


def shape(*dims):
    return jax.ShapeDtypeStruct(dims, F32)


def on_device(iterate, source, labels):
    n_gx, n_gy = lax.axis_size("gx"), lax.axis_size("gy")
    gx = lax.axis_index("gx")
    first = gx % 2 == 0
    flags = jnp.stack([gx % 2, gx > 0, gx < n_gx - 1, gx > 1, gx < n_gx - 2]).astype(jnp.int32)
    chips = [[i, i + 1] for i in range(0, n_gx, 2)]
    between = [[i, (i + 1) % n_gx] for i in range(1, n_gx, 2)]

    lower = jnp.concatenate([iterate[:4], source[:3], conduct(labels[:4])])
    upper = jnp.concatenate([iterate[-4:], source[-3:], conduct(labels[-4:])])
    sib = lax.all_gather(jnp.where(first, upper, lower), "gx", axis_index_groups=chips)
    out = lax.all_gather(jnp.where(first, lower, upper), "gx", axis_index_groups=between)
    full = shape(EXT, NZ, LANES)
    strip = shape(2 * NZ + 2 * CZ, LANES)
    resid, cond, _, coarse, up, dn = call(
        residual_kernel,
        [full, full, full, shape(CROWS, CZ, LANES), strip, strip],
        [(2, CROWS, NZ, LANES)],
        True,
        (flags, iterate, source, labels, sib, out),
    )
    onward = [(i, i + 1) for i in range(n_gy - 1)]
    back = [(i + 1, i) for i in range(n_gy - 1)]
    from_left = lax.ppermute(up, "gy", onward)
    from_right = lax.ppermute(dn, "gy", back)
    block = call(
        coarse_kernel,
        [shape(2, CROWS, CZ, LANES)],
        [(2, 2 * NZ, LANES)],
        False,
        (coarse, up, dn, from_left, from_right),
    )
    pair = lax.all_gather(block, "gx", axis_index_groups=chips)
    beyond = lax.all_gather(pair, "gx", axis_index_groups=between)
    near = jnp.where(first, beyond[0, 1], beyond[1, 0])
    relay = lax.all_gather(near, "gx", axis_index_groups=chips)
    rows = (CEXT, CZ, LANES)
    coarse_out = call(
        coarse_solve_kernel,
        [shape(CROWS, CZ, LANES)],
        [rows, rows, rows, (CROWS, CZ, LANES), (6, *rows)],
        True,
        (flags, pair, beyond, relay),
    )
    owned = lax.all_to_all(coarse_out[:, :, :CLANES], "gy", split_axis=1, concat_axis=2, tiled=True)
    wide = (EXT, NZ, 2 * LANES)
    corrected = call(
        fine_kernel,
        [shape(ROWS, NZ, LANES)],
        [wide, wide, wide, (ROWS, NZ, LANES), (6, *wide), (CROWS, NZ, LANES)],
        False,
        (iterate, resid, cond, up, dn, from_left, from_right, coarse_out),
        flops=20000000,
    )
    return corrected, owned


def solution(mesh):
    spec = P("gx", None, "gy")
    return jax.shard_map(
        on_device, mesh=mesh, in_specs=(spec, spec, spec), out_specs=(spec, P("gx", "gy", None)), check_vma=False
    )
```

```python
import functools

import jax
import jax.numpy as jnp
from jax import lax
from jax.experimental import pallas as pl
from jax.experimental.pallas import tpu as pltpu
from jax.sharding import PartitionSpec as P

SWEEPS = 4
COARSE_SWEEPS = 16
TABLE = (0.5, 1.0, 2.5, 6.0)
LOWER = 0.25
UPPER = 2.0
F32 = jnp.float32

ROWS, NZ, LANES = 16, 32, 128
CROWS, CZ, CLANES = 8, 16, 64
HALO = SWEEPS
EXT = ROWS + 2 * HALO
CEXT = CROWS + 2 * COARSE_SWEEPS


def weights(sweeps):
    centre = (UPPER + LOWER) / 2.0
    radius = (UPPER - LOWER) / 2.0
    sigma = centre / radius
    rho = 1.0 / sigma
    pairs = []
    for _ in range(1, sweeps):
        rho_new = 1.0 / (2.0 * sigma - rho)
        pairs.append((rho_new * rho, 2.0 * rho_new / radius))
        rho = rho_new
    return 1.0 / centre, pairs


def conduct(labels):
    total = jnp.zeros(labels.shape, F32)
    for label_id, value in enumerate(TABLE):
        total = jnp.where(labels == label_id, F32(value), total)
    return total


def roll(x, shift, axis):
    size = x.shape[axis]
    shift = shift % size
    return x if shift == 0 else pltpu.roll(x, shift, axis)


def iota(shape, axis):
    return lax.broadcasted_iota(jnp.int32, shape, axis)


def flux(k_a, k_b, v_a, v_b):
    return 0.5 * (k_a + k_b) * (v_a - v_b)


def dot(a, b):
    return jnp.dot(a, b, precision=lax.Precision.HIGHEST, preferred_element_type=F32)


def residual_kernel(flags, it, src, lab, sib, out, r_ref, k_ref, v_ref, c_ref, up_ref, dn_ref, pool):
    first = flags[0] == 0
    low, high = flags[1].astype(F32), flags[2].astype(F32)
    for i in range(HALO):
        v_ref[i] = jnp.where(first, out[0, i], sib[0, i]) * low
        v_ref[EXT - HALO + i] = jnp.where(first, sib[1, i], out[1, i]) * high
        k_ref[i] = jnp.where(first, out[0, 7 + i], sib[0, 7 + i]) * low
        k_ref[EXT - HALO + i] = jnp.where(first, sib[1, 7 + i], out[1, 7 + i]) * high
    for i in range(ROWS):
        v_ref[HALO + i] = it[i]
        k_ref[HALO + i] = conduct(lab[i])
    z, lane = iota((NZ, LANES), 0), iota((NZ, LANES), 1)
    zero = jnp.zeros((NZ, LANES), F32)
    r_ref[0] = zero
    r_ref[EXT - 1] = zero
    before = flux(k_ref[0], k_ref[1], v_ref[0], v_ref[1])
    for i in range(1, EXT - 1):
        k, v = k_ref[i], v_ref[i]
        if i < HALO:
            s = jnp.where(first, out[0, 3 + i], sib[0, 3 + i]) * low
        elif i < HALO + ROWS:
            s = src[i - HALO]
        else:
            j = 4 + i - HALO - ROWS
            s = jnp.where(first, sib[1, j], out[1, j]) * high
        after = flux(k, k_ref[i + 1], v, v_ref[i + 1])
        fy = jnp.where(lane < LANES - 1, flux(k, roll(k, -1, 1), v, roll(v, -1, 1)), 0.0)
        k_z = jnp.where(z < NZ - 1, roll(k, -1, 0), 0.0)
        v_z = jnp.where(z < NZ - 1, roll(v, -1, 0), 0.0)
        fz = flux(k, k_z, v, v_z)
        fz_in = jnp.where(z > 0, roll(fz, 1, 0), -0.5 * k * v)
        r = s - after + before - fy + roll(fy, 1, 1) - fz + fz_in
        r_ref[i] = r
        before = after
        if HALO <= i < HALO + ROWS:
            j = (i - HALO) // 2
            if i % 2 == 0:
                r_even, k_even = r, k
            else:
                pool[0, j] = r_even + r
                pool[1, j] = k_even + k
    tops = pool[:, :, pl.ds(0, CZ, stride=2), :] + pool[:, :, pl.ds(1, CZ, stride=2), :]
    child, parent = iota((LANES, LANES), 0) // 2, iota((LANES, LANES), 1)
    to_left = jnp.where(child == parent, F32(1.0), F32(0.0))
    to_right = jnp.where(child == parent - CLANES, F32(0.125), F32(0.0))
    coarse = dot(tops[0].reshape(CROWS * CZ, LANES), to_left) + dot(tops[1].reshape(CROWS * CZ, LANES), to_right)
    coarse = coarse.reshape(CROWS, CZ, LANES)
    c_ref[...] = coarse

    for t in range(2):
        up, dn = zero, zero
        for i in range(16 * t, min(16 * t + 16, EXT)):
            k, v, r = k_ref[i], v_ref[i], r_ref[i]
            off = (i % 16) * 8
            here = (lane >= off) & (lane < off + 8)
            top = jnp.where(lane >= 124, k, jnp.where(lane >= 121, roll(r, -4, 1), roll(v, -7, 1)))
            bottom = jnp.where(lane < 4, k, jnp.where(lane < 7, roll(r, 4, 1), roll(v, 7, 1)))
            up = jnp.where(here, roll(top, off - 120, 1), up)
            dn = jnp.where(here, roll(bottom, off, 1), dn)
        up_ref[NZ * t:NZ * (t + 1)] = up
        dn_ref[NZ * t:NZ * (t + 1)] = dn
    lane = iota((CZ, LANES), 1)
    for t in range(2):
        up = dn = jnp.zeros((CZ, LANES), F32)
        for j in range(4 * t, 4 * t + 4):
            row = coarse[j]
            off = (j % 4) * 32
            at_r = (lane >= off) & (lane < off + 16)
            at_k = (lane >= off + 16) & (lane < off + 32)
            up = jnp.where(at_r, roll(row, off - 48, 1), jnp.where(at_k, roll(row, off + 16 - 112, 1), up))
            dn = jnp.where(at_r, roll(row, off, 1), jnp.where(at_k, roll(row, off + 16 - 64, 1), dn))
        up_ref[2 * NZ + CZ * t:2 * NZ + CZ * (t + 1)] = up
        dn_ref[2 * NZ + CZ * t:2 * NZ + CZ * (t + 1)] = dn


def strip_flux(up, dn):
    lane = iota(up.shape, 1)
    face = flux(roll(up, -7, 1), dn, up, roll(dn, -7, 1))
    return jnp.where(lane % 8 == 0, face, 0.0)


def coarse_kernel(c_ref, ou, od, ru, rd, o_ref, pool):
    for n, (a, b) in enumerate(((ou, rd), (ru, od))):
        face = strip_flux(a[0:2 * NZ], b[0:2 * NZ])
        pool[n] = face + roll(face, -8, 1)
    sums = pool[:, pl.ds(0, NZ, stride=2), :] + pool[:, pl.ds(1, NZ, stride=2), :]
    lane = iota((CZ, LANES), 1)
    for j in range(CROWS):
        e = HALO + 2 * j
        rows = slice(CZ * (e // 16), CZ * (e // 16) + CZ)
        src = (e % 16) * 8
        right, left = sums[0, rows], sums[1, rows]
        own = c_ref[j]
        strip = slice(2 * NZ + CZ * (j // 4), 2 * NZ + CZ * (j // 4) + CZ)
        off = (j % 4) * 32
        up, dn = ru[strip], rd[strip]
        for n in range(2):
            value = jnp.where(lane < 64, roll(own, -64 * n, 1), 0.0)
            value = jnp.where((lane >= 64) & (lane < 80), roll(dn, 64 - off - 16 * n, 1), value)
            value = jnp.where(lane >= 112, roll(up, 112 - off - 16 * n, 1), value)
            if n == 0:
                value = value - jnp.where(lane == 63, roll(right, 63 - src, 1), 0.0)
                value = value + jnp.where(lane == 64, roll(right, 64 - src, 1), 0.0)
                value = value - jnp.where(lane == 127, roll(left, 127 - src, 1), 0.0)
                value = value + jnp.where(lane == 0, roll(left, -src, 1), 0.0)
            o_ref[n, j] = value


def coarse_solve_kernel(flags, pair, out, relay, o_ref, p_ref, k_s, r_s, s_s, x_s, c_s):
    first = flags[0] == 0
    low, high = flags[3].astype(F32), flags[4].astype(F32)
    for n, dest in enumerate((r_s, k_s)):
        for j in range(CROWS):
            dest[j] = jnp.where(first, out[0, 0, n, j], relay[0, n, j]) * low
            dest[8 + j] = jnp.where(first, out[0, 1, n, j] * low, pair[0, n, j])
            dest[16 + j] = jnp.where(first, pair[0, n, j], pair[1, n, j])
            dest[24 + j] = jnp.where(first, pair[1, n, j], out[1, 0, n, j] * high)
            dest[32 + j] = jnp.where(first, relay[1, n, j], out[1, 1, n, j]) * high
    z = iota((CZ, LANES), 0)
    start, pairs = weights(COARSE_SWEEPS)
    zero = jnp.zeros((CZ, LANES), F32)
    s_s[0] = zero
    s_s[CEXT - 1] = zero
    below = 2.0 * (k_s[0] + k_s[1])
    for i in range(1, CEXT - 1):
        k = k_s[i]
        above = 2.0 * (k + k_s[i + 1])
        z_up = 2.0 * (k + jnp.where(z < CZ - 1, roll(k, -1, 0), 0.0))
        z_dn = 2.0 * (k + jnp.where(z > 0, roll(k, 1, 0), 0.0))
        y_up = 2.0 * (k + roll(k, -1, 1))
        y_dn = 2.0 * (k + roll(k, 1, 1))
        diagonal = above + below + z_up + z_dn + y_up + y_dn
        inverse = jnp.where(k > 0, 1.0 / jnp.where(k > 0, diagonal, 1.0), 0.0)
        c_s[0, i] = inverse * above
        c_s[1, i] = inverse * below
        c_s[2, i] = jnp.where(z < CZ - 1, inverse * z_up, 0.0)
        c_s[3, i] = jnp.where(z > 0, inverse * z_dn, 0.0)
        c_s[4, i] = inverse * y_up
        c_s[5, i] = inverse * y_dn
        r = inverse * r_s[i]
        r_s[i] = r
        s_s[i] = r * start
        if 16 <= i < 24:
            x_s[i - 16] = r * start
        below = above
    for n in range(1, COARSE_SWEEPS):
        keep, add = pairs[n - 1]
        prev, here = s_s[n], s_s[n + 1]
        for i in range(n + 1, CEXT - 1 - n):
            ahead = s_s[i + 1]
            total = c_s[0, i] * ahead + c_s[1, i] * prev
            total = total + c_s[2, i] * roll(here, -1, 0) + c_s[3, i] * roll(here, 1, 0)
            total = total + c_s[4, i] * roll(here, -1, 1) + c_s[5, i] * roll(here, 1, 1)
            r = r_s[i] - (here - total)
            step = keep * here + add * r
            r_s[i] = r
            s_s[i] = step
            if 16 <= i < 24:
                x_s[i - 16] = x_s[i - 16] + step
            prev, here = here, ahead
    o_ref[...] = x_s[...]
    lane = iota((CZ, LANES), 1)
    for a in range(4):
        p_ref[pl.ds(a, CZ, stride=4), :] = jnp.where(lane < CLANES, x_s[a], roll(x_s[a + 4], CLANES, 1))


def planes_kernel(sources, planes, p_ref, o_ref):
    half = sources // 2
    lane = iota((half, LANES), 1)
    for q in range(planes):
        for a in range(4):
            even = p_ref[pl.ds(4 * q + a, half, stride=8 * planes), :]
            odd = p_ref[pl.ds(4 * (planes + q) + a, half, stride=8 * planes), :]
            to = (a * planes + q) * half
            o_ref[to:to + half] = jnp.where(lane < CLANES, even, roll(odd, CLANES, 1))
            to = ((a + 4) * planes + q) * half
            o_ref[to:to + half] = jnp.where(lane < CLANES, roll(even, CLANES, 1), odd)


def fine_kernel(it, r_ref, k_ref, ou, od, ru, rd, x_ref, o_ref, k_s, r_s, s_s, x_s, c_s, p_s):
    lane = iota((NZ, LANES), 1)
    right = strip_flux(ou[0:2 * NZ], rd[0:2 * NZ])
    left = strip_flux(ru[0:2 * NZ], od[0:2 * NZ])
    dn = rd[0:2 * NZ] + roll(right, 4, 1)
    up = ru[0:2 * NZ] - roll(left, 3, 1)
    for i in range(EXT):
        t = slice(NZ * (i // 16), NZ * (i // 16) + NZ)
        off = (i % 16) * 8
        k_s[i, :, 0:LANES] = k_ref[i]
        k_s[i, :, LANES:] = jnp.where(lane < 4, roll(dn[t], -off, 1), jnp.where(lane >= 124, roll(up[t], 120 - off, 1), 0.0))
        r = r_ref[i] - jnp.where(lane == 127, roll(right[t], 127 - off, 1), 0.0)
        r_s[i, :, 0:LANES] = r + jnp.where(lane == 0, roll(left[t], -off, 1), 0.0)
        r_s[i, :, LANES:] = jnp.where(
            lane < 3, roll(dn[t], -off - 4, 1), jnp.where(lane >= 125, roll(up[t], 124 - off, 1), 0.0)
        )
    z = iota((NZ, 2 * LANES), 0)
    start, pairs = weights(SWEEPS)
    zero = jnp.zeros((NZ, 2 * LANES), F32)
    s_s[0] = zero
    s_s[EXT - 1] = zero
    below = 0.5 * (k_s[0] + k_s[1])
    for i in range(1, EXT - 1):
        k = k_s[i]
        above = 0.5 * (k + k_s[i + 1])
        z_up = 0.5 * (k + jnp.where(z < NZ - 1, roll(k, -1, 0), 0.0))
        z_dn = 0.5 * (k + jnp.where(z > 0, roll(k, 1, 0), 0.0))
        y_up = 0.5 * (k + roll(k, -1, 1))
        y_dn = 0.5 * (k + roll(k, 1, 1))
        diagonal = above + below + z_up + z_dn + y_up + y_dn
        inverse = jnp.where(k > 0, 1.0 / jnp.where(k > 0, diagonal, 1.0), 0.0)
        c_s[0, i] = inverse * above
        c_s[1, i] = inverse * below
        c_s[2, i] = jnp.where(z < NZ - 1, inverse * z_up, 0.0)
        c_s[3, i] = jnp.where(z > 0, inverse * z_dn, 0.0)
        c_s[4, i] = inverse * y_up
        c_s[5, i] = inverse * y_dn
        r = inverse * r_s[i]
        r_s[i] = r
        s_s[i] = r * start
        if HALO <= i < HALO + ROWS:
            x_s[i - HALO] = r[:, 0:LANES] * start
        below = above
    for n in range(1, SWEEPS):
        keep, add = pairs[n - 1]
        prev, here = s_s[n], s_s[n + 1]
        for i in range(n + 1, EXT - 1 - n):
            ahead = s_s[i + 1]
            total = c_s[0, i] * ahead + c_s[1, i] * prev
            total = total + c_s[2, i] * roll(here, -1, 0) + c_s[3, i] * roll(here, 1, 0)
            total = total + c_s[4, i] * roll(here, -1, 1) + c_s[5, i] * roll(here, 1, 1)
            r = r_s[i] - (here - total)
            step = keep * here + add * r
            r_s[i] = r
            s_s[i] = step
            if HALO <= i < HALO + ROWS:
                x_s[i - HALO] = x_s[i - HALO] + step[:, 0:LANES]
            prev, here = here, ahead
    child, parent = iota((LANES, LANES), 1) // 2, iota((LANES, LANES), 0)
    spread = jnp.where(child == parent, F32(1.0), F32(0.0))
    wide = dot(x_ref[...].reshape(CROWS * CZ, LANES), spread).reshape(CROWS, CZ, LANES)
    p_s[:, pl.ds(0, CZ, stride=2), :] = wide
    p_s[:, pl.ds(1, CZ, stride=2), :] = wide
    for i in range(ROWS):
        o_ref[i] = it[i] + x_s[i] + p_s[i // 2]


def call(kernel, outs, scratch, in_smem=False, operands=(), flops=1000000):
    vmem = pl.BlockSpec(memory_space=pltpu.VMEM)
    specs = [vmem] * len(operands)
    if in_smem:
        specs[0] = pl.BlockSpec(memory_space=pltpu.SMEM)
    size = sum(4 * x.size for x in operands) + sum(4 * o.size for o in outs)
    multiple = len(outs) > 1
    return pl.pallas_call(
        kernel,
        out_shape=outs if multiple else outs[0],
        in_specs=specs,
        out_specs=[vmem] * len(outs) if multiple else vmem,
        scratch_shapes=[pltpu.VMEM(s, F32) for s in scratch],
        compiler_params=pltpu.CompilerParams(vmem_limit_bytes=40 * 1024 * 1024),
        cost_estimate=pl.CostEstimate(flops=flops, bytes_accessed=size, transcendentals=0),
    )(*operands)


def shape(*dims):
    return jax.ShapeDtypeStruct(dims, F32)


def on_device(iterate, source, labels):
    n_gx, n_gy = lax.axis_size("gx"), lax.axis_size("gy")
    gx = lax.axis_index("gx")
    first = gx % 2 == 0
    flags = jnp.stack([gx % 2, gx > 0, gx < n_gx - 1, gx > 1, gx < n_gx - 2]).astype(jnp.int32)
    chips = [[i, i + 1] for i in range(0, n_gx, 2)]
    between = [[i, (i + 1) % n_gx] for i in range(1, n_gx, 2)]

    lower = jnp.concatenate([iterate[:4], source[:3], conduct(labels[:4])])
    upper = jnp.concatenate([iterate[-4:], source[-3:], conduct(labels[-4:])])
    sib = lax.all_gather(jnp.where(first, upper, lower), "gx", axis_index_groups=chips)
    out = lax.all_gather(jnp.where(first, lower, upper), "gx", axis_index_groups=between)
    full = shape(EXT, NZ, LANES)
    strip = shape(2 * NZ + 2 * CZ, LANES)
    resid, cond, _, coarse, up, dn = call(
        residual_kernel,
        [full, full, full, shape(CROWS, CZ, LANES), strip, strip],
        [(2, CROWS, NZ, LANES)],
        True,
        (flags, iterate, source, labels, sib, out),
    )
    onward = [(i, i + 1) for i in range(n_gy - 1)]
    back = [(i + 1, i) for i in range(n_gy - 1)]
    from_left = lax.ppermute(up, "gy", onward)
    from_right = lax.ppermute(dn, "gy", back)
    block = call(
        coarse_kernel,
        [shape(2, CROWS, CZ, LANES)],
        [(2, 2 * NZ, LANES)],
        False,
        (coarse, up, dn, from_left, from_right),
    )
    pair = lax.all_gather(block, "gx", axis_index_groups=chips)
    beyond = lax.all_gather(pair, "gx", axis_index_groups=between)
    near = jnp.where(first, beyond[0, 1], beyond[1, 0])
    relay = lax.all_gather(near, "gx", axis_index_groups=chips)
    rows = (CEXT, CZ, LANES)
    coarse_out, planes = call(
        coarse_solve_kernel,
        [shape(CROWS, CZ, LANES), shape(4 * CZ, LANES)],
        [rows, rows, rows, (CROWS, CZ, LANES), (6, *rows)],
        True,
        (flags, pair, beyond, relay),
    )
    per = CZ // n_gy
    planes = lax.all_to_all(planes.reshape(n_gy, 4 * per, LANES), "gy", split_axis=0, concat_axis=0, tiled=True)
    wide = (EXT, NZ, 2 * LANES)
    corrected = call(
        fine_kernel,
        [shape(ROWS, NZ, LANES)],
        [wide, wide, wide, (ROWS, NZ, LANES), (6, *wide), (CROWS, NZ, LANES)],
        False,
        (iterate, resid, cond, up, dn, from_left, from_right, coarse_out),
        flops=20000000,
    )
    owned = call(
        functools.partial(planes_kernel, n_gy, per),
        [shape(4 * CZ, LANES)],
        [],
        False,
        (planes.reshape(4 * CZ, LANES),),
    ).reshape(CROWS, per, CLANES * n_gy)
    return corrected, owned


def solution(mesh):
    spec = P("gx", None, "gy")
    return jax.shard_map(
        on_device, mesh=mesh, in_specs=(spec, spec, spec), out_specs=(spec, P("gx", "gy", None)), check_vma=False
    )
```

```python
import functools

import jax
import jax.numpy as jnp
from jax import lax
from jax.experimental import pallas as pl
from jax.experimental.pallas import tpu as pltpu
from jax.sharding import PartitionSpec as P

SWEEPS = 4
COARSE_SWEEPS = 16
TABLE = (0.5, 1.0, 2.5, 6.0)
LOWER = 0.25
UPPER = 2.0
F32 = jnp.float32

ROWS, NZ, LANES = 16, 32, 128
CROWS, CZ, CLANES = 8, 16, 64
HALO = SWEEPS
EXT = ROWS + 2 * HALO
CEXT = CROWS + 2 * COARSE_SWEEPS
BLOCK = CROWS * CZ


def weights(sweeps):
    centre = (UPPER + LOWER) / 2.0
    radius = (UPPER - LOWER) / 2.0
    sigma = centre / radius
    rho = 1.0 / sigma
    pairs = []
    for _ in range(1, sweeps):
        rho_new = 1.0 / (2.0 * sigma - rho)
        pairs.append((rho_new * rho, 2.0 * rho_new / radius))
        rho = rho_new
    return 1.0 / centre, pairs


def conduct(labels):
    total = jnp.zeros(labels.shape, F32)
    for label_id, value in enumerate(TABLE):
        total = jnp.where(labels == label_id, F32(value), total)
    return total


def roll(x, shift, axis):
    size = x.shape[axis]
    shift = shift % size
    return x if shift == 0 else pltpu.roll(x, shift, axis)


def iota(shape, axis):
    return lax.broadcasted_iota(jnp.int32, shape, axis)


def flux(k_a, k_b, v_a, v_b):
    return 0.5 * (k_a + k_b) * (v_a - v_b)


def dot(a, b):
    return jnp.dot(a, b, precision=lax.Precision.HIGHEST, preferred_element_type=F32)


def residual_kernel(it, src, lab, r_ref, k_ref, c_ref, up_ref, dn_ref, pool):
    for i in range(ROWS):
        k_ref[i] = conduct(lab[i])
    z, lane = iota((NZ, LANES), 0), iota((NZ, LANES), 1)
    zero = jnp.zeros((NZ, LANES), F32)
    before = zero
    up = dn = zero
    for i in range(ROWS):
        k, v = k_ref[i], it[i]
        after = flux(k, k_ref[i + 1], v, it[i + 1]) if i < ROWS - 1 else zero
        fy = jnp.where(lane < LANES - 1, flux(k, roll(k, -1, 1), v, roll(v, -1, 1)), 0.0)
        k_z = jnp.where(z < NZ - 1, roll(k, -1, 0), 0.0)
        v_z = jnp.where(z < NZ - 1, roll(v, -1, 0), 0.0)
        fz = flux(k, k_z, v, v_z)
        fz_in = jnp.where(z > 0, roll(fz, 1, 0), -0.5 * k * v)
        r = src[i] - after + before - fy + roll(fy, 1, 1) - fz + fz_in
        r_ref[i] = r
        before = after
        j = i // 2
        if i % 2 == 0:
            r_even, k_even = r, k
        else:
            pool[0, j] = r_even + r
            pool[1, j] = k_even + k
        off = 8 * i
        here = (lane >= off) & (lane < off + 8)
        top = jnp.where(lane >= 124, k, jnp.where(lane >= 121, roll(r, -4, 1), roll(v, -7, 1)))
        bottom = jnp.where(lane < 4, k, jnp.where(lane < 7, roll(r, 4, 1), roll(v, 7, 1)))
        up = jnp.where(here, roll(top, off - 120, 1), up)
        dn = jnp.where(here, roll(bottom, off, 1), dn)
    up_ref[0:NZ] = up
    dn_ref[0:NZ] = dn
    up = dn = zero
    for g, edge in enumerate((k_ref[0], it[0], k_ref[ROWS - 1], it[ROWS - 1])):
        here = (lane >= 32 * g) & (lane < 32 * g + 32)
        up = jnp.where(here, roll(edge, 32 * g - 96, 1), up)
        dn = jnp.where(here, roll(edge, 32 * g, 1), dn)
    up_ref[NZ:2 * NZ] = up
    dn_ref[NZ:2 * NZ] = dn
    tops = pool[:, :, pl.ds(0, CZ, stride=2), :] + pool[:, :, pl.ds(1, CZ, stride=2), :]
    child, parent = iota((LANES, LANES), 0) // 2, iota((LANES, LANES), 1)
    to_left = jnp.where(child == parent, F32(1.0), F32(0.0))
    to_right = jnp.where(child == parent - CLANES, F32(0.125), F32(0.0))
    coarse = dot(tops[0].reshape(CROWS * CZ, LANES), to_left) + dot(tops[1].reshape(CROWS * CZ, LANES), to_right)
    coarse = coarse.reshape(CROWS, CZ, LANES)
    c_ref[...] = coarse
    lane = iota((CZ, LANES), 1)
    for t in range(2):
        up = dn = jnp.zeros((CZ, LANES), F32)
        for j in range(4 * t, 4 * t + 4):
            row = coarse[j]
            off = (j % 4) * 32
            at_r = (lane >= off) & (lane < off + 16)
            at_k = (lane >= off + 16) & (lane < off + 32)
            up = jnp.where(at_r, roll(row, off - 48, 1), jnp.where(at_k, roll(row, off + 16 - 112, 1), up))
            dn = jnp.where(at_r, roll(row, off, 1), jnp.where(at_k, roll(row, off + 16 - 64, 1), dn))
        up_ref[2 * NZ + CZ * t:2 * NZ + CZ * (t + 1)] = up
        dn_ref[2 * NZ + CZ * t:2 * NZ + CZ * (t + 1)] = dn


def strip_flux(up, dn):
    lane = iota(up.shape, 1)
    face = flux(roll(up, -7, 1), dn, up, roll(dn, -7, 1))
    return jnp.where(lane % 8 == 0, face, 0.0)


def completed(ou, od, ru, rd):
    right = strip_flux(ou[0:NZ], rd[0:NZ])
    left = strip_flux(ru[0:NZ], od[0:NZ])
    return rd[0:NZ] + roll(right, 4, 1), ru[0:NZ] - roll(left, 3, 1), right, left


def block_kernel(flags, it, r_in, k_in, c_ref, ou, od, ru, rd, m_ref, n_ref, pool):
    dn, up, right, left = completed(ou, od, ru, rd)
    pool[0] = right + roll(right, -8, 1)
    pool[1] = left + roll(left, -8, 1)
    sums = pool[:, pl.ds(0, CZ, stride=2), :] + pool[:, pl.ds(1, CZ, stride=2), :]
    lane = iota((CZ, LANES), 1)
    for j in range(CROWS):
        own = c_ref[j]
        strip = slice(2 * NZ + CZ * (j // 4), 2 * NZ + CZ * (j // 4) + CZ)
        off = (j % 4) * 32
        src = 16 * j
        for n in range(2):
            value = jnp.where(lane < 64, roll(own, -64 * n, 1), 0.0)
            value = jnp.where((lane >= 64) & (lane < 80), roll(rd[strip], 64 - off - 16 * n, 1), value)
            value = jnp.where(lane >= 112, roll(ru[strip], 112 - off - 16 * n, 1), value)
            if n == 0:
                value = value - jnp.where(lane == 63, roll(sums[0], 63 - src, 1), 0.0)
                value = value + jnp.where(lane == 64, roll(sums[0], 64 - src, 1), 0.0)
                value = value - jnp.where(lane == 127, roll(sums[1], 127 - src, 1), 0.0)
                value = value + jnp.where(lane == 0, roll(sums[1], -src, 1), 0.0)
            at = CZ * (CROWS * n + j)
            m_ref[at:at + CZ] = value
    lane = iota((NZ, LANES), 1)
    first = flags[0] == 0

    def near(base, top):
        tiles = []
        k_row, r_row, v_row = (12, 13, 15) if top else (0, 0, 0)
        for t in range(4):
            tiles.append(k_in[k_row + t])
        for t in range(3):
            i = r_row + t
            r = r_in[i] - jnp.where(lane == 127, roll(right, 127 - 8 * i, 1), 0.0)
            tiles.append(r + jnp.where(lane == 0, roll(left, -8 * i, 1), 0.0))
        tiles.append(it[v_row])
        tiles.append(jnp.where(lane < 32, roll(dn, -8 * k_row, 1), roll(up, 32 - 8 * k_row, 1)))
        shift = 64 if top else 0
        tiles.append(jnp.where(lane < 64, roll(rd[NZ:2 * NZ], -shift, 1), roll(ru[NZ:2 * NZ], 64 - shift, 1)))
        return tiles

    low, high = near(0, False), near(0, True)
    for t in range(10):
        m_ref[2 * BLOCK + NZ * t:2 * BLOCK + NZ * (t + 1)] = jnp.where(first, high[t], low[t])
        n_ref[NZ * t:NZ * (t + 1)] = jnp.where(first, low[t], high[t])


def edge_flux(a, b, pool):
    pool[0] = flux(a(3), b(0), a(7), b(7))
    u, w = a(9), b(9)
    pool[1] = flux(u, w, roll(u, -32, 1), roll(w, -32, 1))
    sums = pool[:, pl.ds(0, CZ, stride=2), :] + pool[:, pl.ds(1, CZ, stride=2), :]
    child, parent = iota((LANES, LANES), 0), iota((LANES, LANES), 1)
    own = jnp.where(child // 2 == parent, F32(1.0), F32(0.0))
    right = (child < 32) & (child // 2 + 64 == parent)
    left = (child >= 64) & (child < 96) & (child // 2 + 80 == parent)
    beyond = jnp.where(right | left, F32(1.0), F32(0.0))
    return dot(sums[0], own) + dot(sums[1], beyond)


def chip_kernel(pair, near, o_ref, pool):
    def tile(n):
        return lambda t: pair[n, 2 * BLOCK + NZ * t:2 * BLOCK + NZ * (t + 1)]

    inner = edge_flux(tile(0), tile(1), pool)
    for n in range(2):
        o_ref[2 * BLOCK * n:2 * BLOCK * (n + 1)] = pair[n, 0:2 * BLOCK]
    last = BLOCK - CZ
    o_ref[last:BLOCK] = pair[0, last:BLOCK] - inner
    o_ref[2 * BLOCK:2 * BLOCK + CZ] = pair[1, 0:CZ] + inner
    o_ref[4 * BLOCK:] = near[...]


def relay_kernel(flags, out, o_ref, pool):
    first = flags[0] == 0
    low, high = flags[1].astype(F32), flags[2].astype(F32)

    def tile(n, valid):
        return lambda t: out[n, 4 * BLOCK + NZ * t:4 * BLOCK + NZ * (t + 1)] * valid

    outer = edge_flux(tile(0, low), tile(1, high), pool)
    o_ref[0:2 * BLOCK] = jnp.where(first, out[0, 2 * BLOCK:4 * BLOCK] * low, out[1, 0:2 * BLOCK] * high)
    o_ref[2 * BLOCK:] = outer


def sweep(lo, hi, mid, shift, sweeps, r_s, s_s, x_s, c_s, width):
    start, pairs = weights(sweeps)
    for n in range(1, sweeps):
        keep, add = pairs[n - 1]
        prev, here = s_s[lo + n - 1], s_s[lo + n]
        for i in range(lo + n, hi - n):
            ahead = s_s[i + 1]
            total = c_s[0, i] * ahead + c_s[1, i] * prev
            total = total + c_s[2, i] * roll(here, -1, 0) + c_s[3, i] * roll(here, 1, 0)
            total = total + c_s[4, i] * roll(here, -1, 1) + c_s[5, i] * roll(here, 1, 1)
            r = r_s[i] - (here - total)
            step = keep * here + add * r
            r_s[i] = r
            s_s[i] = step
            if shift <= i < shift + mid:
                x_s[i - shift] = x_s[i - shift] + (step[:, 0:width] if width else step)
            prev, here = here, ahead


def prepare(rows, mid, shift, sweeps, factor, k_s, r_s, s_s, x_s, c_s, width):
    depth = k_s.shape[1]
    z = iota(k_s.shape[1:], 0)
    start, _ = weights(sweeps)
    below = factor * (k_s[0] + k_s[1])
    for i in range(1, rows - 1):
        k = k_s[i]
        above = factor * (k + k_s[i + 1])
        z_up = factor * (k + jnp.where(z < depth - 1, roll(k, -1, 0), 0.0))
        z_dn = factor * (k + jnp.where(z > 0, roll(k, 1, 0), 0.0))
        y_up = factor * (k + roll(k, -1, 1))
        y_dn = factor * (k + roll(k, 1, 1))
        diagonal = above + below + z_up + z_dn + y_up + y_dn
        inverse = jnp.where(k > 0, 1.0 / jnp.where(k > 0, diagonal, 1.0), 0.0)
        c_s[0, i] = inverse * above
        c_s[1, i] = inverse * below
        c_s[2, i] = jnp.where(z < depth - 1, inverse * z_up, 0.0)
        c_s[3, i] = jnp.where(z > 0, inverse * z_dn, 0.0)
        c_s[4, i] = inverse * y_up
        c_s[5, i] = inverse * y_dn
        r = inverse * r_s[i]
        r_s[i] = r
        s_s[i] = r * start
        if shift <= i < shift + mid:
            x_s[i - shift] = (r[:, 0:width] if width else r) * start
        below = above


def coarse_part(flags, chip, out, near, x_s, k_s, r_s, s_s, c_s):
    first = flags[0] == 0
    low, high = flags[3].astype(F32), flags[4].astype(F32)
    own = near[flags[0], 2 * BLOCK:]
    other = near[1 - flags[0], 2 * BLOCK:]
    f_low = jnp.where(first, own, other)
    f_high = jnp.where(first, other, own)
    for n, dest in enumerate((r_s, k_s)):
        for j in range(CROWS):
            at = slice(BLOCK * n + CZ * j, BLOCK * n + CZ * (j + 1))
            up = slice(2 * BLOCK + BLOCK * n + CZ * j, 2 * BLOCK + BLOCK * n + CZ * (j + 1))
            rows = (
                jnp.where(first, out[0, at] * low, near[0, at]),
                jnp.where(first, out[0, up] * low, chip[at]),
                jnp.where(first, chip[at], chip[up]),
                jnp.where(first, chip[up], out[1, at] * high),
                jnp.where(first, near[1, at], out[1, up] * high),
            )
            for b in range(5):
                dest[CROWS * b + j] = rows[b]
    low_at, high_at = jnp.where(first, 16, 8), jnp.where(first, 32, 24)
    r_s[low_at - 1] = r_s[low_at - 1] - f_low
    r_s[low_at] = r_s[low_at] + f_low
    r_s[high_at - 1] = r_s[high_at - 1] - f_high
    r_s[high_at] = r_s[high_at] + f_high
    zero = jnp.zeros((CZ, LANES), F32)
    s_s[0] = zero
    s_s[CEXT - 1] = zero
    prepare(CEXT, CROWS, COARSE_SWEEPS, COARSE_SWEEPS, 2.0, k_s, r_s, s_s, x_s, c_s, 0)
    sweep(1, CEXT - 1, CROWS, COARSE_SWEEPS, COARSE_SWEEPS, r_s, s_s, x_s, c_s, 0)


def fine_part(flags, it, r_in, k_in, pair, out, ou, od, ru, rd, x_s, k_s, r_s, s_s, c_s):
    first = flags[0] == 0
    low, high = flags[1].astype(F32), flags[2].astype(F32)
    lane = iota((NZ, LANES), 1)
    dn, up, right, left = completed(ou, od, ru, rd)

    def beside(rights, lefts, count):
        return jnp.where(lane < count, rights, jnp.where(lane >= LANES - count, lefts, 0.0))

    def join(a, b):
        return jnp.concatenate([a, b], axis=1)

    for i in range(ROWS):
        off = 8 * i
        e = HALO + i
        k_s[e, :, 0:LANES] = k_in[i]
        k_s[e, :, LANES:] = beside(roll(dn, -off, 1), roll(up, 120 - off, 1), 4)
        r = r_in[i] - jnp.where(lane == 127, roll(right, 127 - off, 1), 0.0)
        r_s[e, :, 0:LANES] = r + jnp.where(lane == 0, roll(left, -off, 1), 0.0)
        r_s[e, :, LANES:] = beside(roll(dn, -off - 4, 1), roll(up, 124 - off, 1), 3)
    edges = rd[NZ:2 * NZ], ru[NZ:2 * NZ]
    for side in range(2):
        def tile(t, side=side):
            at = slice(4 * BLOCK + NZ * t, 4 * BLOCK + NZ * (t + 1))
            by = slice(2 * BLOCK + NZ * t, 2 * BLOCK + NZ * (t + 1))
            if side == 0:
                return jnp.where(first, out[0, at], pair[0, by]) * low
            return jnp.where(first, pair[1, by], out[1, at]) * high

        base = 0 if side == 0 else HALO + ROWS
        halo, face = tile(8), tile(9)
        for q in range(4):
            k_s[base + q, :, 0:LANES] = tile(q)
            k_s[base + q, :, LANES:] = beside(roll(halo, -8 * q, 1), roll(halo, 88 - 8 * q, 1), 4)
        for t in range(3):
            q = t + 1 - side
            r_s[base + q, :, 0:LANES] = tile(4 + t)
            r_s[base + q, :, LANES:] = beside(roll(halo, -8 * q - 4, 1), roll(halo, 92 - 8 * q, 1), 3)
        v_out = join(tile(7), beside(roll(face, -32, 1), face, 4))
        if side == 0:
            v_in = join(it[0], beside(roll(edges[0], -32, 1), roll(edges[1], 64, 1), 4))
            through = flux(k_s[HALO - 1], k_s[HALO], v_out, v_in)
            r_s[HALO - 1] = r_s[HALO - 1] - through
            r_s[HALO] = r_s[HALO] + through
        else:
            v_in = join(it[ROWS - 1], beside(roll(edges[0], -96, 1), edges[1], 4))
            through = flux(k_s[HALO + ROWS - 1], k_s[HALO + ROWS], v_in, v_out)
            r_s[HALO + ROWS - 1] = r_s[HALO + ROWS - 1] - through
            r_s[HALO + ROWS] = r_s[HALO + ROWS] + through
    zero = jnp.zeros((NZ, 2 * LANES), F32)
    s_s[0] = zero
    s_s[EXT - 1] = zero
    prepare(EXT, ROWS, HALO, SWEEPS, 0.5, k_s, r_s, s_s, x_s, c_s, LANES)
    sweep(1, EXT - 1, ROWS, HALO, SWEEPS, r_s, s_s, x_s, c_s, LANES)


def final_kernel(
    flags, it, r_in, k_in, ou, od, ru, rd, pair, chip, out, near, o_ref, p_ref,
    x_c, k_c, r_c, s_c, c_c, x_f, k_f, r_f, s_f, c_f, wide_s,
):
    coarse_part(flags, chip, out, near, x_c, k_c, r_c, s_c, c_c)
    lane = iota((CZ, LANES), 1)
    for a in range(4):
        p_ref[pl.ds(a, CZ, stride=4), :] = jnp.where(lane < CLANES, x_c[a], roll(x_c[a + 4], CLANES, 1))
    fine_part(flags, it, r_in, k_in, pair, out, ou, od, ru, rd, x_f, k_f, r_f, s_f, c_f)
    child, parent = iota((LANES, LANES), 1) // 2, iota((LANES, LANES), 0)
    spread = jnp.where(child == parent, F32(1.0), F32(0.0))
    wide = dot(x_c[...].reshape(CROWS * CZ, LANES), spread).reshape(CROWS, CZ, LANES)
    wide_s[:, pl.ds(0, CZ, stride=2), :] = wide
    wide_s[:, pl.ds(1, CZ, stride=2), :] = wide
    for i in range(ROWS):
        o_ref[i] = it[i] + x_f[i] + wide_s[i // 2]


def planes_kernel(sources, planes, p_ref, o_ref):
    half = sources // 2
    lane = iota((half, LANES), 1)
    for q in range(planes):
        for a in range(4):
            even = p_ref[pl.ds(4 * q + a, half, stride=8 * planes), :]
            odd = p_ref[pl.ds(4 * (planes + q) + a, half, stride=8 * planes), :]
            to = (a * planes + q) * half
            o_ref[to:to + half] = jnp.where(lane < CLANES, even, roll(odd, CLANES, 1))
            to = ((a + 4) * planes + q) * half
            o_ref[to:to + half] = jnp.where(lane < CLANES, roll(even, CLANES, 1), odd)


def call(kernel, outs, scratch, in_smem=False, operands=(), flops=1000000):
    vmem = pl.BlockSpec(memory_space=pltpu.VMEM)
    specs = [vmem] * len(operands)
    if in_smem:
        specs[0] = pl.BlockSpec(memory_space=pltpu.SMEM)
    size = sum(4 * x.size for x in operands) + sum(4 * o.size for o in outs)
    multiple = len(outs) > 1
    return pl.pallas_call(
        kernel,
        out_shape=outs if multiple else outs[0],
        in_specs=specs,
        out_specs=[vmem] * len(outs) if multiple else vmem,
        scratch_shapes=[pltpu.VMEM(s, F32) for s in scratch],
        compiler_params=pltpu.CompilerParams(vmem_limit_bytes=40 * 1024 * 1024),
        cost_estimate=pl.CostEstimate(flops=flops, bytes_accessed=size, transcendentals=0),
    )(*operands)


def shape(*dims):
    return jax.ShapeDtypeStruct(dims, F32)


def on_device(iterate, source, labels):
    n_gx, n_gy = lax.axis_size("gx"), lax.axis_size("gy")
    gx = lax.axis_index("gx")
    flags = jnp.stack([gx % 2, gx > 0, gx < n_gx - 1, gx > 1, gx < n_gx - 2]).astype(jnp.int32)
    chips = [[i, i + 1] for i in range(0, n_gx, 2)]
    between = [[i, (i + 1) % n_gx] for i in range(1, n_gx, 2)]
    own = shape(ROWS, NZ, LANES)
    strip = shape(3 * NZ, LANES)
    resid, cond, coarse, up, dn = call(
        residual_kernel,
        [own, own, shape(CROWS, CZ, LANES), strip, strip],
        [(2, CROWS, NZ, LANES)],
        False,
        (iterate, source, labels),
    )
    onward = [(i, i + 1) for i in range(n_gy - 1)]
    back = [(i + 1, i) for i in range(n_gy - 1)]
    from_left = lax.ppermute(up, "gy", onward)
    from_right = lax.ppermute(dn, "gy", back)
    strips = (up, dn, from_left, from_right)
    block, near = call(
        block_kernel,
        [shape(2 * BLOCK + 10 * NZ, LANES), shape(10 * NZ, LANES)],
        [(2, NZ, LANES)],
        True,
        (flags, iterate, resid, cond, coarse, *strips),
    )
    pair = lax.all_gather(block, "gx", axis_index_groups=chips)
    chip = call(chip_kernel, [shape(4 * BLOCK + 10 * NZ, LANES)], [(2, NZ, LANES)], False, (pair, near))
    beyond = lax.all_gather(chip, "gx", axis_index_groups=between)
    relay = call(relay_kernel, [shape(2 * BLOCK + CZ, LANES)], [(2, NZ, LANES)], True, (flags, beyond))
    relay = lax.all_gather(relay, "gx", axis_index_groups=chips)
    rows, wide = (CEXT, CZ, LANES), (EXT, NZ, 2 * LANES)
    corrected, planes = call(
        final_kernel,
        [own, shape(4 * CZ, LANES)],
        [(CROWS, CZ, LANES), rows, rows, rows, (6, *rows)]
        + [(ROWS, NZ, LANES), wide, wide, wide, (6, *wide), (CROWS, NZ, LANES)],
        True,
        (flags, iterate, resid, cond, *strips, pair, chip, beyond, relay),
    )
    per = CZ // n_gy
    planes = lax.all_to_all(planes.reshape(n_gy, 4 * per, LANES), "gy", split_axis=0, concat_axis=0, tiled=True)
    owned = call(
        functools.partial(planes_kernel, n_gy, per),
        [shape(4 * CZ, LANES)],
        [],
        False,
        (planes.reshape(4 * CZ, LANES),),
    ).reshape(CROWS, per, CLANES * n_gy)
    return corrected, owned


def solution(mesh):
    spec = P("gx", None, "gy")
    return jax.shard_map(
        on_device, mesh=mesh, in_specs=(spec, spec, spec), out_specs=(spec, P("gx", "gy", None)), check_vma=False
    )
```

```python
import functools

import jax
import jax.numpy as jnp
from jax import lax
from jax.experimental import pallas as pl
from jax.experimental.pallas import tpu as pltpu
from jax.sharding import PartitionSpec as P

SWEEPS = 4
COARSE_SWEEPS = 16
TABLE = (0.5, 1.0, 2.5, 6.0)
LOWER = 0.25
UPPER = 2.0
F32 = jnp.float32

ROWS, NZ, LANES = 16, 32, 128
CROWS, CZ, CLANES = 8, 16, 64
HALO = SWEEPS
EXT = ROWS + 2 * HALO
CEXT = CROWS + 2 * COARSE_SWEEPS
OWN = CROWS * CZ
BLOCK = OWN + 4 * CZ
NEAR = 10 * NZ
PARTS = 4


def weights(sweeps):
    centre = (UPPER + LOWER) / 2.0
    radius = (UPPER - LOWER) / 2.0
    sigma = centre / radius
    rho = 1.0 / sigma
    pairs = []
    for _ in range(1, sweeps):
        rho_new = 1.0 / (2.0 * sigma - rho)
        pairs.append((rho_new * rho, 2.0 * rho_new / radius))
        rho = rho_new
    return 1.0 / centre, pairs


def conduct(labels):
    total = jnp.zeros(labels.shape, F32)
    for label_id, value in enumerate(TABLE):
        total = jnp.where(labels == label_id, F32(value), total)
    return total


def roll(x, shift, axis):
    size = x.shape[axis]
    shift = shift % size
    return x if shift == 0 else pltpu.roll(x, shift, axis)


def iota(shape, axis):
    return lax.broadcasted_iota(jnp.int32, shape, axis)


def flux(k_a, k_b, v_a, v_b):
    return 0.5 * (k_a + k_b) * (v_a - v_b)


def dot(a, b):
    return jnp.dot(a, b, precision=lax.Precision.HIGHEST, preferred_element_type=F32)


def residual_kernel(it_in, src_in, lab_in, r_ref, k_ref, c_ref, up_ref, dn_ref, pool, it, src, lab, sems):
    copies = []
    for part in range(PARTS):
        rows = pl.ds(part * ROWS // PARTS, ROWS // PARTS)
        copies.append(
            [
                pltpu.make_async_copy(a.at[rows], b.at[rows], sems.at[n, part])
                for n, (a, b) in enumerate(((lab_in, lab), (it_in, it), (src_in, src)))
            ]
        )
        for copy in copies[-1]:
            copy.start()

    def arrive(part):
        for copy in copies[part]:
            copy.wait()
        for i in range(part * ROWS // PARTS, (part + 1) * ROWS // PARTS):
            k_ref[i] = conduct(lab[i])

    arrive(0)
    z, lane = iota((NZ, LANES), 0), iota((NZ, LANES), 1)
    zero = jnp.zeros((NZ, LANES), F32)
    before = zero
    up = dn = zero
    for i in range(ROWS):
        if (i + 1) % (ROWS // PARTS) == 0 and i < ROWS - 1:
            arrive((i + 1) // (ROWS // PARTS))
        k, v = k_ref[i], it[i]
        after = flux(k, k_ref[i + 1], v, it[i + 1]) if i < ROWS - 1 else zero
        fy = jnp.where(lane < LANES - 1, flux(k, roll(k, -1, 1), v, roll(v, -1, 1)), 0.0)
        k_z = jnp.where(z < NZ - 1, roll(k, -1, 0), 0.0)
        v_z = jnp.where(z < NZ - 1, roll(v, -1, 0), 0.0)
        fz = flux(k, k_z, v, v_z)
        fz_in = jnp.where(z > 0, roll(fz, 1, 0), -0.5 * k * v)
        r = src[i] - after + before - fy + roll(fy, 1, 1) - fz + fz_in
        r_ref[i] = r
        before = after
        j = i // 2
        if i % 2 == 0:
            r_even, k_even = r, k
        else:
            pool[0, j] = r_even + r
            pool[1, j] = k_even + k
        off = 8 * i
        here = (lane >= off) & (lane < off + 8)
        top = jnp.where(lane >= 124, k, jnp.where(lane >= 121, roll(r, -4, 1), roll(v, -7, 1)))
        bottom = jnp.where(lane < 4, k, jnp.where(lane < 7, roll(r, 4, 1), roll(v, 7, 1)))
        up = jnp.where(here, roll(top, off - 120, 1), up)
        dn = jnp.where(here, roll(bottom, off, 1), dn)
    up_ref[0:NZ] = up
    dn_ref[0:NZ] = dn
    up = dn = zero
    for g, edge in enumerate((k_ref[0], it[0], k_ref[ROWS - 1], it[ROWS - 1])):
        here = (lane >= 32 * g) & (lane < 32 * g + 32)
        up = jnp.where(here, roll(edge, 32 * g - 96, 1), up)
        dn = jnp.where(here, roll(edge, 32 * g, 1), dn)
    up_ref[NZ:2 * NZ] = up
    dn_ref[NZ:2 * NZ] = dn
    tops = pool[:, :, pl.ds(0, CZ, stride=2), :] + pool[:, :, pl.ds(1, CZ, stride=2), :]
    child, parent = iota((LANES, LANES), 0) // 2, iota((LANES, LANES), 1)
    to_left = jnp.where(child == parent, F32(1.0), F32(0.0))
    to_right = jnp.where(child == parent - CLANES, F32(0.125), F32(0.0))
    coarse = dot(tops[0].reshape(CROWS * CZ, LANES), to_left) + dot(tops[1].reshape(CROWS * CZ, LANES), to_right)
    coarse = coarse.reshape(CROWS, CZ, LANES)
    c_ref[...] = coarse
    lane = iota((CZ, LANES), 1)
    for t in range(2):
        up = dn = jnp.zeros((CZ, LANES), F32)
        for j in range(4 * t, 4 * t + 4):
            row = coarse[j]
            off = (j % 4) * 32
            at_r = (lane >= off) & (lane < off + 16)
            at_k = (lane >= off + 16) & (lane < off + 32)
            up = jnp.where(at_r, roll(row, off - 48, 1), jnp.where(at_k, roll(row, off + 16 - 112, 1), up))
            dn = jnp.where(at_r, roll(row, off, 1), jnp.where(at_k, roll(row, off + 16 - 64, 1), dn))
        up_ref[2 * NZ + CZ * t:2 * NZ + CZ * (t + 1)] = up
        dn_ref[2 * NZ + CZ * t:2 * NZ + CZ * (t + 1)] = dn


def strip_flux(up, dn):
    lane = iota(up.shape, 1)
    face = flux(roll(up, -7, 1), dn, up, roll(dn, -7, 1))
    return jnp.where(lane % 8 == 0, face, 0.0)


def completed(ou, od, ru, rd):
    right = strip_flux(ou[0:NZ], rd[0:NZ])
    left = strip_flux(ru[0:NZ], od[0:NZ])
    return rd[0:NZ] + roll(right, 4, 1), ru[0:NZ] - roll(left, 3, 1), right, left


def block_kernel(flags, it, r_in, k_in, c_ref, ou, od, ru, rd, m_ref, n_ref, pool):
    dn, up, right, left = completed(ou, od, ru, rd)
    pool[0] = right + roll(right, -8, 1)
    pool[1] = left + roll(left, -8, 1)
    sums = pool[:, pl.ds(0, CZ, stride=2), :] + pool[:, pl.ds(1, CZ, stride=2), :]
    lane = iota((CZ, LANES), 1)
    for j in range(CROWS):
        value = c_ref[j] - jnp.where(lane == 63, roll(sums[0], 63 - 16 * j, 1), 0.0)
        m_ref[CZ * j:CZ * (j + 1)] = value + jnp.where(lane == 0, roll(sums[1], -16 * j, 1), 0.0)
    for t in range(2):
        at = slice(2 * NZ + CZ * t, 2 * NZ + CZ * (t + 1))
        more, less = rd[at], ru[at]
        for q in range(4):
            src = 16 * (4 * t + q)
            more = more + jnp.where(lane == 32 * q, roll(sums[0], 32 * q - src, 1), 0.0)
            less = less - jnp.where(lane == 32 * q + 15, roll(sums[1], 32 * q + 15 - src, 1), 0.0)
        m_ref[OWN + CZ * t:OWN + CZ * (t + 1)] = more
        m_ref[OWN + CZ * (2 + t):OWN + CZ * (3 + t)] = less
    lane = iota((NZ, LANES), 1)
    first = flags[0] == 0

    def near(base, top):
        tiles = []
        k_row, r_row, v_row = (12, 13, 15) if top else (0, 0, 0)
        for t in range(4):
            tiles.append(k_in[k_row + t])
        for t in range(3):
            i = r_row + t
            r = r_in[i] - jnp.where(lane == 127, roll(right, 127 - 8 * i, 1), 0.0)
            tiles.append(r + jnp.where(lane == 0, roll(left, -8 * i, 1), 0.0))
        tiles.append(it[v_row])
        tiles.append(jnp.where(lane < 32, roll(dn, -8 * k_row, 1), roll(up, 32 - 8 * k_row, 1)))
        shift = 64 if top else 0
        tiles.append(jnp.where(lane < 64, roll(rd[NZ:2 * NZ], -shift, 1), roll(ru[NZ:2 * NZ], 64 - shift, 1)))
        return tiles

    low, high = near(0, False), near(0, True)
    for t in range(10):
        m_ref[BLOCK + NZ * t:BLOCK + NZ * (t + 1)] = jnp.where(first, high[t], low[t])
        n_ref[NZ * t:NZ * (t + 1)] = jnp.where(first, low[t], high[t])


def edge_flux(a, b, pool):
    pool[0] = flux(a(3), b(0), a(7), b(7))
    u, w = a(9), b(9)
    pool[1] = flux(u, w, roll(u, -32, 1), roll(w, -32, 1))
    sums = pool[:, pl.ds(0, CZ, stride=2), :] + pool[:, pl.ds(1, CZ, stride=2), :]
    child, parent = iota((LANES, LANES), 0), iota((LANES, LANES), 1)
    own = jnp.where(child // 2 == parent, F32(1.0), F32(0.0))
    right = (child < 32) & (child // 2 + 64 == parent)
    left = (child >= 64) & (child < 96) & (child // 2 + 80 == parent)
    beyond = jnp.where(right | left, F32(1.0), F32(0.0))
    return dot(sums[0], own) + dot(sums[1], beyond)


def chip_kernel(pair, near, o_ref, pool):
    def tile(n):
        return lambda t: pair[n, BLOCK + NZ * t:BLOCK + NZ * (t + 1)]

    inner = edge_flux(tile(0), tile(1), pool)
    for n in range(2):
        o_ref[BLOCK * n:BLOCK * (n + 1)] = pair[n, 0:BLOCK]
    lane = iota((CZ, LANES), 1)
    for n, j in ((0, CROWS - 1), (1, 0)):
        change = inner if n else -inner
        off = 32 * (j % 4)
        side = (lane >= off) & (lane < off + 16)
        changes = (
            (CZ * j, jnp.where(lane < CLANES, change, 0.0)),
            (OWN + CZ * (j // 4), jnp.where(side, roll(change, off - 64, 1), 0.0)),
            (OWN + CZ * (2 + j // 4), jnp.where(side, roll(change, off - 112, 1), 0.0)),
        )
        for at, part in changes:
            o_ref[BLOCK * n + at:BLOCK * n + at + CZ] = pair[n, at:at + CZ] + part
    o_ref[2 * BLOCK:] = near[...]


def relay_kernel(flags, out, o_ref, pool):
    first = flags[0] == 0
    low, high = flags[1].astype(F32), flags[2].astype(F32)

    def tile(n, valid):
        return lambda t: out[n, 2 * BLOCK + NZ * t:2 * BLOCK + NZ * (t + 1)] * valid

    outer = edge_flux(tile(0, low), tile(1, high), pool)
    o_ref[0:BLOCK] = jnp.where(first, out[0, BLOCK:2 * BLOCK] * low, out[1, 0:BLOCK] * high)
    o_ref[BLOCK:] = outer


def sweep(lo, hi, mid, shift, sweeps, r_s, s_s, x_s, c_s, width):
    start, pairs = weights(sweeps)
    for n in range(1, sweeps):
        keep, add = pairs[n - 1]
        prev, here = s_s[lo + n - 1], s_s[lo + n]
        for i in range(lo + n, hi - n):
            ahead = s_s[i + 1]
            total = c_s[0, i] * ahead + c_s[1, i] * prev
            total = total + c_s[2, i] * roll(here, -1, 0) + c_s[3, i] * roll(here, 1, 0)
            total = total + c_s[4, i] * roll(here, -1, 1) + c_s[5, i] * roll(here, 1, 1)
            r = r_s[i] - (here - total)
            step = keep * here + add * r
            r_s[i] = r
            s_s[i] = step
            if shift <= i < shift + mid:
                x_s[i - shift] = x_s[i - shift] + (step[:, 0:width] if width else step)
            prev, here = here, ahead


def prepare(rows, mid, shift, sweeps, factor, k_s, r_s, s_s, x_s, c_s, width):
    depth = k_s.shape[1]
    z = iota(k_s.shape[1:], 0)
    start, _ = weights(sweeps)
    below = factor * (k_s[0] + k_s[1])
    for i in range(1, rows - 1):
        k = k_s[i]
        above = factor * (k + k_s[i + 1])
        z_up = factor * (k + jnp.where(z < depth - 1, roll(k, -1, 0), 0.0))
        z_dn = factor * (k + jnp.where(z > 0, roll(k, 1, 0), 0.0))
        y_up = factor * (k + roll(k, -1, 1))
        y_dn = factor * (k + roll(k, 1, 1))
        diagonal = above + below + z_up + z_dn + y_up + y_dn
        inverse = jnp.where(k > 0, 1.0 / jnp.where(k > 0, diagonal, 1.0), 0.0)
        c_s[0, i] = inverse * above
        c_s[1, i] = inverse * below
        c_s[2, i] = jnp.where(z < depth - 1, inverse * z_up, 0.0)
        c_s[3, i] = jnp.where(z > 0, inverse * z_dn, 0.0)
        c_s[4, i] = inverse * y_up
        c_s[5, i] = inverse * y_dn
        r = inverse * r_s[i]
        r_s[i] = r
        s_s[i] = r * start
        if shift <= i < shift + mid:
            x_s[i - shift] = (r[:, 0:width] if width else r) * start
        below = above


def coarse_part(flags, chip, out, near, x_s, k_s, r_s, s_s, c_s):
    first = flags[0] == 0
    low, high = flags[3].astype(F32), flags[4].astype(F32)
    own = near[flags[0], BLOCK:]
    other = near[1 - flags[0], BLOCK:]
    f_low = jnp.where(first, own, other)
    f_high = jnp.where(first, other, own)
    lane = iota((CZ, LANES), 1)

    def packed(at):
        up = slice(BLOCK + at.start, BLOCK + at.stop)
        return (
            jnp.where(first, out[0, at] * low, near[0, at]),
            jnp.where(first, out[0, up] * low, chip[at]),
            jnp.where(first, chip[at], chip[up]),
            jnp.where(first, chip[up], out[1, at] * high),
            jnp.where(first, near[1, at], out[1, up] * high),
        )

    sides = [packed(slice(OWN + CZ * t, OWN + CZ * (t + 1))) for t in range(4)]
    for j in range(CROWS):
        off = 32 * (j % 4)
        rows = packed(slice(CZ * j, CZ * (j + 1)))
        for b in range(5):
            more, less = sides[j // 4][b], sides[2 + j // 4][b]
            for n, dest in enumerate((r_s, k_s)):
                value = jnp.where(lane < CLANES, roll(rows[b], -CLANES * n, 1), 0.0)
                value = jnp.where((lane >= 64) & (lane < 80), roll(more, 64 - off - 16 * n, 1), value)
                dest[CROWS * b + j] = jnp.where(lane >= 112, roll(less, 112 - off - 16 * n, 1), value)
    low_at, high_at = jnp.where(first, 16, 8), jnp.where(first, 32, 24)
    r_s[low_at - 1] = r_s[low_at - 1] - f_low
    r_s[low_at] = r_s[low_at] + f_low
    r_s[high_at - 1] = r_s[high_at - 1] - f_high
    r_s[high_at] = r_s[high_at] + f_high
    zero = jnp.zeros((CZ, LANES), F32)
    s_s[0] = zero
    s_s[CEXT - 1] = zero
    prepare(CEXT, CROWS, COARSE_SWEEPS, COARSE_SWEEPS, 2.0, k_s, r_s, s_s, x_s, c_s, 0)
    sweep(1, CEXT - 1, CROWS, COARSE_SWEEPS, COARSE_SWEEPS, r_s, s_s, x_s, c_s, 0)


def fine_part(flags, it, r_in, k_in, pair, out, ou, od, ru, rd, x_s, k_s, r_s, s_s, c_s):
    first = flags[0] == 0
    low, high = flags[1].astype(F32), flags[2].astype(F32)
    lane = iota((NZ, LANES), 1)
    dn, up, right, left = completed(ou, od, ru, rd)

    def beside(rights, lefts, count):
        return jnp.where(lane < count, rights, jnp.where(lane >= LANES - count, lefts, 0.0))

    def join(a, b):
        return jnp.concatenate([a, b], axis=1)

    for i in range(ROWS):
        off = 8 * i
        e = HALO + i
        k_s[e, :, 0:LANES] = k_in[i]
        k_s[e, :, LANES:] = beside(roll(dn, -off, 1), roll(up, 120 - off, 1), 4)
        r = r_in[i] - jnp.where(lane == 127, roll(right, 127 - off, 1), 0.0)
        r_s[e, :, 0:LANES] = r + jnp.where(lane == 0, roll(left, -off, 1), 0.0)
        r_s[e, :, LANES:] = beside(roll(dn, -off - 4, 1), roll(up, 124 - off, 1), 3)
    edges = rd[NZ:2 * NZ], ru[NZ:2 * NZ]
    for side in range(2):
        def tile(t, side=side):
            at = slice(2 * BLOCK + NZ * t, 2 * BLOCK + NZ * (t + 1))
            by = slice(BLOCK + NZ * t, BLOCK + NZ * (t + 1))
            if side == 0:
                return jnp.where(first, out[0, at], pair[0, by]) * low
            return jnp.where(first, pair[1, by], out[1, at]) * high

        base = 0 if side == 0 else HALO + ROWS
        halo, face = tile(8), tile(9)
        for q in range(4):
            k_s[base + q, :, 0:LANES] = tile(q)
            k_s[base + q, :, LANES:] = beside(roll(halo, -8 * q, 1), roll(halo, 88 - 8 * q, 1), 4)
        for t in range(3):
            q = t + 1 - side
            r_s[base + q, :, 0:LANES] = tile(4 + t)
            r_s[base + q, :, LANES:] = beside(roll(halo, -8 * q - 4, 1), roll(halo, 92 - 8 * q, 1), 3)
        v_out = join(tile(7), beside(roll(face, -32, 1), face, 4))
        if side == 0:
            v_in = join(it[0], beside(roll(edges[0], -32, 1), roll(edges[1], 64, 1), 4))
            through = flux(k_s[HALO - 1], k_s[HALO], v_out, v_in)
            r_s[HALO - 1] = r_s[HALO - 1] - through
            r_s[HALO] = r_s[HALO] + through
        else:
            v_in = join(it[ROWS - 1], beside(roll(edges[0], -96, 1), edges[1], 4))
            through = flux(k_s[HALO + ROWS - 1], k_s[HALO + ROWS], v_in, v_out)
            r_s[HALO + ROWS - 1] = r_s[HALO + ROWS - 1] - through
            r_s[HALO + ROWS] = r_s[HALO + ROWS] + through
    zero = jnp.zeros((NZ, 2 * LANES), F32)
    s_s[0] = zero
    s_s[EXT - 1] = zero
    prepare(EXT, ROWS, HALO, SWEEPS, 0.5, k_s, r_s, s_s, x_s, c_s, LANES)
    sweep(1, EXT - 1, ROWS, HALO, SWEEPS, r_s, s_s, x_s, c_s, LANES)


def coarse_kernel(flags, chip, out, near, x_ref, p_ref, k_s, r_s, s_s, c_s):
    coarse_part(flags, chip, out, near, x_ref, k_s, r_s, s_s, c_s)
    lane = iota((CZ, LANES), 1)
    for a in range(4):
        p_ref[pl.ds(a, CZ, stride=4), :] = jnp.where(lane < CLANES, x_ref[a], roll(x_ref[a + 4], CLANES, 1))


def fine_kernel(
    flags, it, r_in, k_in, ou, od, ru, rd, pair, out, x_c, o_ref, x_f, k_f, r_f, s_f, c_f, wide_s
):
    fine_part(flags, it, r_in, k_in, pair, out, ou, od, ru, rd, x_f, k_f, r_f, s_f, c_f)
    child, parent = iota((LANES, LANES), 1) // 2, iota((LANES, LANES), 0)
    spread = jnp.where(child == parent, F32(1.0), F32(0.0))
    wide = dot(x_c[...].reshape(CROWS * CZ, LANES), spread).reshape(CROWS, CZ, LANES)
    wide_s[:, pl.ds(0, CZ, stride=2), :] = wide
    wide_s[:, pl.ds(1, CZ, stride=2), :] = wide
    for i in range(ROWS):
        o_ref[i] = it[i] + x_f[i] + wide_s[i // 2]


def planes_kernel(sources, planes, p_ref, o_ref):
    half = sources // 2
    lane = iota((half, LANES), 1)
    for q in range(planes):
        for a in range(4):
            even = p_ref[pl.ds(4 * q + a, half, stride=8 * planes), :]
            odd = p_ref[pl.ds(4 * (planes + q) + a, half, stride=8 * planes), :]
            to = (a * planes + q) * half
            o_ref[to:to + half] = jnp.where(lane < CLANES, even, roll(odd, CLANES, 1))
            to = ((a + 4) * planes + q) * half
            o_ref[to:to + half] = jnp.where(lane < CLANES, roll(even, CLANES, 1), odd)


def call(kernel, outs, scratch, in_smem=False, operands=(), flops=1000000, copies=False):
    vmem = pl.BlockSpec(memory_space=pltpu.VMEM)
    specs = [pl.BlockSpec(memory_space=pltpu.HBM) if copies else vmem] * len(operands)
    if in_smem:
        specs[0] = pl.BlockSpec(memory_space=pltpu.SMEM)
    size = sum(4 * x.size for x in operands) + sum(4 * o.size for o in outs)
    multiple = len(outs) > 1
    held = [pltpu.VMEM(s, F32) for s in scratch]
    if copies:
        held += [pltpu.VMEM(x.shape, x.dtype) for x in operands]
        held.append(pltpu.SemaphoreType.DMA((len(operands), PARTS)))
    return pl.pallas_call(
        kernel,
        out_shape=outs if multiple else outs[0],
        in_specs=specs,
        out_specs=[vmem] * len(outs) if multiple else vmem,
        scratch_shapes=held,
        compiler_params=pltpu.CompilerParams(vmem_limit_bytes=(54500 if copies else 40960) * 1024),
        cost_estimate=pl.CostEstimate(flops=flops, bytes_accessed=size, transcendentals=0),
    )(*operands)


def shape(*dims):
    return jax.ShapeDtypeStruct(dims, F32)


def on_device(iterate, source, labels):
    n_gx, n_gy = lax.axis_size("gx"), lax.axis_size("gy")
    gx = lax.axis_index("gx")
    flags = jnp.stack([gx % 2, gx > 0, gx < n_gx - 1, gx > 1, gx < n_gx - 2]).astype(jnp.int32)
    chips = [[i, i + 1] for i in range(0, n_gx, 2)]
    between = [[i, (i + 1) % n_gx] for i in range(1, n_gx, 2)]
    own = shape(ROWS, NZ, LANES)
    strip = shape(3 * NZ, LANES)
    resid, cond, coarse, up, dn = call(
        residual_kernel,
        [own, own, shape(CROWS, CZ, LANES), strip, strip],
        [(2, CROWS, NZ, LANES)],
        False,
        (iterate, source, labels),
        copies=True,
    )
    onward = [(i, i + 1) for i in range(n_gy - 1)]
    back = [(i + 1, i) for i in range(n_gy - 1)]
    from_left = lax.ppermute(up, "gy", onward)
    from_right = lax.ppermute(dn, "gy", back)
    strips = (up, dn, from_left, from_right)
    block, near = call(
        block_kernel,
        [shape(BLOCK + NEAR, LANES), shape(NEAR, LANES)],
        [(2, NZ, LANES)],
        True,
        (flags, iterate, resid, cond, coarse, *strips),
    )
    pair = lax.all_gather(block, "gx", axis_index_groups=chips)
    chip = call(chip_kernel, [shape(2 * BLOCK + NEAR, LANES)], [(2, NZ, LANES)], False, (pair, near))
    beyond = lax.all_gather(chip, "gx", axis_index_groups=between)
    relay = call(relay_kernel, [shape(BLOCK + CZ, LANES)], [(2, NZ, LANES)], True, (flags, beyond))
    relay = lax.all_gather(relay, "gx", axis_index_groups=chips)
    rows, wide = (CEXT, CZ, LANES), (EXT, NZ, 2 * LANES)
    coarse_out, planes = call(
        coarse_kernel,
        [shape(CROWS, CZ, LANES), shape(4 * CZ, LANES)],
        [rows, rows, rows, (6, *rows)],
        True,
        (flags, chip, beyond, relay),
    )
    per = CZ // n_gy
    planes = lax.all_to_all(planes.reshape(n_gy, 4 * per, LANES), "gy", split_axis=0, concat_axis=0, tiled=True)
    corrected = call(
        fine_kernel,
        [own],
        [(ROWS, NZ, LANES), wide, wide, wide, (6, *wide), (CROWS, NZ, LANES)],
        True,
        (flags, iterate, resid, cond, *strips, pair, beyond, coarse_out),
        flops=20000000,
    )
    owned = call(
        functools.partial(planes_kernel, n_gy, per),
        [shape(4 * CZ, LANES)],
        [],
        False,
        (planes.reshape(4 * CZ, LANES),),
    ).reshape(CROWS, per, CLANES * n_gy)
    return corrected, owned


def solution(mesh):
    spec = P("gx", None, "gy")
    return jax.shard_map(
        on_device, mesh=mesh, in_specs=(spec, spec, spec), out_specs=(spec, P("gx", "gy", None)), check_vma=False
    )
```

```python
import functools

import jax
import jax.numpy as jnp
from jax import lax
from jax.experimental import pallas as pl
from jax.experimental.pallas import tpu as pltpu
from jax.sharding import PartitionSpec as P

SWEEPS = 4
COARSE_SWEEPS = 16
TABLE = (0.5, 1.0, 2.5, 6.0)
LOWER = 0.25
UPPER = 2.0
F32 = jnp.float32

ROWS, NZ, LANES = 16, 32, 128
CROWS, CZ, CLANES = 8, 16, 64
HALO = SWEEPS
EXT = ROWS + 2 * HALO
CEXT = CROWS + 2 * COARSE_SWEEPS
OWN = CROWS * CZ
BLOCK = OWN + 4 * CZ
NEAR = 10 * NZ
STRIP = 3 * NZ
UP, DN, FACING = OWN, OWN + STRIP, OWN + 2 * STRIP
SHARED = FACING + 8 * NZ
PARTS = 4


def weights(sweeps):
    centre = (UPPER + LOWER) / 2.0
    radius = (UPPER - LOWER) / 2.0
    sigma = centre / radius
    rho = 1.0 / sigma
    pairs = []
    for _ in range(1, sweeps):
        rho_new = 1.0 / (2.0 * sigma - rho)
        pairs.append((rho_new * rho, 2.0 * rho_new / radius))
        rho = rho_new
    return 1.0 / centre, pairs


def conduct(labels):
    total = jnp.zeros(labels.shape, F32)
    for label_id, value in enumerate(TABLE):
        total = jnp.where(labels == label_id, F32(value), total)
    return total


def roll(x, shift, axis):
    size = x.shape[axis]
    shift = shift % size
    return x if shift == 0 else pltpu.roll(x, shift, axis)


def iota(shape, axis):
    return lax.broadcasted_iota(jnp.int32, shape, axis)


def flux(k_a, k_b, v_a, v_b):
    return 0.5 * (k_a + k_b) * (v_a - v_b)


def dot(a, b):
    return jnp.dot(a, b, precision=lax.Precision.HIGHEST, preferred_element_type=F32)


def residual_kernel(flags, it_in, src_in, lab_in, r_ref, k_ref, a_ref, pool, it, src, lab, sems):
    copies = []
    for part in range(PARTS):
        rows = pl.ds(part * ROWS // PARTS, ROWS // PARTS)
        copies.append(
            [
                pltpu.make_async_copy(a.at[rows], b.at[rows], sems.at[n, part])
                for n, (a, b) in enumerate(((lab_in, lab), (it_in, it), (src_in, src)))
            ]
        )
        for copy in copies[-1]:
            copy.start()

    def arrive(part):
        for copy in copies[part]:
            copy.wait()
        for i in range(part * ROWS // PARTS, (part + 1) * ROWS // PARTS):
            k_ref[i] = conduct(lab[i])

    arrive(0)
    z, lane = iota((NZ, LANES), 0), iota((NZ, LANES), 1)
    zero = jnp.zeros((NZ, LANES), F32)
    before = zero
    up = dn = zero
    for i in range(ROWS):
        if (i + 1) % (ROWS // PARTS) == 0 and i < ROWS - 1:
            arrive((i + 1) // (ROWS // PARTS))
        k, v = k_ref[i], it[i]
        after = flux(k, k_ref[i + 1], v, it[i + 1]) if i < ROWS - 1 else zero
        fy = jnp.where(lane < LANES - 1, flux(k, roll(k, -1, 1), v, roll(v, -1, 1)), 0.0)
        k_z = jnp.where(z < NZ - 1, roll(k, -1, 0), 0.0)
        v_z = jnp.where(z < NZ - 1, roll(v, -1, 0), 0.0)
        fz = flux(k, k_z, v, v_z)
        fz_in = jnp.where(z > 0, roll(fz, 1, 0), -0.5 * k * v)
        r = src[i] - after + before - fy + roll(fy, 1, 1) - fz + fz_in
        r_ref[i] = r
        before = after
        j = i // 2
        if i % 2 == 0:
            r_even, k_even = r, k
        else:
            pool[0, j] = r_even + r
            pool[1, j] = k_even + k
        off = 8 * i
        here = (lane >= off) & (lane < off + 8)
        top = jnp.where(lane >= 124, k, jnp.where(lane >= 121, roll(r, -4, 1), roll(v, -7, 1)))
        bottom = jnp.where(lane < 4, k, jnp.where(lane < 7, roll(r, 4, 1), roll(v, 7, 1)))
        up = jnp.where(here, roll(top, off - 120, 1), up)
        dn = jnp.where(here, roll(bottom, off, 1), dn)
    a_ref[UP:UP + NZ] = up
    a_ref[DN:DN + NZ] = dn
    up = dn = zero
    for g, edge in enumerate((k_ref[0], it[0], k_ref[ROWS - 1], it[ROWS - 1])):
        here = (lane >= 32 * g) & (lane < 32 * g + 32)
        up = jnp.where(here, roll(edge, 32 * g - 96, 1), up)
        dn = jnp.where(here, roll(edge, 32 * g, 1), dn)
    a_ref[UP + NZ:UP + 2 * NZ] = up
    a_ref[DN + NZ:DN + 2 * NZ] = dn
    tops = pool[:, :, pl.ds(0, CZ, stride=2), :] + pool[:, :, pl.ds(1, CZ, stride=2), :]
    child, parent = iota((LANES, LANES), 0) // 2, iota((LANES, LANES), 1)
    to_left = jnp.where(child == parent, F32(1.0), F32(0.0))
    to_right = jnp.where(child == parent - CLANES, F32(0.125), F32(0.0))
    coarse = dot(tops[0].reshape(CROWS * CZ, LANES), to_left) + dot(tops[1].reshape(CROWS * CZ, LANES), to_right)
    a_ref[0:OWN] = coarse
    coarse = coarse.reshape(CROWS, CZ, LANES)
    lane = iota((CZ, LANES), 1)
    for t in range(2):
        up = dn = jnp.zeros((CZ, LANES), F32)
        for j in range(4 * t, 4 * t + 4):
            row = coarse[j]
            off = (j % 4) * 32
            at_r = (lane >= off) & (lane < off + 16)
            at_k = (lane >= off + 16) & (lane < off + 32)
            up = jnp.where(at_r, roll(row, off - 48, 1), jnp.where(at_k, roll(row, off + 16 - 112, 1), up))
            dn = jnp.where(at_r, roll(row, off, 1), jnp.where(at_k, roll(row, off + 16 - 64, 1), dn))
        a_ref[UP + 2 * NZ + CZ * t:UP + 2 * NZ + CZ * (t + 1)] = up
        a_ref[DN + 2 * NZ + CZ * t:DN + 2 * NZ + CZ * (t + 1)] = dn
    first = flags[0] == 0
    rows = [jnp.where(first, k_ref[ROWS - 4 + t], k_ref[t]) for t in range(4)]
    rows += [jnp.where(first, r_ref[ROWS - 3 + t], r_ref[t]) for t in range(3)]
    rows.append(jnp.where(first, it[ROWS - 1], it[0]))
    for t in range(8):
        a_ref[FACING + NZ * t:FACING + NZ * (t + 1)] = rows[t]


def strip_flux(up, dn):
    lane = iota(up.shape, 1)
    face = flux(roll(up, -7, 1), dn, up, roll(dn, -7, 1))
    return jnp.where(lane % 8 == 0, face, 0.0)


def came(flags, strips, n, start, rows):
    at = slice(STRIP * n + start, STRIP * n + start + rows)
    rd = strips[flags[5], at] * flags[7].astype(F32)
    return rd, strips[1 - flags[5], at] * flags[6].astype(F32)


def completed(ou, od, ru, rd):
    right = strip_flux(ou, rd)
    left = strip_flux(ru, od)
    return rd + roll(right, 4, 1), ru - roll(left, 3, 1), right, left


def beside_rows(flags, strips, n, ks, rs, v, done, top):
    lane = iota((NZ, LANES), 1)
    dn, up, right, left = done
    k_row, r_row = (ROWS - 4, ROWS - 3) if top else (0, 0)
    tiles = list(ks)
    for t in range(3):
        i = r_row + t
        r = rs[t] - jnp.where(lane == 127, roll(right, 127 - 8 * i, 1), 0.0)
        tiles.append(r + jnp.where(lane == 0, roll(left, -8 * i, 1), 0.0))
    tiles.append(v)
    tiles.append(jnp.where(lane < 32, roll(dn, -8 * k_row, 1), roll(up, 32 - 8 * k_row, 1)))
    tiles.append(outermost(flags, strips, n, top))
    return tiles


def outermost(flags, strips, n, top):
    lane = iota((NZ, LANES), 1)
    shift = 64 if top else 0
    rd, ru = came(flags, strips, n, NZ, NZ)
    return jnp.where(lane < 64, roll(rd, -shift, 1), roll(ru, 64 - shift, 1))


def edge_flux(a, b, pool):
    pool[0] = flux(a(3), b(0), a(7), b(7))
    u, w = a(9), b(9)
    pool[1] = flux(u, w, roll(u, -32, 1), roll(w, -32, 1))
    sums = pool[:, pl.ds(0, CZ, stride=2), :] + pool[:, pl.ds(1, CZ, stride=2), :]
    child, parent = iota((LANES, LANES), 0), iota((LANES, LANES), 1)
    own = jnp.where(child // 2 == parent, F32(1.0), F32(0.0))
    right = (child < 32) & (child // 2 + 64 == parent)
    left = (child >= 64) & (child < 96) & (child // 2 + 80 == parent)
    beyond = jnp.where(right | left, F32(1.0), F32(0.0))
    return dot(sums[0], own) + dot(sums[1], beyond)


def chip_kernel(flags, it, r_in, k_in, pair, strips, o_ref, pool):
    first = flags[0] == 0
    lane = iota((CZ, LANES), 1)
    nears = []
    for n in range(2):
        rd, ru = came(flags, strips, n, 0, NZ)
        done = completed(pair[n, UP:UP + NZ], pair[n, DN:DN + NZ], ru, rd)
        pool[0] = done[2] + roll(done[2], -8, 1)
        pool[1] = done[3] + roll(done[3], -8, 1)
        sums = pool[:, pl.ds(0, CZ, stride=2), :] + pool[:, pl.ds(1, CZ, stride=2), :]
        base = BLOCK * n
        for j in range(CROWS):
            value = pair[n, CZ * j:CZ * (j + 1)] - jnp.where(lane == 63, roll(sums[0], 63 - 16 * j, 1), 0.0)
            value = value + jnp.where(lane == 0, roll(sums[1], -16 * j, 1), 0.0)
            o_ref[base + CZ * j:base + CZ * (j + 1)] = value
        for t in range(2):
            more, less = came(flags, strips, n, 2 * NZ + CZ * t, CZ)
            for q in range(4):
                src = 16 * (4 * t + q)
                more = more + jnp.where(lane == 32 * q, roll(sums[0], 32 * q - src, 1), 0.0)
                less = less - jnp.where(lane == 32 * q + 15, roll(sums[1], 32 * q + 15 - src, 1), 0.0)
            o_ref[base + OWN + CZ * t:base + OWN + CZ * (t + 1)] = more
            o_ref[base + OWN + CZ * (2 + t):base + OWN + CZ * (3 + t)] = less
        k_row, r_row, v_row = (ROWS - 4, ROWS - 3, ROWS - 1) if n else (0, 0, 0)
        ks = [k_in[k_row + t] for t in range(4)]
        rs = [r_in[r_row + t] for t in range(3)]
        nears.append(beside_rows(flags, strips, n, ks, rs, it[v_row], done, n == 1))
    for t in range(10):
        o_ref[2 * BLOCK + NZ * t:2 * BLOCK + NZ * (t + 1)] = jnp.where(first, nears[0][t], nears[1][t])

    def tile(n):
        def get(t):
            if t == 9:
                return outermost(flags, strips, n, n == 0)
            return pair[n, FACING + NZ * t:FACING + NZ * (t + 1)]

        return get

    inner = edge_flux(tile(0), tile(1), pool)
    for n, j in ((0, CROWS - 1), (1, 0)):
        change = inner if n else -inner
        off = 32 * (j % 4)
        side = (lane >= off) & (lane < off + 16)
        changes = (
            (CZ * j, jnp.where(lane < CLANES, change, 0.0)),
            (OWN + CZ * (j // 4), jnp.where(side, roll(change, off - 64, 1), 0.0)),
            (OWN + CZ * (2 + j // 4), jnp.where(side, roll(change, off - 112, 1), 0.0)),
        )
        for at, part in changes:
            at = BLOCK * n + at
            o_ref[at:at + CZ] = o_ref[at:at + CZ] + part


def relay_kernel(flags, out, o_ref, pool):
    first = flags[0] == 0
    low, high = flags[1].astype(F32), flags[2].astype(F32)

    def tile(n, valid):
        return lambda t: out[n, 2 * BLOCK + NZ * t:2 * BLOCK + NZ * (t + 1)] * valid

    outer = edge_flux(tile(0, low), tile(1, high), pool)
    o_ref[0:BLOCK] = jnp.where(first, out[0, BLOCK:2 * BLOCK] * low, out[1, 0:BLOCK] * high)
    o_ref[BLOCK:] = outer


def sweep(lo, hi, mid, shift, sweeps, r_s, s_s, x_s, c_s, width):
    start, pairs = weights(sweeps)
    for n in range(1, sweeps):
        keep, add = pairs[n - 1]
        prev, here = s_s[lo + n - 1], s_s[lo + n]
        for i in range(lo + n, hi - n):
            ahead = s_s[i + 1]
            total = c_s[0, i] * ahead + c_s[1, i] * prev
            total = total + c_s[2, i] * roll(here, -1, 0) + c_s[3, i] * roll(here, 1, 0)
            total = total + c_s[4, i] * roll(here, -1, 1) + c_s[5, i] * roll(here, 1, 1)
            r = r_s[i] - (here - total)
            step = keep * here + add * r
            r_s[i] = r
            s_s[i] = step
            if shift <= i < shift + mid:
                x_s[i - shift] = x_s[i - shift] + (step[:, 0:width] if width else step)
            prev, here = here, ahead


def prepare(rows, mid, shift, sweeps, factor, k_s, r_s, s_s, x_s, c_s, width):
    depth = k_s.shape[1]
    z = iota(k_s.shape[1:], 0)
    start, _ = weights(sweeps)
    below = factor * (k_s[0] + k_s[1])
    for i in range(1, rows - 1):
        k = k_s[i]
        above = factor * (k + k_s[i + 1])
        z_up = factor * (k + jnp.where(z < depth - 1, roll(k, -1, 0), 0.0))
        z_dn = factor * (k + jnp.where(z > 0, roll(k, 1, 0), 0.0))
        y_up = factor * (k + roll(k, -1, 1))
        y_dn = factor * (k + roll(k, 1, 1))
        diagonal = above + below + z_up + z_dn + y_up + y_dn
        inverse = jnp.where(k > 0, 1.0 / jnp.where(k > 0, diagonal, 1.0), 0.0)
        c_s[0, i] = inverse * above
        c_s[1, i] = inverse * below
        c_s[2, i] = jnp.where(z < depth - 1, inverse * z_up, 0.0)
        c_s[3, i] = jnp.where(z > 0, inverse * z_dn, 0.0)
        c_s[4, i] = inverse * y_up
        c_s[5, i] = inverse * y_dn
        r = inverse * r_s[i]
        r_s[i] = r
        s_s[i] = r * start
        if shift <= i < shift + mid:
            x_s[i - shift] = (r[:, 0:width] if width else r) * start
        below = above


def coarse_part(flags, chip, out, near, x_s, k_s, r_s, s_s, c_s):
    first = flags[0] == 0
    low, high = flags[3].astype(F32), flags[4].astype(F32)
    own = near[flags[0], BLOCK:]
    other = near[1 - flags[0], BLOCK:]
    f_low = jnp.where(first, own, other)
    f_high = jnp.where(first, other, own)
    lane = iota((CZ, LANES), 1)

    def packed(at):
        up = slice(BLOCK + at.start, BLOCK + at.stop)
        return (
            jnp.where(first, out[0, at] * low, near[0, at]),
            jnp.where(first, out[0, up] * low, chip[at]),
            jnp.where(first, chip[at], chip[up]),
            jnp.where(first, chip[up], out[1, at] * high),
            jnp.where(first, near[1, at], out[1, up] * high),
        )

    sides = [packed(slice(OWN + CZ * t, OWN + CZ * (t + 1))) for t in range(4)]
    for j in range(CROWS):
        off = 32 * (j % 4)
        rows = packed(slice(CZ * j, CZ * (j + 1)))
        for b in range(5):
            more, less = sides[j // 4][b], sides[2 + j // 4][b]
            for n, dest in enumerate((r_s, k_s)):
                value = jnp.where(lane < CLANES, roll(rows[b], -CLANES * n, 1), 0.0)
                value = jnp.where((lane >= 64) & (lane < 80), roll(more, 64 - off - 16 * n, 1), value)
                dest[CROWS * b + j] = jnp.where(lane >= 112, roll(less, 112 - off - 16 * n, 1), value)
    low_at, high_at = jnp.where(first, 16, 8), jnp.where(first, 32, 24)
    r_s[low_at - 1] = r_s[low_at - 1] - f_low
    r_s[low_at] = r_s[low_at] + f_low
    r_s[high_at - 1] = r_s[high_at - 1] - f_high
    r_s[high_at] = r_s[high_at] + f_high
    zero = jnp.zeros((CZ, LANES), F32)
    s_s[0] = zero
    s_s[CEXT - 1] = zero
    prepare(CEXT, CROWS, COARSE_SWEEPS, COARSE_SWEEPS, 2.0, k_s, r_s, s_s, x_s, c_s, 0)
    sweep(1, CEXT - 1, CROWS, COARSE_SWEEPS, COARSE_SWEEPS, r_s, s_s, x_s, c_s, 0)


def fine_part(flags, it, r_in, k_in, pair, strips, out, x_s, k_s, r_s, s_s, c_s):
    first = flags[0] == 0
    low, high = flags[1].astype(F32), flags[2].astype(F32)
    lane = iota((NZ, LANES), 1)
    facing = []
    for n in range(2):
        rd, ru = came(flags, strips, n, 0, NZ)
        done = completed(pair[n, UP:UP + NZ], pair[n, DN:DN + NZ], ru, rd)
        rows = [pair[n, FACING + NZ * t:FACING + NZ * (t + 1)] for t in range(8)]
        facing.append(beside_rows(flags, strips, n, rows[0:4], rows[4:7], rows[7], done, n == 0))
    mine = flags[0]
    rd, ru = (jnp.where(first, a, b) for a, b in zip(came(flags, strips, 0, 0, NZ), came(flags, strips, 1, 0, NZ)))
    dn, up, right, left = completed(pair[mine, UP:UP + NZ], pair[mine, DN:DN + NZ], ru, rd)

    def beside(rights, lefts, count):
        return jnp.where(lane < count, rights, jnp.where(lane >= LANES - count, lefts, 0.0))

    def join(a, b):
        return jnp.concatenate([a, b], axis=1)

    for i in range(ROWS):
        off = 8 * i
        e = HALO + i
        k_s[e, :, 0:LANES] = k_in[i]
        k_s[e, :, LANES:] = beside(roll(dn, -off, 1), roll(up, 120 - off, 1), 4)
        r = r_in[i] - jnp.where(lane == 127, roll(right, 127 - off, 1), 0.0)
        r_s[e, :, 0:LANES] = r + jnp.where(lane == 0, roll(left, -off, 1), 0.0)
        r_s[e, :, LANES:] = beside(roll(dn, -off - 4, 1), roll(up, 124 - off, 1), 3)
    edges = [jnp.where(first, a, b) for a, b in zip(came(flags, strips, 0, NZ, NZ), came(flags, strips, 1, NZ, NZ))]
    for side in range(2):
        def tile(t, side=side):
            at = slice(2 * BLOCK + NZ * t, 2 * BLOCK + NZ * (t + 1))
            if side == 0:
                return jnp.where(first, out[0, at], facing[0][t]) * low
            return jnp.where(first, facing[1][t], out[1, at]) * high

        base = 0 if side == 0 else HALO + ROWS
        halo, face = tile(8), tile(9)
        for q in range(4):
            k_s[base + q, :, 0:LANES] = tile(q)
            k_s[base + q, :, LANES:] = beside(roll(halo, -8 * q, 1), roll(halo, 88 - 8 * q, 1), 4)
        for t in range(3):
            q = t + 1 - side
            r_s[base + q, :, 0:LANES] = tile(4 + t)
            r_s[base + q, :, LANES:] = beside(roll(halo, -8 * q - 4, 1), roll(halo, 92 - 8 * q, 1), 3)
        v_out = join(tile(7), beside(roll(face, -32, 1), face, 4))
        if side == 0:
            v_in = join(it[0], beside(roll(edges[0], -32, 1), roll(edges[1], 64, 1), 4))
            through = flux(k_s[HALO - 1], k_s[HALO], v_out, v_in)
            r_s[HALO - 1] = r_s[HALO - 1] - through
            r_s[HALO] = r_s[HALO] + through
        else:
            v_in = join(it[ROWS - 1], beside(roll(edges[0], -96, 1), edges[1], 4))
            through = flux(k_s[HALO + ROWS - 1], k_s[HALO + ROWS], v_in, v_out)
            r_s[HALO + ROWS - 1] = r_s[HALO + ROWS - 1] - through
            r_s[HALO + ROWS] = r_s[HALO + ROWS] + through
    zero = jnp.zeros((NZ, 2 * LANES), F32)
    s_s[0] = zero
    s_s[EXT - 1] = zero
    prepare(EXT, ROWS, HALO, SWEEPS, 0.5, k_s, r_s, s_s, x_s, c_s, LANES)
    sweep(1, EXT - 1, ROWS, HALO, SWEEPS, r_s, s_s, x_s, c_s, LANES)


def coarse_kernel(flags, chip, out, near, x_ref, p_ref, k_s, r_s, s_s, c_s):
    coarse_part(flags, chip, out, near, x_ref, k_s, r_s, s_s, c_s)
    lane = iota((CZ, LANES), 1)
    for a in range(4):
        p_ref[pl.ds(a, CZ, stride=4), :] = jnp.where(lane < CLANES, x_ref[a], roll(x_ref[a + 4], CLANES, 1))


def fine_kernel(
    flags, it, r_in, k_in, pair, strips, out, x_c, o_ref, x_f, k_f, r_f, s_f, c_f, wide_s
):
    fine_part(flags, it, r_in, k_in, pair, strips, out, x_f, k_f, r_f, s_f, c_f)
    child, parent = iota((LANES, LANES), 1) // 2, iota((LANES, LANES), 0)
    spread = jnp.where(child == parent, F32(1.0), F32(0.0))
    wide = dot(x_c[...].reshape(CROWS * CZ, LANES), spread).reshape(CROWS, CZ, LANES)
    wide_s[:, pl.ds(0, CZ, stride=2), :] = wide
    wide_s[:, pl.ds(1, CZ, stride=2), :] = wide
    for i in range(ROWS):
        o_ref[i] = it[i] + x_f[i] + wide_s[i // 2]


def planes_kernel(sources, planes, p_ref, o_ref):
    half = sources // 2
    lane = iota((half, LANES), 1)
    for q in range(planes):
        for a in range(4):
            even = p_ref[pl.ds(4 * q + a, half, stride=8 * planes), :]
            odd = p_ref[pl.ds(4 * (planes + q) + a, half, stride=8 * planes), :]
            to = (a * planes + q) * half
            o_ref[to:to + half] = jnp.where(lane < CLANES, even, roll(odd, CLANES, 1))
            to = ((a + 4) * planes + q) * half
            o_ref[to:to + half] = jnp.where(lane < CLANES, roll(even, CLANES, 1), odd)


def call(kernel, outs, scratch, in_smem=False, operands=(), flops=1000000, copies=False):
    vmem = pl.BlockSpec(memory_space=pltpu.VMEM)
    specs = [pl.BlockSpec(memory_space=pltpu.HBM) if copies else vmem] * len(operands)
    if in_smem:
        specs[0] = pl.BlockSpec(memory_space=pltpu.SMEM)
    size = sum(4 * x.size for x in operands) + sum(4 * o.size for o in outs)
    multiple = len(outs) > 1
    held = [pltpu.VMEM(s, F32) for s in scratch]
    if copies:
        held += [pltpu.VMEM(x.shape, x.dtype) for x in operands[1:]]
        held.append(pltpu.SemaphoreType.DMA((len(operands) - 1, PARTS)))
    return pl.pallas_call(
        kernel,
        out_shape=outs if multiple else outs[0],
        in_specs=specs,
        out_specs=[vmem] * len(outs) if multiple else vmem,
        scratch_shapes=held,
        compiler_params=pltpu.CompilerParams(vmem_limit_bytes=(54500 if copies else 40960) * 1024),
        cost_estimate=pl.CostEstimate(flops=flops, bytes_accessed=size, transcendentals=0),
    )(*operands)


def shape(*dims):
    return jax.ShapeDtypeStruct(dims, F32)


def on_device(iterate, source, labels):
    n_gx, n_gy = lax.axis_size("gx"), lax.axis_size("gy")
    gx = lax.axis_index("gx")
    gy = lax.axis_index("gy")
    flags = [gx % 2, gx > 0, gx < n_gx - 1, gx > 1, gx < n_gx - 2, gy % 2, gy > 0, gy < n_gy - 1]
    flags = jnp.stack([jnp.int32(f) for f in flags])
    chips = [[i, i + 1] for i in range(0, n_gx, 2)]
    between = [[i, (i + 1) % n_gx] for i in range(1, n_gx, 2)]
    along = [
        [i * n_gy + j, i * n_gy + (j + 1) % n_gy] for i in range(n_gx) for j in range(i % 2, n_gy, 2)
    ]
    own = shape(ROWS, NZ, LANES)
    resid, cond, shared = call(
        residual_kernel,
        [own, own, shape(SHARED, LANES)],
        [(2, CROWS, NZ, LANES)],
        True,
        (flags, iterate, source, labels),
        copies=True,
    )
    pair = lax.all_gather(shared, "gx", axis_index_groups=chips)
    lower = (gx + gy) % 2 == 0
    strips = jnp.where(lower, pair[:, UP:DN], pair[:, DN:FACING]).reshape(2 * STRIP, LANES)
    strips = lax.all_gather(strips, ("gx", "gy"), axis_index_groups=along)
    strips = lax.all_gather(jnp.where(lower, strips[1], strips[0]), "gx", axis_index_groups=chips)
    chip = call(
        chip_kernel,
        [shape(2 * BLOCK + NEAR, LANES)],
        [(2, NZ, LANES)],
        True,
        (flags, iterate, resid, cond, pair, strips),
    )
    beyond = lax.all_gather(chip, "gx", axis_index_groups=between)
    relay = call(relay_kernel, [shape(BLOCK + CZ, LANES)], [(2, NZ, LANES)], True, (flags, beyond))
    relay = lax.all_gather(relay, "gx", axis_index_groups=chips)
    rows, wide = (CEXT, CZ, LANES), (EXT, NZ, 2 * LANES)
    coarse_out, planes = call(
        coarse_kernel,
        [shape(CROWS, CZ, LANES), shape(4 * CZ, LANES)],
        [rows, rows, rows, (6, *rows)],
        True,
        (flags, chip, beyond, relay),
    )
    per = CZ // n_gy
    planes = lax.all_to_all(planes.reshape(n_gy, 4 * per, LANES), "gy", split_axis=0, concat_axis=0, tiled=True)
    corrected = call(
        fine_kernel,
        [own],
        [(ROWS, NZ, LANES), wide, wide, wide, (6, *wide), (CROWS, NZ, LANES)],
        True,
        (flags, iterate, resid, cond, pair, strips, beyond, coarse_out),
        flops=20000000,
    )
    owned = call(
        functools.partial(planes_kernel, n_gy, per),
        [shape(4 * CZ, LANES)],
        [],
        False,
        (planes.reshape(4 * CZ, LANES),),
    ).reshape(CROWS, per, CLANES * n_gy)
    return corrected, owned


def solution(mesh):
    spec = P("gx", None, "gy")
    return jax.shard_map(
        on_device, mesh=mesh, in_specs=(spec, spec, spec), out_specs=(spec, P("gx", "gy", None)), check_vma=False
    )
```

```python
import functools

import jax
import jax.numpy as jnp
from jax import lax
from jax.experimental import pallas as pl
from jax.experimental.pallas import tpu as pltpu
from jax.sharding import PartitionSpec as P

SWEEPS = 4
COARSE_SWEEPS = 16
TABLE = (0.5, 1.0, 2.5, 6.0)
LOWER = 0.25
UPPER = 2.0
F32 = jnp.float32

ROWS, NZ, LANES = 16, 32, 128
CROWS, CZ, CLANES = 8, 16, 64
HALO = SWEEPS
EXT = ROWS + 2 * HALO
CEXT = CROWS + 2 * COARSE_SWEEPS
OWN = CROWS * CZ
BLOCK = OWN + 4 * CZ
NEAR = 10 * NZ
STRIP = 3 * NZ
UP, DN, FACING = OWN, OWN + STRIP, OWN + 2 * STRIP
SHARED = FACING + 8 * NZ
PARTS = 4


def weights(sweeps):
    centre = (UPPER + LOWER) / 2.0
    radius = (UPPER - LOWER) / 2.0
    sigma = centre / radius
    rho = 1.0 / sigma
    pairs = []
    for _ in range(1, sweeps):
        rho_new = 1.0 / (2.0 * sigma - rho)
        pairs.append((rho_new * rho, 2.0 * rho_new / radius))
        rho = rho_new
    return 1.0 / centre, pairs


def conduct(labels):
    total = jnp.zeros(labels.shape, F32)
    for label_id, value in enumerate(TABLE):
        total = jnp.where(labels == label_id, F32(value), total)
    return total


def roll(x, shift, axis):
    size = x.shape[axis]
    shift = shift % size
    return x if shift == 0 else pltpu.roll(x, shift, axis)


def iota(shape, axis):
    return lax.broadcasted_iota(jnp.int32, shape, axis)


def flux(k_a, k_b, v_a, v_b):
    return 0.5 * (k_a + k_b) * (v_a - v_b)


def dot(a, b):
    return jnp.dot(a, b, precision=lax.Precision.HIGHEST, preferred_element_type=F32)


def residual_kernel(flags, it_in, src_in, lab_in, r_ref, k_ref, a_ref, pool, it, src, lab, sems):
    copies = []
    for part in range(PARTS):
        rows = pl.ds(part * ROWS // PARTS, ROWS // PARTS)
        copies.append(
            [
                pltpu.make_async_copy(a.at[rows], b.at[rows], sems.at[n, part])
                for n, (a, b) in enumerate(((lab_in, lab), (it_in, it), (src_in, src)))
            ]
        )
        for copy in copies[-1]:
            copy.start()

    def arrive(part):
        for copy in copies[part]:
            copy.wait()
        for i in range(part * ROWS // PARTS, (part + 1) * ROWS // PARTS):
            k_ref[i] = conduct(lab[i])

    arrive(0)
    z, lane = iota((NZ, LANES), 0), iota((NZ, LANES), 1)
    zero = jnp.zeros((NZ, LANES), F32)
    before = zero
    up = dn = zero
    for i in range(ROWS):
        if (i + 1) % (ROWS // PARTS) == 0 and i < ROWS - 1:
            arrive((i + 1) // (ROWS // PARTS))
        k, v = k_ref[i], it[i]
        after = flux(k, k_ref[i + 1], v, it[i + 1]) if i < ROWS - 1 else zero
        fy = jnp.where(lane < LANES - 1, flux(k, roll(k, -1, 1), v, roll(v, -1, 1)), 0.0)
        k_z = jnp.where(z < NZ - 1, roll(k, -1, 0), 0.0)
        v_z = jnp.where(z < NZ - 1, roll(v, -1, 0), 0.0)
        fz = flux(k, k_z, v, v_z)
        fz_in = jnp.where(z > 0, roll(fz, 1, 0), -0.5 * k * v)
        r = src[i] - after + before - fy + roll(fy, 1, 1) - fz + fz_in
        r_ref[i] = r
        before = after
        j = i // 2
        if i % 2 == 0:
            r_even, k_even = r, k
        else:
            pool[0, j] = r_even + r
            pool[1, j] = k_even + k
        off = 8 * i
        here = (lane >= off) & (lane < off + 8)
        top = jnp.where(lane >= 124, k, jnp.where(lane >= 121, roll(r, -4, 1), roll(v, -7, 1)))
        bottom = jnp.where(lane < 4, k, jnp.where(lane < 7, roll(r, 4, 1), roll(v, 7, 1)))
        up = jnp.where(here, roll(top, off - 120, 1), up)
        dn = jnp.where(here, roll(bottom, off, 1), dn)
    a_ref[UP:UP + NZ] = up
    a_ref[DN:DN + NZ] = dn
    up = dn = zero
    for g, edge in enumerate((k_ref[0], it[0], k_ref[ROWS - 1], it[ROWS - 1])):
        here = (lane >= 32 * g) & (lane < 32 * g + 32)
        up = jnp.where(here, roll(edge, 32 * g - 96, 1), up)
        dn = jnp.where(here, roll(edge, 32 * g, 1), dn)
    a_ref[UP + NZ:UP + 2 * NZ] = up
    a_ref[DN + NZ:DN + 2 * NZ] = dn
    tops = pool[:, :, pl.ds(0, CZ, stride=2), :] + pool[:, :, pl.ds(1, CZ, stride=2), :]
    child, parent = iota((LANES, LANES), 0) // 2, iota((LANES, LANES), 1)
    to_left = jnp.where(child == parent, F32(1.0), F32(0.0))
    to_right = jnp.where(child == parent - CLANES, F32(0.125), F32(0.0))
    coarse = dot(tops[0].reshape(CROWS * CZ, LANES), to_left) + dot(tops[1].reshape(CROWS * CZ, LANES), to_right)
    a_ref[0:OWN] = coarse
    coarse = coarse.reshape(CROWS, CZ, LANES)
    lane = iota((CZ, LANES), 1)
    for t in range(2):
        up = dn = jnp.zeros((CZ, LANES), F32)
        for j in range(4 * t, 4 * t + 4):
            row = coarse[j]
            off = (j % 4) * 32
            at_r = (lane >= off) & (lane < off + 16)
            at_k = (lane >= off + 16) & (lane < off + 32)
            up = jnp.where(at_r, roll(row, off - 48, 1), jnp.where(at_k, roll(row, off + 16 - 112, 1), up))
            dn = jnp.where(at_r, roll(row, off, 1), jnp.where(at_k, roll(row, off + 16 - 64, 1), dn))
        a_ref[UP + 2 * NZ + CZ * t:UP + 2 * NZ + CZ * (t + 1)] = up
        a_ref[DN + 2 * NZ + CZ * t:DN + 2 * NZ + CZ * (t + 1)] = dn
    first = flags[0] == 0
    rows = [jnp.where(first, k_ref[ROWS - 4 + t], k_ref[t]) for t in range(4)]
    rows += [jnp.where(first, r_ref[ROWS - 3 + t], r_ref[t]) for t in range(3)]
    rows.append(jnp.where(first, it[ROWS - 1], it[0]))
    for t in range(8):
        a_ref[FACING + NZ * t:FACING + NZ * (t + 1)] = rows[t]


def strip_flux(up, dn):
    lane = iota(up.shape, 1)
    face = flux(roll(up, -7, 1), dn, up, roll(dn, -7, 1))
    return jnp.where(lane % 8 == 0, face, 0.0)


def came(flags, strips, n, start, rows):
    at = slice(STRIP * n + start, STRIP * n + start + rows)
    rd = strips[flags[5], at] * flags[7].astype(F32)
    return rd, strips[1 - flags[5], at] * flags[6].astype(F32)


def completed(ou, od, ru, rd):
    right = strip_flux(ou, rd)
    left = strip_flux(ru, od)
    return rd + roll(right, 4, 1), ru - roll(left, 3, 1), right, left


def beside_rows(flags, strips, n, ks, rs, v, done, top):
    lane = iota((NZ, LANES), 1)
    dn, up, right, left = done
    k_row, r_row = (ROWS - 4, ROWS - 3) if top else (0, 0)
    tiles = list(ks)
    for t in range(3):
        i = r_row + t
        r = rs[t] - jnp.where(lane == 127, roll(right, 127 - 8 * i, 1), 0.0)
        tiles.append(r + jnp.where(lane == 0, roll(left, -8 * i, 1), 0.0))
    tiles.append(v)
    tiles.append(jnp.where(lane < 32, roll(dn, -8 * k_row, 1), roll(up, 32 - 8 * k_row, 1)))
    tiles.append(outermost(flags, strips, n, top))
    return tiles


def outermost(flags, strips, n, top):
    lane = iota((NZ, LANES), 1)
    shift = 64 if top else 0
    rd, ru = came(flags, strips, n, NZ, NZ)
    return jnp.where(lane < 64, roll(rd, -shift, 1), roll(ru, 64 - shift, 1))


def edge_flux(a, b, pool):
    pool[0] = flux(a(3), b(0), a(7), b(7))
    u, w = a(9), b(9)
    pool[1] = flux(u, w, roll(u, -32, 1), roll(w, -32, 1))
    sums = pool[:, pl.ds(0, CZ, stride=2), :] + pool[:, pl.ds(1, CZ, stride=2), :]
    child, parent = iota((LANES, LANES), 0), iota((LANES, LANES), 1)
    own = jnp.where(child // 2 == parent, F32(1.0), F32(0.0))
    right = (child < 32) & (child // 2 + 64 == parent)
    left = (child >= 64) & (child < 96) & (child // 2 + 80 == parent)
    beyond = jnp.where(right | left, F32(1.0), F32(0.0))
    return dot(sums[0], own) + dot(sums[1], beyond)


def chip_kernel(flags, it, r_in, k_in, pair, strips, o_ref, pool):
    first = flags[0] == 0
    lane = iota((CZ, LANES), 1)
    nears = []
    for n in range(2):
        rd, ru = came(flags, strips, n, 0, NZ)
        done = completed(pair[n, UP:UP + NZ], pair[n, DN:DN + NZ], ru, rd)
        pool[0] = done[2] + roll(done[2], -8, 1)
        pool[1] = done[3] + roll(done[3], -8, 1)
        sums = pool[:, pl.ds(0, CZ, stride=2), :] + pool[:, pl.ds(1, CZ, stride=2), :]
        base = BLOCK * n
        for j in range(CROWS):
            value = pair[n, CZ * j:CZ * (j + 1)] - jnp.where(lane == 63, roll(sums[0], 63 - 16 * j, 1), 0.0)
            value = value + jnp.where(lane == 0, roll(sums[1], -16 * j, 1), 0.0)
            o_ref[base + CZ * j:base + CZ * (j + 1)] = value
        for t in range(2):
            more, less = came(flags, strips, n, 2 * NZ + CZ * t, CZ)
            for q in range(4):
                src = 16 * (4 * t + q)
                more = more + jnp.where(lane == 32 * q, roll(sums[0], 32 * q - src, 1), 0.0)
                less = less - jnp.where(lane == 32 * q + 15, roll(sums[1], 32 * q + 15 - src, 1), 0.0)
            o_ref[base + OWN + CZ * t:base + OWN + CZ * (t + 1)] = more
            o_ref[base + OWN + CZ * (2 + t):base + OWN + CZ * (3 + t)] = less
        k_row, r_row, v_row = (ROWS - 4, ROWS - 3, ROWS - 1) if n else (0, 0, 0)
        ks = [k_in[k_row + t] for t in range(4)]
        rs = [r_in[r_row + t] for t in range(3)]
        nears.append(beside_rows(flags, strips, n, ks, rs, it[v_row], done, n == 1))
    for t in range(10):
        o_ref[2 * BLOCK + NZ * t:2 * BLOCK + NZ * (t + 1)] = jnp.where(first, nears[0][t], nears[1][t])

    def tile(n):
        def get(t):
            if t == 9:
                return outermost(flags, strips, n, n == 0)
            return pair[n, FACING + NZ * t:FACING + NZ * (t + 1)]

        return get

    inner = edge_flux(tile(0), tile(1), pool)
    for n, j in ((0, CROWS - 1), (1, 0)):
        change = inner if n else -inner
        off = 32 * (j % 4)
        side = (lane >= off) & (lane < off + 16)
        changes = (
            (CZ * j, jnp.where(lane < CLANES, change, 0.0)),
            (OWN + CZ * (j // 4), jnp.where(side, roll(change, off - 64, 1), 0.0)),
            (OWN + CZ * (2 + j // 4), jnp.where(side, roll(change, off - 112, 1), 0.0)),
        )
        for at, part in changes:
            at = BLOCK * n + at
            o_ref[at:at + CZ] = o_ref[at:at + CZ] + part


def relay_kernel(flags, out, o_ref, pool):
    first = flags[0] == 0
    low, high = flags[1].astype(F32), flags[2].astype(F32)

    def tile(n, valid):
        return lambda t: out[n, 2 * BLOCK + NZ * t:2 * BLOCK + NZ * (t + 1)] * valid

    outer = edge_flux(tile(0, low), tile(1, high), pool)
    o_ref[0:BLOCK] = jnp.where(first, out[0, BLOCK:2 * BLOCK] * low, out[1, 0:BLOCK] * high)
    o_ref[BLOCK:] = outer


def sweep(lo, hi, mid, shift, sweeps, r_s, s_s, x_s, c_s, width):
    start, pairs = weights(sweeps)
    for n in range(1, sweeps):
        keep, add = pairs[n - 1]
        prev, here = s_s[lo + n - 1], s_s[lo + n]
        for i in range(lo + n, hi - n):
            ahead = s_s[i + 1]
            total = c_s[0, i] * ahead + c_s[1, i] * prev
            total = total + c_s[2, i] * roll(here, -1, 0) + c_s[3, i] * roll(here, 1, 0)
            total = total + c_s[4, i] * roll(here, -1, 1) + c_s[5, i] * roll(here, 1, 1)
            r = r_s[i] - (here - total)
            step = keep * here + add * r
            r_s[i] = r
            s_s[i] = step
            if shift <= i < shift + mid:
                x_s[i - shift] = x_s[i - shift] + (step[:, 0:width] if width else step)
            prev, here = here, ahead


def prepare(rows, mid, shift, sweeps, factor, k_s, r_s, s_s, x_s, c_s, width):
    depth = k_s.shape[1]
    z = iota(k_s.shape[1:], 0)
    start, _ = weights(sweeps)
    below = factor * (k_s[0] + k_s[1])
    for i in range(1, rows - 1):
        k = k_s[i]
        above = factor * (k + k_s[i + 1])
        z_up = factor * (k + jnp.where(z < depth - 1, roll(k, -1, 0), 0.0))
        z_dn = factor * (k + jnp.where(z > 0, roll(k, 1, 0), 0.0))
        y_up = factor * (k + roll(k, -1, 1))
        y_dn = factor * (k + roll(k, 1, 1))
        diagonal = above + below + z_up + z_dn + y_up + y_dn
        inverse = jnp.where(k > 0, 1.0 / jnp.where(k > 0, diagonal, 1.0), 0.0)
        c_s[0, i] = inverse * above
        c_s[1, i] = inverse * below
        c_s[2, i] = jnp.where(z < depth - 1, inverse * z_up, 0.0)
        c_s[3, i] = jnp.where(z > 0, inverse * z_dn, 0.0)
        c_s[4, i] = inverse * y_up
        c_s[5, i] = inverse * y_dn
        r = inverse * r_s[i]
        r_s[i] = r
        s_s[i] = r * start
        if shift <= i < shift + mid:
            x_s[i - shift] = (r[:, 0:width] if width else r) * start
        below = above


def coarse_part(flags, chip, out, near, x_s, k_s, r_s, s_s, c_s):
    first = flags[0] == 0
    low, high = flags[3].astype(F32), flags[4].astype(F32)
    own = near[flags[0], BLOCK:]
    other = near[1 - flags[0], BLOCK:]
    f_low = jnp.where(first, own, other)
    f_high = jnp.where(first, other, own)
    lane = iota((CZ, LANES), 1)

    def packed(at):
        up = slice(BLOCK + at.start, BLOCK + at.stop)
        return (
            jnp.where(first, out[0, at] * low, near[0, at]),
            jnp.where(first, out[0, up] * low, chip[at]),
            jnp.where(first, chip[at], chip[up]),
            jnp.where(first, chip[up], out[1, at] * high),
            jnp.where(first, near[1, at], out[1, up] * high),
        )

    sides = [packed(slice(OWN + CZ * t, OWN + CZ * (t + 1))) for t in range(4)]
    for j in range(CROWS):
        off = 32 * (j % 4)
        rows = packed(slice(CZ * j, CZ * (j + 1)))
        for b in range(5):
            more, less = sides[j // 4][b], sides[2 + j // 4][b]
            for n, dest in enumerate((r_s, k_s)):
                value = jnp.where(lane < CLANES, roll(rows[b], -CLANES * n, 1), 0.0)
                value = jnp.where((lane >= 64) & (lane < 80), roll(more, 64 - off - 16 * n, 1), value)
                dest[CROWS * b + j] = jnp.where(lane >= 112, roll(less, 112 - off - 16 * n, 1), value)
    low_at, high_at = jnp.where(first, 16, 8), jnp.where(first, 32, 24)
    r_s[low_at - 1] = r_s[low_at - 1] - f_low
    r_s[low_at] = r_s[low_at] + f_low
    r_s[high_at - 1] = r_s[high_at - 1] - f_high
    r_s[high_at] = r_s[high_at] + f_high
    zero = jnp.zeros((CZ, LANES), F32)
    s_s[0] = zero
    s_s[CEXT - 1] = zero
    prepare(CEXT, CROWS, COARSE_SWEEPS, COARSE_SWEEPS, 2.0, k_s, r_s, s_s, x_s, c_s, 0)
    sweep(1, CEXT - 1, CROWS, COARSE_SWEEPS, COARSE_SWEEPS, r_s, s_s, x_s, c_s, 0)


def fine_part(flags, it, r_in, k_in, pair, strips, out, x_s, k_s, r_s, s_s, c_s):
    first = flags[0] == 0
    low, high = flags[1].astype(F32), flags[2].astype(F32)
    lane = iota((NZ, LANES), 1)
    facing = []
    for n in range(2):
        rd, ru = came(flags, strips, n, 0, NZ)
        done = completed(pair[n, UP:UP + NZ], pair[n, DN:DN + NZ], ru, rd)
        rows = [pair[n, FACING + NZ * t:FACING + NZ * (t + 1)] for t in range(8)]
        facing.append(beside_rows(flags, strips, n, rows[0:4], rows[4:7], rows[7], done, n == 0))
    mine = flags[0]
    rd, ru = (jnp.where(first, a, b) for a, b in zip(came(flags, strips, 0, 0, NZ), came(flags, strips, 1, 0, NZ)))
    dn, up, right, left = completed(pair[mine, UP:UP + NZ], pair[mine, DN:DN + NZ], ru, rd)

    def beside(rights, lefts, count):
        return jnp.where(lane < count, rights, jnp.where(lane >= LANES - count, lefts, 0.0))

    def join(a, b):
        return jnp.concatenate([a, b], axis=1)

    for i in range(ROWS):
        off = 8 * i
        e = HALO + i
        k_s[e, :, 0:LANES] = k_in[i]
        k_s[e, :, LANES:] = beside(roll(dn, -off, 1), roll(up, 120 - off, 1), 4)
        r = r_in[i] - jnp.where(lane == 127, roll(right, 127 - off, 1), 0.0)
        r_s[e, :, 0:LANES] = r + jnp.where(lane == 0, roll(left, -off, 1), 0.0)
        r_s[e, :, LANES:] = beside(roll(dn, -off - 4, 1), roll(up, 124 - off, 1), 3)
    edges = [jnp.where(first, a, b) for a, b in zip(came(flags, strips, 0, NZ, NZ), came(flags, strips, 1, NZ, NZ))]
    for side in range(2):
        def tile(t, side=side):
            at = slice(2 * BLOCK + NZ * t, 2 * BLOCK + NZ * (t + 1))
            if side == 0:
                return jnp.where(first, out[0, at], facing[0][t]) * low
            return jnp.where(first, facing[1][t], out[1, at]) * high

        base = 0 if side == 0 else HALO + ROWS
        halo, face = tile(8), tile(9)
        for q in range(4):
            k_s[base + q, :, 0:LANES] = tile(q)
            k_s[base + q, :, LANES:] = beside(roll(halo, -8 * q, 1), roll(halo, 88 - 8 * q, 1), 4)
        for t in range(3):
            q = t + 1 - side
            r_s[base + q, :, 0:LANES] = tile(4 + t)
            r_s[base + q, :, LANES:] = beside(roll(halo, -8 * q - 4, 1), roll(halo, 92 - 8 * q, 1), 3)
        v_out = join(tile(7), beside(roll(face, -32, 1), face, 4))
        if side == 0:
            v_in = join(it[0], beside(roll(edges[0], -32, 1), roll(edges[1], 64, 1), 4))
            through = flux(k_s[HALO - 1], k_s[HALO], v_out, v_in)
            r_s[HALO - 1] = r_s[HALO - 1] - through
            r_s[HALO] = r_s[HALO] + through
        else:
            v_in = join(it[ROWS - 1], beside(roll(edges[0], -96, 1), edges[1], 4))
            through = flux(k_s[HALO + ROWS - 1], k_s[HALO + ROWS], v_in, v_out)
            r_s[HALO + ROWS - 1] = r_s[HALO + ROWS - 1] - through
            r_s[HALO + ROWS] = r_s[HALO + ROWS] + through
    zero = jnp.zeros((NZ, 2 * LANES), F32)
    s_s[0] = zero
    s_s[EXT - 1] = zero
    prepare(EXT, ROWS, HALO, SWEEPS, 0.5, k_s, r_s, s_s, x_s, c_s, LANES)
    sweep(1, EXT - 1, ROWS, HALO, SWEEPS, r_s, s_s, x_s, c_s, LANES)


def coarse_kernel(flags, chip, out, near, x_ref, p_ref, k_s, r_s, s_s, c_s):
    coarse_part(flags, chip, out, near, x_ref, k_s, r_s, s_s, c_s)
    lane = iota((CZ, LANES), 1)
    for a in range(4):
        p_ref[pl.ds(a, CZ, stride=4), :] = jnp.where(lane < CLANES, x_ref[a], roll(x_ref[a + 4], CLANES, 1))


def fine_kernel(
    flags, it, r_in, k_in, pair, strips, out, x_c, o_ref, x_f, k_f, r_f, s_f, c_f, wide_s
):
    fine_part(flags, it, r_in, k_in, pair, strips, out, x_f, k_f, r_f, s_f, c_f)
    child, parent = iota((LANES, LANES), 1) // 2, iota((LANES, LANES), 0)
    spread = jnp.where(child == parent, F32(1.0), F32(0.0))
    wide = dot(x_c[...].reshape(CROWS * CZ, LANES), spread).reshape(CROWS, CZ, LANES)
    wide_s[:, pl.ds(0, CZ, stride=2), :] = wide
    wide_s[:, pl.ds(1, CZ, stride=2), :] = wide
    for i in range(ROWS):
        o_ref[i] = it[i] + x_f[i] + wide_s[i // 2]


def planes_kernel(sources, planes, p_ref, o_ref):
    half = sources // 2
    lane = iota((half, LANES), 1)
    for q in range(planes):
        for a in range(4):
            even = p_ref[pl.ds(4 * q + a, half, stride=8 * planes), :]
            odd = p_ref[pl.ds(4 * (planes + q) + a, half, stride=8 * planes), :]
            to = (a * planes + q) * half
            o_ref[to:to + half] = jnp.where(lane < CLANES, even, roll(odd, CLANES, 1))
            to = ((a + 4) * planes + q) * half
            o_ref[to:to + half] = jnp.where(lane < CLANES, roll(even, CLANES, 1), odd)


def place():
    gx, gy = lax.axis_index("gx"), lax.axis_index("gy")
    n_gx, n_gy = lax.axis_size("gx"), lax.axis_size("gy")
    marks = [gx % 2, gx > 0, gx < n_gx - 1, gx > 1, gx < n_gx - 2, gy % 2, gy > 0, gy < n_gy - 1]
    return [m.astype(jnp.int32) for m in marks]


def call(kernel, outs, scratch, placed=False, operands=(), flops=1000000, copies=False):
    vmem = pl.BlockSpec(memory_space=pltpu.VMEM)
    specs = [pl.BlockSpec(memory_space=pltpu.HBM) if copies else vmem] * len(operands)
    size = sum(4 * x.size for x in operands) + sum(4 * o.size for o in outs)
    multiple = len(outs) > 1
    held = [pltpu.VMEM(s, F32) for s in scratch]
    if copies:
        held += [pltpu.VMEM(x.shape, x.dtype) for x in operands]
        held.append(pltpu.SemaphoreType.DMA((len(operands), PARTS)))

    def body(*refs):
        if placed:
            kernel(place(), *refs)
        else:
            kernel(*refs)

    return pl.pallas_call(
        body,
        out_shape=outs if multiple else outs[0],
        in_specs=specs,
        out_specs=[vmem] * len(outs) if multiple else vmem,
        scratch_shapes=held,
        compiler_params=pltpu.CompilerParams(vmem_limit_bytes=(54500 if copies else 40960) * 1024),
        cost_estimate=pl.CostEstimate(flops=flops, bytes_accessed=size, transcendentals=0),
    )(*operands)


def shape(*dims):
    return jax.ShapeDtypeStruct(dims, F32)


def on_device(iterate, source, labels):
    n_gx, n_gy = lax.axis_size("gx"), lax.axis_size("gy")
    gx = lax.axis_index("gx")
    gy = lax.axis_index("gy")
    chips = [[i, i + 1] for i in range(0, n_gx, 2)]
    between = [[i, (i + 1) % n_gx] for i in range(1, n_gx, 2)]
    along = [
        [i * n_gy + j, i * n_gy + (j + 1) % n_gy] for i in range(n_gx) for j in range(i % 2, n_gy, 2)
    ]
    own = shape(ROWS, NZ, LANES)
    resid, cond, shared = call(
        residual_kernel,
        [own, own, shape(SHARED, LANES)],
        [(2, CROWS, NZ, LANES)],
        True,
        (iterate, source, labels),
        copies=True,
    )
    pair = lax.all_gather(shared, "gx", axis_index_groups=chips)
    lower = (gx + gy) % 2 == 0
    strips = jnp.where(lower, pair[:, UP:DN], pair[:, DN:FACING]).reshape(2 * STRIP, LANES)
    strips = lax.all_gather(strips, ("gx", "gy"), axis_index_groups=along)
    strips = lax.all_gather(jnp.where(lower, strips[1], strips[0]), "gx", axis_index_groups=chips)
    chip = call(
        chip_kernel,
        [shape(2 * BLOCK + NEAR, LANES)],
        [(2, NZ, LANES)],
        True,
        (iterate, resid, cond, pair, strips),
    )
    beyond = lax.all_gather(chip, "gx", axis_index_groups=between)
    relay = call(relay_kernel, [shape(BLOCK + CZ, LANES)], [(2, NZ, LANES)], True, (beyond,))
    relay = lax.all_gather(relay, "gx", axis_index_groups=chips)
    rows, wide = (CEXT, CZ, LANES), (EXT, NZ, 2 * LANES)
    coarse_out, planes = call(
        coarse_kernel,
        [shape(CROWS, CZ, LANES), shape(4 * CZ, LANES)],
        [rows, rows, rows, (6, *rows)],
        True,
        (chip, beyond, relay),
    )
    per = CZ // n_gy
    planes = lax.all_to_all(planes.reshape(n_gy, 4 * per, LANES), "gy", split_axis=0, concat_axis=0, tiled=True)
    corrected = call(
        fine_kernel,
        [own],
        [(ROWS, NZ, LANES), wide, wide, wide, (6, *wide), (CROWS, NZ, LANES)],
        True,
        (iterate, resid, cond, pair, strips, beyond, coarse_out),
        flops=20000000,
    )
    owned = call(
        functools.partial(planes_kernel, n_gy, per),
        [shape(4 * CZ, LANES)],
        [],
        False,
        (planes.reshape(4 * CZ, LANES),),
    ).reshape(CROWS, per, CLANES * n_gy)
    return corrected, owned


def solution(mesh):
    spec = P("gx", None, "gy")
    return jax.shard_map(
        on_device, mesh=mesh, in_specs=(spec, spec, spec), out_specs=(spec, P("gx", "gy", None)), check_vma=False
    )
```

```python
import functools

import jax
import jax.numpy as jnp
from jax import lax
from jax.experimental import pallas as pl
from jax.experimental.pallas import tpu as pltpu
from jax.sharding import PartitionSpec as P

SWEEPS = 4
COARSE_SWEEPS = 16
TABLE = (0.5, 1.0, 2.5, 6.0)
LOWER = 0.25
UPPER = 2.0
F32 = jnp.float32

ROWS, NZ, LANES = 16, 32, 128
CROWS, CZ, CLANES = 8, 16, 64
HALO = SWEEPS
EXT = ROWS + 2 * HALO
CEXT = CROWS + 2 * COARSE_SWEEPS
OWN = CROWS * CZ
BLOCK = OWN + 4 * CZ
NEAR = 10 * NZ
STRIP = 3 * NZ
UP, DN, FACING = OWN, OWN + STRIP, OWN + 2 * STRIP
SHARED = FACING + 8 * NZ
PARTS = 4


def weights(sweeps):
    centre = (UPPER + LOWER) / 2.0
    radius = (UPPER - LOWER) / 2.0
    sigma = centre / radius
    rho = 1.0 / sigma
    pairs = []
    for _ in range(1, sweeps):
        rho_new = 1.0 / (2.0 * sigma - rho)
        pairs.append((rho_new * rho, 2.0 * rho_new / radius))
        rho = rho_new
    return 1.0 / centre, pairs


def conduct(labels):
    total = jnp.zeros(labels.shape, F32)
    for label_id, value in enumerate(TABLE):
        total = jnp.where(labels == label_id, F32(value), total)
    return total


def roll(x, shift, axis):
    size = x.shape[axis]
    shift = shift % size
    return x if shift == 0 else pltpu.roll(x, shift, axis)


def iota(shape, axis):
    return lax.broadcasted_iota(jnp.int32, shape, axis)


def flux(k_a, k_b, v_a, v_b):
    return 0.5 * (k_a + k_b) * (v_a - v_b)


def dot(a, b):
    return jnp.dot(a, b, precision=lax.Precision.HIGHEST, preferred_element_type=F32)


def residual_rows(k_ref, it, src, arrive=None):
    z, lane = iota((NZ, LANES), 0), iota((NZ, LANES), 1)
    before = zero = jnp.zeros((NZ, LANES), F32)
    for i in range(ROWS):
        if arrive:
            arrive(i + 1)
        k, v = k_ref[i], it[i]
        after = flux(k, k_ref[i + 1], v, it[i + 1]) if i < ROWS - 1 else zero
        fy = jnp.where(lane < LANES - 1, flux(k, roll(k, -1, 1), v, roll(v, -1, 1)), 0.0)
        k_z = jnp.where(z < NZ - 1, roll(k, -1, 0), 0.0)
        v_z = jnp.where(z < NZ - 1, roll(v, -1, 0), 0.0)
        fz = flux(k, k_z, v, v_z)
        fz_in = jnp.where(z > 0, roll(fz, 1, 0), -0.5 * k * v)
        yield i, k, v, src[i] - after + before - fy + roll(fy, 1, 1) - fz + fz_in
        before = after


def residual_kernel(flags, it_in, src_in, lab_in, out_ref, n_ref, pool, k_ref, a_ref, it, src, lab, sems, done_sems):
    copies = []
    for part in range(PARTS):
        rows = pl.ds(part * ROWS // PARTS, ROWS // PARTS)
        copies.append(
            [
                pltpu.make_async_copy(a.at[rows], b.at[rows], sems.at[n, part])
                for n, (a, b) in enumerate(((lab_in, lab), (it_in, it), (src_in, src)))
            ]
        )
        for copy in copies[-1]:
            copy.start()

    def arrive(row):
        part, within = divmod(row, ROWS // PARTS)
        if within or part == PARTS:
            return
        for copy in copies[part]:
            copy.wait()
        for i in range(row, row + ROWS // PARTS):
            k_ref[i] = conduct(lab[i])

    arrive(0)
    lane = iota((NZ, LANES), 1)
    zero = jnp.zeros((NZ, LANES), F32)
    up = dn = zero
    low, high = {}, {}
    for i, k, v, r in residual_rows(k_ref, it, src, arrive):
        if i < 3:
            low[i] = r
        if i >= ROWS - 3:
            high[i - ROWS + 3] = r
        j = i // 2
        if i % 2 == 0:
            r_even, k_even = r, k
        else:
            pool[0, j] = r_even + r
            pool[1, j] = k_even + k
        off = 8 * i
        here = (lane >= off) & (lane < off + 8)
        top = jnp.where(lane >= 124, k, jnp.where(lane >= 121, roll(r, -4, 1), roll(v, -7, 1)))
        bottom = jnp.where(lane < 4, k, jnp.where(lane < 7, roll(r, 4, 1), roll(v, 7, 1)))
        up = jnp.where(here, roll(top, off - 120, 1), up)
        dn = jnp.where(here, roll(bottom, off, 1), dn)
    a_ref[UP:UP + NZ] = up
    a_ref[DN:DN + NZ] = dn
    up = dn = zero
    for g, edge in enumerate((k_ref[0], it[0], k_ref[ROWS - 1], it[ROWS - 1])):
        here = (lane >= 32 * g) & (lane < 32 * g + 32)
        up = jnp.where(here, roll(edge, 32 * g - 96, 1), up)
        dn = jnp.where(here, roll(edge, 32 * g, 1), dn)
    a_ref[UP + NZ:UP + 2 * NZ] = up
    a_ref[DN + NZ:DN + 2 * NZ] = dn
    first = flags[0] == 0
    lows = [k_ref[t] for t in range(4)] + [low[t] for t in range(3)] + [it[0]]
    highs = [k_ref[ROWS - 4 + t] for t in range(4)] + [high[t] for t in range(3)] + [it[ROWS - 1]]
    for t in range(8):
        a_ref[FACING + NZ * t:FACING + NZ * (t + 1)] = jnp.where(first, highs[t], lows[t])
        n_ref[NZ * t:NZ * (t + 1)] = jnp.where(first, lows[t], highs[t])
    sent = []

    def send(start, rows):
        at = pl.ds(start, rows)
        sent.append(pltpu.make_async_copy(a_ref.at[at], out_ref.at[at], done_sems.at[len(sent)]))
        sent[-1].start()

    send(FACING, 8 * NZ)
    send(UP, 2 * NZ)
    send(DN, 2 * NZ)
    tops = pool[:, :, pl.ds(0, CZ, stride=2), :] + pool[:, :, pl.ds(1, CZ, stride=2), :]
    child, parent = iota((LANES, LANES), 0) // 2, iota((LANES, LANES), 1)
    to_left = jnp.where(child == parent, F32(1.0), F32(0.0))
    to_right = jnp.where(child == parent - CLANES, F32(0.125), F32(0.0))
    coarse = dot(tops[0].reshape(CROWS * CZ, LANES), to_left) + dot(tops[1].reshape(CROWS * CZ, LANES), to_right)
    a_ref[0:OWN] = coarse
    coarse = coarse.reshape(CROWS, CZ, LANES)
    lane = iota((CZ, LANES), 1)
    for t in range(2):
        up = dn = jnp.zeros((CZ, LANES), F32)
        for j in range(4 * t, 4 * t + 4):
            row = coarse[j]
            off = (j % 4) * 32
            at_r = (lane >= off) & (lane < off + 16)
            at_k = (lane >= off + 16) & (lane < off + 32)
            up = jnp.where(at_r, roll(row, off - 48, 1), jnp.where(at_k, roll(row, off + 16 - 112, 1), up))
            dn = jnp.where(at_r, roll(row, off, 1), jnp.where(at_k, roll(row, off + 16 - 64, 1), dn))
        a_ref[UP + 2 * NZ + CZ * t:UP + 2 * NZ + CZ * (t + 1)] = up
        a_ref[DN + 2 * NZ + CZ * t:DN + 2 * NZ + CZ * (t + 1)] = dn
    send(0, OWN)
    send(UP + 2 * NZ, 2 * CZ)
    send(DN + 2 * NZ, 2 * CZ)
    for copy in sent:
        copy.wait()


def strip_flux(up, dn):
    lane = iota(up.shape, 1)
    face = flux(roll(up, -7, 1), dn, up, roll(dn, -7, 1))
    return jnp.where(lane % 8 == 0, face, 0.0)


def came(flags, strips, n, start, rows):
    at = slice(STRIP * n + start, STRIP * n + start + rows)
    rd = strips[flags[5], at] * flags[7].astype(F32)
    return rd, strips[1 - flags[5], at] * flags[6].astype(F32)


def completed(ou, od, ru, rd):
    right = strip_flux(ou, rd)
    left = strip_flux(ru, od)
    return rd + roll(right, 4, 1), ru - roll(left, 3, 1), right, left


def beside_rows(flags, strips, n, ks, rs, v, done, top):
    lane = iota((NZ, LANES), 1)
    dn, up, right, left = done
    k_row, r_row = (ROWS - 4, ROWS - 3) if top else (0, 0)
    tiles = list(ks)
    for t in range(3):
        i = r_row + t
        r = rs[t] - jnp.where(lane == 127, roll(right, 127 - 8 * i, 1), 0.0)
        tiles.append(r + jnp.where(lane == 0, roll(left, -8 * i, 1), 0.0))
    tiles.append(v)
    tiles.append(jnp.where(lane < 32, roll(dn, -8 * k_row, 1), roll(up, 32 - 8 * k_row, 1)))
    tiles.append(outermost(flags, strips, n, top))
    return tiles


def outermost(flags, strips, n, top):
    lane = iota((NZ, LANES), 1)
    shift = 64 if top else 0
    rd, ru = came(flags, strips, n, NZ, NZ)
    return jnp.where(lane < 64, roll(rd, -shift, 1), roll(ru, 64 - shift, 1))


def edge_flux(a, b, pool):
    pool[0] = flux(a(3), b(0), a(7), b(7))
    u, w = a(9), b(9)
    pool[1] = flux(u, w, roll(u, -32, 1), roll(w, -32, 1))
    sums = pool[:, pl.ds(0, CZ, stride=2), :] + pool[:, pl.ds(1, CZ, stride=2), :]
    child, parent = iota((LANES, LANES), 0), iota((LANES, LANES), 1)
    own = jnp.where(child // 2 == parent, F32(1.0), F32(0.0))
    right = (child < 32) & (child // 2 + 64 == parent)
    left = (child >= 64) & (child < 96) & (child // 2 + 80 == parent)
    beyond = jnp.where(right | left, F32(1.0), F32(0.0))
    return dot(sums[0], own) + dot(sums[1], beyond)


def chip_kernel(flags, near, pair, strips, o_ref, pool):
    first = flags[0] == 0
    lane = iota((CZ, LANES), 1)
    nears = []
    for n in range(2):
        rd, ru = came(flags, strips, n, 0, NZ)
        done = completed(pair[n, UP:UP + NZ], pair[n, DN:DN + NZ], ru, rd)
        pool[0] = done[2] + roll(done[2], -8, 1)
        pool[1] = done[3] + roll(done[3], -8, 1)
        sums = pool[:, pl.ds(0, CZ, stride=2), :] + pool[:, pl.ds(1, CZ, stride=2), :]
        base = BLOCK * n
        for j in range(CROWS):
            value = pair[n, CZ * j:CZ * (j + 1)] - jnp.where(lane == 63, roll(sums[0], 63 - 16 * j, 1), 0.0)
            value = value + jnp.where(lane == 0, roll(sums[1], -16 * j, 1), 0.0)
            o_ref[base + CZ * j:base + CZ * (j + 1)] = value
        for t in range(2):
            more, less = came(flags, strips, n, 2 * NZ + CZ * t, CZ)
            for q in range(4):
                src = 16 * (4 * t + q)
                more = more + jnp.where(lane == 32 * q, roll(sums[0], 32 * q - src, 1), 0.0)
                less = less - jnp.where(lane == 32 * q + 15, roll(sums[1], 32 * q + 15 - src, 1), 0.0)
            o_ref[base + OWN + CZ * t:base + OWN + CZ * (t + 1)] = more
            o_ref[base + OWN + CZ * (2 + t):base + OWN + CZ * (3 + t)] = less
        rows = [near[NZ * t:NZ * (t + 1)] for t in range(8)]
        nears.append(beside_rows(flags, strips, n, rows[0:4], rows[4:7], rows[7], done, n == 1))
    for t in range(10):
        o_ref[2 * BLOCK + NZ * t:2 * BLOCK + NZ * (t + 1)] = jnp.where(first, nears[0][t], nears[1][t])

    def tile(n):
        def get(t):
            if t == 9:
                return outermost(flags, strips, n, n == 0)
            return pair[n, FACING + NZ * t:FACING + NZ * (t + 1)]

        return get

    inner = edge_flux(tile(0), tile(1), pool)
    for n, j in ((0, CROWS - 1), (1, 0)):
        change = inner if n else -inner
        off = 32 * (j % 4)
        side = (lane >= off) & (lane < off + 16)
        changes = (
            (CZ * j, jnp.where(lane < CLANES, change, 0.0)),
            (OWN + CZ * (j // 4), jnp.where(side, roll(change, off - 64, 1), 0.0)),
            (OWN + CZ * (2 + j // 4), jnp.where(side, roll(change, off - 112, 1), 0.0)),
        )
        for at, part in changes:
            at = BLOCK * n + at
            o_ref[at:at + CZ] = o_ref[at:at + CZ] + part


def relay_kernel(flags, out, o_ref, pool):
    first = flags[0] == 0
    low, high = flags[1].astype(F32), flags[2].astype(F32)

    def tile(n, valid):
        return lambda t: out[n, 2 * BLOCK + NZ * t:2 * BLOCK + NZ * (t + 1)] * valid

    outer = edge_flux(tile(0, low), tile(1, high), pool)
    o_ref[0:BLOCK] = jnp.where(first, out[0, BLOCK:2 * BLOCK] * low, out[1, 0:BLOCK] * high)
    o_ref[BLOCK:] = outer


def sweep(lo, hi, mid, shift, sweeps, r_s, s_s, x_s, c_s, width):
    start, pairs = weights(sweeps)
    for n in range(1, sweeps):
        keep, add = pairs[n - 1]
        prev, here = s_s[lo + n - 1], s_s[lo + n]
        for i in range(lo + n, hi - n):
            ahead = s_s[i + 1]
            total = c_s[0, i] * ahead + c_s[1, i] * prev
            total = total + c_s[2, i] * roll(here, -1, 0) + c_s[3, i] * roll(here, 1, 0)
            total = total + c_s[4, i] * roll(here, -1, 1) + c_s[5, i] * roll(here, 1, 1)
            r = r_s[i] - (here - total)
            step = keep * here + add * r
            r_s[i] = r
            s_s[i] = step
            if shift <= i < shift + mid:
                x_s[i - shift] = x_s[i - shift] + (step[:, 0:width] if width else step)
            prev, here = here, ahead


def prepare(rows, mid, shift, sweeps, factor, k_s, r_s, s_s, x_s, c_s, width):
    depth = k_s.shape[1]
    z = iota(k_s.shape[1:], 0)
    start, _ = weights(sweeps)
    below = factor * (k_s[0] + k_s[1])
    for i in range(1, rows - 1):
        k = k_s[i]
        above = factor * (k + k_s[i + 1])
        z_up = factor * (k + jnp.where(z < depth - 1, roll(k, -1, 0), 0.0))
        z_dn = factor * (k + jnp.where(z > 0, roll(k, 1, 0), 0.0))
        y_up = factor * (k + roll(k, -1, 1))
        y_dn = factor * (k + roll(k, 1, 1))
        diagonal = above + below + z_up + z_dn + y_up + y_dn
        inverse = jnp.where(k > 0, 1.0 / jnp.where(k > 0, diagonal, 1.0), 0.0)
        c_s[0, i] = inverse * above
        c_s[1, i] = inverse * below
        c_s[2, i] = jnp.where(z < depth - 1, inverse * z_up, 0.0)
        c_s[3, i] = jnp.where(z > 0, inverse * z_dn, 0.0)
        c_s[4, i] = inverse * y_up
        c_s[5, i] = inverse * y_dn
        r = inverse * r_s[i]
        r_s[i] = r
        s_s[i] = r * start
        if shift <= i < shift + mid:
            x_s[i - shift] = (r[:, 0:width] if width else r) * start
        below = above


def coarse_part(flags, chip, out, near, x_s, k_s, r_s, s_s, c_s):
    first = flags[0] == 0
    low, high = flags[3].astype(F32), flags[4].astype(F32)
    own = near[flags[0], BLOCK:]
    other = near[1 - flags[0], BLOCK:]
    f_low = jnp.where(first, own, other)
    f_high = jnp.where(first, other, own)
    lane = iota((CZ, LANES), 1)

    def packed(at):
        up = slice(BLOCK + at.start, BLOCK + at.stop)
        return (
            jnp.where(first, out[0, at] * low, near[0, at]),
            jnp.where(first, out[0, up] * low, chip[at]),
            jnp.where(first, chip[at], chip[up]),
            jnp.where(first, chip[up], out[1, at] * high),
            jnp.where(first, near[1, at], out[1, up] * high),
        )

    sides = [packed(slice(OWN + CZ * t, OWN + CZ * (t + 1))) for t in range(4)]
    for j in range(CROWS):
        off = 32 * (j % 4)
        rows = packed(slice(CZ * j, CZ * (j + 1)))
        for b in range(5):
            more, less = sides[j // 4][b], sides[2 + j // 4][b]
            for n, dest in enumerate((r_s, k_s)):
                value = jnp.where(lane < CLANES, roll(rows[b], -CLANES * n, 1), 0.0)
                value = jnp.where((lane >= 64) & (lane < 80), roll(more, 64 - off - 16 * n, 1), value)
                dest[CROWS * b + j] = jnp.where(lane >= 112, roll(less, 112 - off - 16 * n, 1), value)
    low_at, high_at = jnp.where(first, 16, 8), jnp.where(first, 32, 24)
    r_s[low_at - 1] = r_s[low_at - 1] - f_low
    r_s[low_at] = r_s[low_at] + f_low
    r_s[high_at - 1] = r_s[high_at - 1] - f_high
    r_s[high_at] = r_s[high_at] + f_high
    zero = jnp.zeros((CZ, LANES), F32)
    s_s[0] = zero
    s_s[CEXT - 1] = zero
    prepare(CEXT, CROWS, COARSE_SWEEPS, COARSE_SWEEPS, 2.0, k_s, r_s, s_s, x_s, c_s, 0)
    sweep(1, CEXT - 1, CROWS, COARSE_SWEEPS, COARSE_SWEEPS, r_s, s_s, x_s, c_s, 0)


def fine_part(flags, it, src, lab, pair, strips, out, k_in, r_in, x_s, k_s, r_s, s_s, c_s):
    first = flags[0] == 0
    low, high = flags[1].astype(F32), flags[2].astype(F32)
    lane = iota((NZ, LANES), 1)
    for i in range(ROWS):
        k_in[i] = conduct(lab[i])
    for i, _, _, r in residual_rows(k_in, it, src):
        r_in[i] = r
    facing = []
    for n in range(2):
        rd, ru = came(flags, strips, n, 0, NZ)
        done = completed(pair[n, UP:UP + NZ], pair[n, DN:DN + NZ], ru, rd)
        rows = [pair[n, FACING + NZ * t:FACING + NZ * (t + 1)] for t in range(8)]
        facing.append(beside_rows(flags, strips, n, rows[0:4], rows[4:7], rows[7], done, n == 0))
    mine = flags[0]
    rd, ru = (jnp.where(first, a, b) for a, b in zip(came(flags, strips, 0, 0, NZ), came(flags, strips, 1, 0, NZ)))
    dn, up, right, left = completed(pair[mine, UP:UP + NZ], pair[mine, DN:DN + NZ], ru, rd)

    def beside(rights, lefts, count):
        return jnp.where(lane < count, rights, jnp.where(lane >= LANES - count, lefts, 0.0))

    def join(a, b):
        return jnp.concatenate([a, b], axis=1)

    for i in range(ROWS):
        off = 8 * i
        e = HALO + i
        k_s[e, :, 0:LANES] = k_in[i]
        k_s[e, :, LANES:] = beside(roll(dn, -off, 1), roll(up, 120 - off, 1), 4)
        r = r_in[i] - jnp.where(lane == 127, roll(right, 127 - off, 1), 0.0)
        r_s[e, :, 0:LANES] = r + jnp.where(lane == 0, roll(left, -off, 1), 0.0)
        r_s[e, :, LANES:] = beside(roll(dn, -off - 4, 1), roll(up, 124 - off, 1), 3)
    edges = [jnp.where(first, a, b) for a, b in zip(came(flags, strips, 0, NZ, NZ), came(flags, strips, 1, NZ, NZ))]
    for side in range(2):
        def tile(t, side=side):
            at = slice(2 * BLOCK + NZ * t, 2 * BLOCK + NZ * (t + 1))
            if side == 0:
                return jnp.where(first, out[0, at], facing[0][t]) * low
            return jnp.where(first, facing[1][t], out[1, at]) * high

        base = 0 if side == 0 else HALO + ROWS
        halo, face = tile(8), tile(9)
        for q in range(4):
            k_s[base + q, :, 0:LANES] = tile(q)
            k_s[base + q, :, LANES:] = beside(roll(halo, -8 * q, 1), roll(halo, 88 - 8 * q, 1), 4)
        for t in range(3):
            q = t + 1 - side
            r_s[base + q, :, 0:LANES] = tile(4 + t)
            r_s[base + q, :, LANES:] = beside(roll(halo, -8 * q - 4, 1), roll(halo, 92 - 8 * q, 1), 3)
        v_out = join(tile(7), beside(roll(face, -32, 1), face, 4))
        if side == 0:
            v_in = join(it[0], beside(roll(edges[0], -32, 1), roll(edges[1], 64, 1), 4))
            through = flux(k_s[HALO - 1], k_s[HALO], v_out, v_in)
            r_s[HALO - 1] = r_s[HALO - 1] - through
            r_s[HALO] = r_s[HALO] + through
        else:
            v_in = join(it[ROWS - 1], beside(roll(edges[0], -96, 1), edges[1], 4))
            through = flux(k_s[HALO + ROWS - 1], k_s[HALO + ROWS], v_in, v_out)
            r_s[HALO + ROWS - 1] = r_s[HALO + ROWS - 1] - through
            r_s[HALO + ROWS] = r_s[HALO + ROWS] + through
    zero = jnp.zeros((NZ, 2 * LANES), F32)
    s_s[0] = zero
    s_s[EXT - 1] = zero
    prepare(EXT, ROWS, HALO, SWEEPS, 0.5, k_s, r_s, s_s, x_s, c_s, LANES)
    sweep(1, EXT - 1, ROWS, HALO, SWEEPS, r_s, s_s, x_s, c_s, LANES)


def coarse_kernel(flags, chip, out, near, x_ref, p_ref, k_s, r_s, s_s, c_s):
    coarse_part(flags, chip, out, near, x_ref, k_s, r_s, s_s, c_s)
    lane = iota((CZ, LANES), 1)
    for a in range(4):
        p_ref[pl.ds(a, CZ, stride=4), :] = jnp.where(lane < CLANES, x_ref[a], roll(x_ref[a + 4], CLANES, 1))


def fine_kernel(
    flags, it, src, lab, pair, strips, out, x_c, o_ref, k_in, r_in, x_f, k_f, r_f, s_f, c_f, wide_s
):
    fine_part(flags, it, src, lab, pair, strips, out, k_in, r_in, x_f, k_f, r_f, s_f, c_f)
    child, parent = iota((LANES, LANES), 1) // 2, iota((LANES, LANES), 0)
    spread = jnp.where(child == parent, F32(1.0), F32(0.0))
    wide = dot(x_c[...].reshape(CROWS * CZ, LANES), spread).reshape(CROWS, CZ, LANES)
    wide_s[:, pl.ds(0, CZ, stride=2), :] = wide
    wide_s[:, pl.ds(1, CZ, stride=2), :] = wide
    for i in range(ROWS):
        o_ref[i] = it[i] + x_f[i] + wide_s[i // 2]


def planes_kernel(sources, planes, p_ref, o_ref):
    half = sources // 2
    lane = iota((half, LANES), 1)
    for q in range(planes):
        for a in range(4):
            even = p_ref[pl.ds(4 * q + a, half, stride=8 * planes), :]
            odd = p_ref[pl.ds(4 * (planes + q) + a, half, stride=8 * planes), :]
            to = (a * planes + q) * half
            o_ref[to:to + half] = jnp.where(lane < CLANES, even, roll(odd, CLANES, 1))
            to = ((a + 4) * planes + q) * half
            o_ref[to:to + half] = jnp.where(lane < CLANES, roll(even, CLANES, 1), odd)


def place():
    gx, gy = lax.axis_index("gx"), lax.axis_index("gy")
    n_gx, n_gy = lax.axis_size("gx"), lax.axis_size("gy")
    marks = [gx % 2, gx > 0, gx < n_gx - 1, gx > 1, gx < n_gx - 2, gy % 2, gy > 0, gy < n_gy - 1]
    return [m.astype(jnp.int32) for m in marks]


def call(kernel, outs, scratch, placed=False, operands=(), flops=1000000, copies=False):
    vmem = pl.BlockSpec(memory_space=pltpu.VMEM)
    specs = [pl.BlockSpec(memory_space=pltpu.HBM) if copies else vmem] * len(operands)
    size = sum(4 * x.size for x in operands) + sum(4 * o.size for o in outs)
    multiple = len(outs) > 1
    held = [pltpu.VMEM(s, F32) for s in scratch]
    out_specs = [vmem] * len(outs)
    if copies:
        out_specs[0] = pl.BlockSpec(memory_space=pltpu.HBM)
        held += [pltpu.VMEM(x.shape, x.dtype) for x in operands]
        held.append(pltpu.SemaphoreType.DMA((len(operands), PARTS)))
        held.append(pltpu.SemaphoreType.DMA((6,)))

    def body(*refs):
        if placed:
            kernel(place(), *refs)
        else:
            kernel(*refs)

    return pl.pallas_call(
        body,
        out_shape=outs if multiple else outs[0],
        in_specs=specs,
        out_specs=out_specs if multiple else out_specs[0],
        scratch_shapes=held,
        compiler_params=pltpu.CompilerParams(vmem_limit_bytes=(54900 if copies else 40960) * 1024),
        cost_estimate=pl.CostEstimate(flops=flops, bytes_accessed=size, transcendentals=0),
    )(*operands)


def shape(*dims):
    return jax.ShapeDtypeStruct(dims, F32)


def on_device(iterate, source, labels):
    n_gx, n_gy = lax.axis_size("gx"), lax.axis_size("gy")
    gx = lax.axis_index("gx")
    gy = lax.axis_index("gy")
    chips = [[i, i + 1] for i in range(0, n_gx, 2)]
    between = [[i, (i + 1) % n_gx] for i in range(1, n_gx, 2)]
    along = [
        [i * n_gy + j, i * n_gy + (j + 1) % n_gy] for i in range(n_gx) for j in range(i % 2, n_gy, 2)
    ]
    own = shape(ROWS, NZ, LANES)
    shared, near = call(
        residual_kernel,
        [shape(SHARED, LANES), shape(8 * NZ, LANES)],
        [(2, CROWS, NZ, LANES), own.shape, (SHARED, LANES)],
        True,
        (iterate, source, labels),
        copies=True,
    )
    pair = lax.all_gather(shared, "gx", axis_index_groups=chips)
    lower = (gx + gy) % 2 == 0
    strips = jnp.where(lower, pair[:, UP:DN], pair[:, DN:FACING]).reshape(2 * STRIP, LANES)
    strips = lax.all_gather(strips, ("gx", "gy"), axis_index_groups=along)
    strips = lax.all_gather(jnp.where(lower, strips[1], strips[0]), "gx", axis_index_groups=chips)
    chip = call(
        chip_kernel,
        [shape(2 * BLOCK + NEAR, LANES)],
        [(2, NZ, LANES)],
        True,
        (near, pair, strips),
    )
    beyond = lax.all_gather(chip, "gx", axis_index_groups=between)
    relay = call(relay_kernel, [shape(BLOCK + CZ, LANES)], [(2, NZ, LANES)], True, (beyond,))
    relay = lax.all_gather(relay, "gx", axis_index_groups=chips)
    rows, wide = (CEXT, CZ, LANES), (EXT, NZ, 2 * LANES)
    coarse_out, planes = call(
        coarse_kernel,
        [shape(CROWS, CZ, LANES), shape(4 * CZ, LANES)],
        [rows, rows, rows, (6, *rows)],
        True,
        (chip, beyond, relay),
    )
    per = CZ // n_gy
    planes = lax.all_to_all(planes.reshape(n_gy, 4 * per, LANES), "gy", split_axis=0, concat_axis=0, tiled=True)
    corrected = call(
        fine_kernel,
        [own],
        [own.shape, own.shape, own.shape, wide, wide, wide, (6, *wide), (CROWS, NZ, LANES)],
        True,
        (iterate, source, labels, pair, strips, beyond, coarse_out),
        flops=20000000,
    )
    owned = call(
        functools.partial(planes_kernel, n_gy, per),
        [shape(4 * CZ, LANES)],
        [],
        False,
        (planes.reshape(4 * CZ, LANES),),
    ).reshape(CROWS, per, CLANES * n_gy)
    return corrected, owned


def solution(mesh):
    spec = P("gx", None, "gy")
    return jax.shard_map(
        on_device, mesh=mesh, in_specs=(spec, spec, spec), out_specs=(spec, P("gx", "gy", None)), check_vma=False
    )
```

```python
import functools

import jax
import jax.numpy as jnp
from jax import lax
from jax.experimental import pallas as pl
from jax.experimental.pallas import tpu as pltpu
from jax.sharding import PartitionSpec as P

SWEEPS = 4
COARSE_SWEEPS = 16
TABLE = (0.5, 1.0, 2.5, 6.0)
LOWER = 0.25
UPPER = 2.0
F32 = jnp.float32

ROWS, NZ, LANES = 16, 32, 128
CROWS, CZ, CLANES = 8, 16, 64
HALO = SWEEPS
EXT = ROWS + 2 * HALO
CEXT = CROWS + 2 * COARSE_SWEEPS
OWN = CROWS * CZ
BLOCK = OWN + 4 * CZ
NEAR = 10 * NZ
STRIP = 3 * NZ
UP, DN, FACING = OWN, OWN + STRIP, OWN + 2 * STRIP
SHARED = FACING + 8 * NZ
PARTS = 4


def weights(sweeps):
    centre = (UPPER + LOWER) / 2.0
    radius = (UPPER - LOWER) / 2.0
    sigma = centre / radius
    rho = 1.0 / sigma
    pairs = []
    for _ in range(1, sweeps):
        rho_new = 1.0 / (2.0 * sigma - rho)
        pairs.append((rho_new * rho, 2.0 * rho_new / radius))
        rho = rho_new
    return 1.0 / centre, pairs


def conduct(labels):
    total = jnp.zeros(labels.shape, F32)
    for label_id, value in enumerate(TABLE):
        total = jnp.where(labels == label_id, F32(value), total)
    return total


def roll(x, shift, axis):
    size = x.shape[axis]
    shift = shift % size
    return x if shift == 0 else pltpu.roll(x, shift, axis)


def iota(shape, axis):
    return lax.broadcasted_iota(jnp.int32, shape, axis)


def flux(k_a, k_b, v_a, v_b):
    return 0.5 * (k_a + k_b) * (v_a - v_b)


def dot(a, b):
    return jnp.dot(a, b, precision=lax.Precision.HIGHEST, preferred_element_type=F32)


def residual_rows(k_ref, it, src, arrive=None):
    z, lane = iota((NZ, LANES), 0), iota((NZ, LANES), 1)
    before = zero = jnp.zeros((NZ, LANES), F32)
    for i in range(ROWS):
        if arrive:
            arrive(i + 1)
        k, v = k_ref[i], it[i]
        after = flux(k, k_ref[i + 1], v, it[i + 1]) if i < ROWS - 1 else zero
        fy = jnp.where(lane < LANES - 1, flux(k, roll(k, -1, 1), v, roll(v, -1, 1)), 0.0)
        k_z = jnp.where(z < NZ - 1, roll(k, -1, 0), 0.0)
        v_z = jnp.where(z < NZ - 1, roll(v, -1, 0), 0.0)
        fz = flux(k, k_z, v, v_z)
        fz_in = jnp.where(z > 0, roll(fz, 1, 0), -0.5 * k * v)
        yield i, k, v, src[i] - after + before - fy + roll(fy, 1, 1) - fz + fz_in
        before = after


def residual_kernel(flags, it_in, src_in, lab_in, out_ref, n_ref, pool, k_ref, a_ref, it, src, lab, sems, done_sems):
    copies = []
    for part in range(PARTS):
        rows = pl.ds(part * ROWS // PARTS, ROWS // PARTS)
        copies.append(
            [
                pltpu.make_async_copy(a.at[rows], b.at[rows], sems.at[n, part])
                for n, (a, b) in enumerate(((lab_in, lab), (it_in, it), (src_in, src)))
            ]
        )
        for copy in copies[-1]:
            copy.start()

    def arrive(row):
        part, within = divmod(row, ROWS // PARTS)
        if within or part == PARTS:
            return
        for copy in copies[part]:
            copy.wait()
        for i in range(row, row + ROWS // PARTS):
            k_ref[i] = conduct(lab[i])

    arrive(0)
    lane = iota((NZ, LANES), 1)
    zero = jnp.zeros((NZ, LANES), F32)
    up = dn = zero
    low, high = {}, {}
    for i, k, v, r in residual_rows(k_ref, it, src, arrive):
        if i < 3:
            low[i] = r
        if i >= ROWS - 3:
            high[i - ROWS + 3] = r
        j = i // 2
        if i % 2 == 0:
            r_even, k_even = r, k
        else:
            pool[0, j] = r_even + r
            pool[1, j] = k_even + k
        off = 8 * i
        here = (lane >= off) & (lane < off + 8)
        top = jnp.where(lane >= 124, k, jnp.where(lane >= 121, roll(r, -4, 1), roll(v, -7, 1)))
        bottom = jnp.where(lane < 4, k, jnp.where(lane < 7, roll(r, 4, 1), roll(v, 7, 1)))
        up = jnp.where(here, roll(top, off - 120, 1), up)
        dn = jnp.where(here, roll(bottom, off, 1), dn)
    a_ref[UP:UP + NZ] = up
    a_ref[DN:DN + NZ] = dn
    up = dn = zero
    for g, edge in enumerate((k_ref[0], it[0], k_ref[ROWS - 1], it[ROWS - 1])):
        here = (lane >= 32 * g) & (lane < 32 * g + 32)
        up = jnp.where(here, roll(edge, 32 * g - 96, 1), up)
        dn = jnp.where(here, roll(edge, 32 * g, 1), dn)
    a_ref[UP + NZ:UP + 2 * NZ] = up
    a_ref[DN + NZ:DN + 2 * NZ] = dn
    first = flags[0] == 0
    lows = [k_ref[t] for t in range(4)] + [low[t] for t in range(3)] + [it[0]]
    highs = [k_ref[ROWS - 4 + t] for t in range(4)] + [high[t] for t in range(3)] + [it[ROWS - 1]]
    for t in range(8):
        a_ref[FACING + NZ * t:FACING + NZ * (t + 1)] = jnp.where(first, highs[t], lows[t])
        n_ref[NZ * t:NZ * (t + 1)] = jnp.where(first, lows[t], highs[t])
    sent = []

    def send(start, rows):
        at = pl.ds(start, rows)
        sent.append(pltpu.make_async_copy(a_ref.at[at], out_ref.at[at], done_sems.at[len(sent)]))
        sent[-1].start()

    send(FACING, 8 * NZ)
    send(UP, 2 * NZ)
    send(DN, 2 * NZ)
    tops = pool[:, :, pl.ds(0, CZ, stride=2), :] + pool[:, :, pl.ds(1, CZ, stride=2), :]
    child, parent = iota((LANES, LANES), 0) // 2, iota((LANES, LANES), 1)
    to_left = jnp.where(child == parent, F32(1.0), F32(0.0))
    to_right = jnp.where(child == parent - CLANES, F32(0.125), F32(0.0))
    held = tops[1].reshape(CROWS * CZ, LANES).astype(jnp.bfloat16)
    coarse = jnp.dot(held, to_right.astype(jnp.bfloat16), preferred_element_type=F32)
    coarse = dot(tops[0].reshape(CROWS * CZ, LANES), to_left) + coarse
    a_ref[0:OWN] = coarse
    coarse = coarse.reshape(CROWS, CZ, LANES)
    lane = iota((CZ, LANES), 1)
    for t in range(2):
        up = dn = jnp.zeros((CZ, LANES), F32)
        for j in range(4 * t, 4 * t + 4):
            row = coarse[j]
            off = (j % 4) * 32
            at_r = (lane >= off) & (lane < off + 16)
            at_k = (lane >= off + 16) & (lane < off + 32)
            up = jnp.where(at_r, roll(row, off - 48, 1), jnp.where(at_k, roll(row, off + 16 - 112, 1), up))
            dn = jnp.where(at_r, roll(row, off, 1), jnp.where(at_k, roll(row, off + 16 - 64, 1), dn))
        a_ref[UP + 2 * NZ + CZ * t:UP + 2 * NZ + CZ * (t + 1)] = up
        a_ref[DN + 2 * NZ + CZ * t:DN + 2 * NZ + CZ * (t + 1)] = dn
    send(0, OWN)
    send(UP + 2 * NZ, 2 * CZ)
    send(DN + 2 * NZ, 2 * CZ)
    for copy in sent:
        copy.wait()


def strip_flux(up, dn):
    lane = iota(up.shape, 1)
    face = flux(roll(up, -7, 1), dn, up, roll(dn, -7, 1))
    return jnp.where(lane % 8 == 0, face, 0.0)


def came(flags, strips, n, start, rows):
    at = slice(STRIP * n + start, STRIP * n + start + rows)
    rd = strips[flags[5], at] * flags[7].astype(F32)
    return rd, strips[1 - flags[5], at] * flags[6].astype(F32)


def completed(ou, od, ru, rd):
    right = strip_flux(ou, rd)
    left = strip_flux(ru, od)
    return rd + roll(right, 4, 1), ru - roll(left, 3, 1), right, left


def beside_rows(flags, strips, n, ks, rs, v, done, top):
    lane = iota((NZ, LANES), 1)
    dn, up, right, left = done
    k_row, r_row = (ROWS - 4, ROWS - 3) if top else (0, 0)
    tiles = list(ks)
    for t in range(3):
        i = r_row + t
        r = rs[t] - jnp.where(lane == 127, roll(right, 127 - 8 * i, 1), 0.0)
        tiles.append(r + jnp.where(lane == 0, roll(left, -8 * i, 1), 0.0))
    tiles.append(v)
    tiles.append(jnp.where(lane < 32, roll(dn, -8 * k_row, 1), roll(up, 32 - 8 * k_row, 1)))
    tiles.append(outermost(flags, strips, n, top))
    return tiles


def outermost(flags, strips, n, top):
    lane = iota((NZ, LANES), 1)
    shift = 64 if top else 0
    rd, ru = came(flags, strips, n, NZ, NZ)
    return jnp.where(lane < 64, roll(rd, -shift, 1), roll(ru, 64 - shift, 1))


def edge_flux(a, b, pool):
    pool[0] = flux(a(3), b(0), a(7), b(7))
    u, w = a(9), b(9)
    pool[1] = flux(u, w, roll(u, -32, 1), roll(w, -32, 1))
    sums = pool[:, pl.ds(0, CZ, stride=2), :] + pool[:, pl.ds(1, CZ, stride=2), :]
    child, parent = iota((LANES, LANES), 0), iota((LANES, LANES), 1)
    own = jnp.where(child // 2 == parent, F32(1.0), F32(0.0))
    right = (child < 32) & (child // 2 + 64 == parent)
    left = (child >= 64) & (child < 96) & (child // 2 + 80 == parent)
    beyond = jnp.where(right | left, F32(1.0), F32(0.0))
    return dot(sums[0], own) + dot(sums[1], beyond)


def chip_kernel(flags, near, pair, strips, o_ref, pool):
    first = flags[0] == 0
    lane = iota((CZ, LANES), 1)
    nears = []
    for n in range(2):
        rd, ru = came(flags, strips, n, 0, NZ)
        done = completed(pair[n, UP:UP + NZ], pair[n, DN:DN + NZ], ru, rd)
        pool[0] = done[2] + roll(done[2], -8, 1)
        pool[1] = done[3] + roll(done[3], -8, 1)
        sums = pool[:, pl.ds(0, CZ, stride=2), :] + pool[:, pl.ds(1, CZ, stride=2), :]
        base = BLOCK * n
        for j in range(CROWS):
            value = pair[n, CZ * j:CZ * (j + 1)] - jnp.where(lane == 63, roll(sums[0], 63 - 16 * j, 1), 0.0)
            value = value + jnp.where(lane == 0, roll(sums[1], -16 * j, 1), 0.0)
            o_ref[base + CZ * j:base + CZ * (j + 1)] = value
        for t in range(2):
            more, less = came(flags, strips, n, 2 * NZ + CZ * t, CZ)
            for q in range(4):
                src = 16 * (4 * t + q)
                more = more + jnp.where(lane == 32 * q, roll(sums[0], 32 * q - src, 1), 0.0)
                less = less - jnp.where(lane == 32 * q + 15, roll(sums[1], 32 * q + 15 - src, 1), 0.0)
            o_ref[base + OWN + CZ * t:base + OWN + CZ * (t + 1)] = more
            o_ref[base + OWN + CZ * (2 + t):base + OWN + CZ * (3 + t)] = less
        rows = [near[NZ * t:NZ * (t + 1)] for t in range(8)]
        nears.append(beside_rows(flags, strips, n, rows[0:4], rows[4:7], rows[7], done, n == 1))
    for t in range(10):
        o_ref[2 * BLOCK + NZ * t:2 * BLOCK + NZ * (t + 1)] = jnp.where(first, nears[0][t], nears[1][t])

    def tile(n):
        def get(t):
            if t == 9:
                return outermost(flags, strips, n, n == 0)
            return pair[n, FACING + NZ * t:FACING + NZ * (t + 1)]

        return get

    inner = edge_flux(tile(0), tile(1), pool)
    for n, j in ((0, CROWS - 1), (1, 0)):
        change = inner if n else -inner
        off = 32 * (j % 4)
        side = (lane >= off) & (lane < off + 16)
        changes = (
            (CZ * j, jnp.where(lane < CLANES, change, 0.0)),
            (OWN + CZ * (j // 4), jnp.where(side, roll(change, off - 64, 1), 0.0)),
            (OWN + CZ * (2 + j // 4), jnp.where(side, roll(change, off - 112, 1), 0.0)),
        )
        for at, part in changes:
            at = BLOCK * n + at
            o_ref[at:at + CZ] = o_ref[at:at + CZ] + part


def relay_kernel(flags, out, o_ref, pool):
    first = flags[0] == 0
    low, high = flags[1].astype(F32), flags[2].astype(F32)

    def tile(n, valid):
        return lambda t: out[n, 2 * BLOCK + NZ * t:2 * BLOCK + NZ * (t + 1)] * valid

    outer = edge_flux(tile(0, low), tile(1, high), pool)
    o_ref[0:BLOCK] = jnp.where(first, out[0, BLOCK:2 * BLOCK] * low, out[1, 0:BLOCK] * high)
    o_ref[BLOCK:] = outer


def sweep(lo, hi, mid, shift, sweeps, r_s, s_s, x_s, c_s, width):
    start, pairs = weights(sweeps)
    for n in range(1, sweeps):
        keep, add = pairs[n - 1]
        prev, here = s_s[lo + n - 1], s_s[lo + n]
        for i in range(lo + n, hi - n):
            ahead = s_s[i + 1]
            total = c_s[0, i] * ahead + c_s[1, i] * prev
            total = total + c_s[2, i] * roll(here, -1, 0) + c_s[3, i] * roll(here, 1, 0)
            total = total + c_s[4, i] * roll(here, -1, 1) + c_s[5, i] * roll(here, 1, 1)
            r = r_s[i] - (here - total)
            step = keep * here + add * r
            r_s[i] = r
            s_s[i] = step
            if shift <= i < shift + mid:
                x_s[i - shift] = x_s[i - shift] + (step[:, 0:width] if width else step)
            prev, here = here, ahead


def prepare(rows, mid, shift, sweeps, factor, k_s, r_s, s_s, x_s, c_s, width):
    depth = k_s.shape[1]
    z = iota(k_s.shape[1:], 0)
    start, _ = weights(sweeps)
    below = factor * (k_s[0] + k_s[1])
    for i in range(1, rows - 1):
        k = k_s[i]
        above = factor * (k + k_s[i + 1])
        z_up = factor * (k + jnp.where(z < depth - 1, roll(k, -1, 0), 0.0))
        z_dn = factor * (k + jnp.where(z > 0, roll(k, 1, 0), 0.0))
        y_up = factor * (k + roll(k, -1, 1))
        y_dn = factor * (k + roll(k, 1, 1))
        diagonal = above + below + z_up + z_dn + y_up + y_dn
        inverse = jnp.where(k > 0, 1.0 / jnp.where(k > 0, diagonal, 1.0), 0.0)
        c_s[0, i] = inverse * above
        c_s[1, i] = inverse * below
        c_s[2, i] = jnp.where(z < depth - 1, inverse * z_up, 0.0)
        c_s[3, i] = jnp.where(z > 0, inverse * z_dn, 0.0)
        c_s[4, i] = inverse * y_up
        c_s[5, i] = inverse * y_dn
        r = inverse * r_s[i]
        r_s[i] = r
        s_s[i] = r * start
        if shift <= i < shift + mid:
            x_s[i - shift] = (r[:, 0:width] if width else r) * start
        below = above


def coarse_part(flags, chip, out, near, x_s, k_s, r_s, s_s, c_s):
    first = flags[0] == 0
    low, high = flags[3].astype(F32), flags[4].astype(F32)
    own = near[flags[0], BLOCK:]
    other = near[1 - flags[0], BLOCK:]
    f_low = jnp.where(first, own, other)
    f_high = jnp.where(first, other, own)
    lane = iota((CZ, LANES), 1)

    def packed(at):
        up = slice(BLOCK + at.start, BLOCK + at.stop)
        return (
            jnp.where(first, out[0, at] * low, near[0, at]),
            jnp.where(first, out[0, up] * low, chip[at]),
            jnp.where(first, chip[at], chip[up]),
            jnp.where(first, chip[up], out[1, at] * high),
            jnp.where(first, near[1, at], out[1, up] * high),
        )

    sides = [packed(slice(OWN + CZ * t, OWN + CZ * (t + 1))) for t in range(4)]
    for j in range(CROWS):
        off = 32 * (j % 4)
        rows = packed(slice(CZ * j, CZ * (j + 1)))
        for b in range(5):
            more, less = sides[j // 4][b], sides[2 + j // 4][b]
            for n, dest in enumerate((r_s, k_s)):
                value = jnp.where(lane < CLANES, roll(rows[b], -CLANES * n, 1), 0.0)
                value = jnp.where((lane >= 64) & (lane < 80), roll(more, 64 - off - 16 * n, 1), value)
                dest[CROWS * b + j] = jnp.where(lane >= 112, roll(less, 112 - off - 16 * n, 1), value)
    low_at, high_at = jnp.where(first, 16, 8), jnp.where(first, 32, 24)
    r_s[low_at - 1] = r_s[low_at - 1] - f_low
    r_s[low_at] = r_s[low_at] + f_low
    r_s[high_at - 1] = r_s[high_at - 1] - f_high
    r_s[high_at] = r_s[high_at] + f_high
    zero = jnp.zeros((CZ, LANES), F32)
    s_s[0] = zero
    s_s[CEXT - 1] = zero
    prepare(CEXT, CROWS, COARSE_SWEEPS, COARSE_SWEEPS, 2.0, k_s, r_s, s_s, x_s, c_s, 0)
    sweep(1, CEXT - 1, CROWS, COARSE_SWEEPS, COARSE_SWEEPS, r_s, s_s, x_s, c_s, 0)


def fine_part(flags, it, src, lab, pair, strips, out, k_in, r_in, x_s, k_s, r_s, s_s, c_s):
    first = flags[0] == 0
    low, high = flags[1].astype(F32), flags[2].astype(F32)
    lane = iota((NZ, LANES), 1)
    for i in range(ROWS):
        k_in[i] = conduct(lab[i])
    for i, _, _, r in residual_rows(k_in, it, src):
        r_in[i] = r
    facing = []
    for n in range(2):
        rd, ru = came(flags, strips, n, 0, NZ)
        done = completed(pair[n, UP:UP + NZ], pair[n, DN:DN + NZ], ru, rd)
        rows = [pair[n, FACING + NZ * t:FACING + NZ * (t + 1)] for t in range(8)]
        facing.append(beside_rows(flags, strips, n, rows[0:4], rows[4:7], rows[7], done, n == 0))
    mine = flags[0]
    rd, ru = (jnp.where(first, a, b) for a, b in zip(came(flags, strips, 0, 0, NZ), came(flags, strips, 1, 0, NZ)))
    dn, up, right, left = completed(pair[mine, UP:UP + NZ], pair[mine, DN:DN + NZ], ru, rd)

    def beside(rights, lefts, count):
        return jnp.where(lane < count, rights, jnp.where(lane >= LANES - count, lefts, 0.0))

    def join(a, b):
        return jnp.concatenate([a, b], axis=1)

    for i in range(ROWS):
        off = 8 * i
        e = HALO + i
        k_s[e, :, 0:LANES] = k_in[i]
        k_s[e, :, LANES:] = beside(roll(dn, -off, 1), roll(up, 120 - off, 1), 4)
        r = r_in[i] - jnp.where(lane == 127, roll(right, 127 - off, 1), 0.0)
        r_s[e, :, 0:LANES] = r + jnp.where(lane == 0, roll(left, -off, 1), 0.0)
        r_s[e, :, LANES:] = beside(roll(dn, -off - 4, 1), roll(up, 124 - off, 1), 3)
    edges = [jnp.where(first, a, b) for a, b in zip(came(flags, strips, 0, NZ, NZ), came(flags, strips, 1, NZ, NZ))]
    for side in range(2):
        def tile(t, side=side):
            at = slice(2 * BLOCK + NZ * t, 2 * BLOCK + NZ * (t + 1))
            if side == 0:
                return jnp.where(first, out[0, at], facing[0][t]) * low
            return jnp.where(first, facing[1][t], out[1, at]) * high

        base = 0 if side == 0 else HALO + ROWS
        halo, face = tile(8), tile(9)
        for q in range(4):
            k_s[base + q, :, 0:LANES] = tile(q)
            k_s[base + q, :, LANES:] = beside(roll(halo, -8 * q, 1), roll(halo, 88 - 8 * q, 1), 4)
        for t in range(3):
            q = t + 1 - side
            r_s[base + q, :, 0:LANES] = tile(4 + t)
            r_s[base + q, :, LANES:] = beside(roll(halo, -8 * q - 4, 1), roll(halo, 92 - 8 * q, 1), 3)
        v_out = join(tile(7), beside(roll(face, -32, 1), face, 4))
        if side == 0:
            v_in = join(it[0], beside(roll(edges[0], -32, 1), roll(edges[1], 64, 1), 4))
            through = flux(k_s[HALO - 1], k_s[HALO], v_out, v_in)
            r_s[HALO - 1] = r_s[HALO - 1] - through
            r_s[HALO] = r_s[HALO] + through
        else:
            v_in = join(it[ROWS - 1], beside(roll(edges[0], -96, 1), edges[1], 4))
            through = flux(k_s[HALO + ROWS - 1], k_s[HALO + ROWS], v_in, v_out)
            r_s[HALO + ROWS - 1] = r_s[HALO + ROWS - 1] - through
            r_s[HALO + ROWS] = r_s[HALO + ROWS] + through
    zero = jnp.zeros((NZ, 2 * LANES), F32)
    s_s[0] = zero
    s_s[EXT - 1] = zero
    prepare(EXT, ROWS, HALO, SWEEPS, 0.5, k_s, r_s, s_s, x_s, c_s, LANES)
    sweep(1, EXT - 1, ROWS, HALO, SWEEPS, r_s, s_s, x_s, c_s, LANES)


def coarse_kernel(flags, chip, out, near, x_ref, p_ref, k_s, r_s, s_s, c_s):
    coarse_part(flags, chip, out, near, x_ref, k_s, r_s, s_s, c_s)
    lane = iota((CZ, LANES), 1)
    for a in range(4):
        p_ref[pl.ds(a, CZ, stride=4), :] = jnp.where(lane < CLANES, x_ref[a], roll(x_ref[a + 4], CLANES, 1))


def fine_kernel(
    flags, it, src, lab, pair, strips, out, x_c, o_ref, k_in, r_in, x_f, k_f, r_f, s_f, c_f, wide_s
):
    fine_part(flags, it, src, lab, pair, strips, out, k_in, r_in, x_f, k_f, r_f, s_f, c_f)
    child, parent = iota((LANES, LANES), 1) // 2, iota((LANES, LANES), 0)
    spread = jnp.where(child == parent, F32(1.0), F32(0.0))
    wide = dot(x_c[...].reshape(CROWS * CZ, LANES), spread).reshape(CROWS, CZ, LANES)
    wide_s[:, pl.ds(0, CZ, stride=2), :] = wide
    wide_s[:, pl.ds(1, CZ, stride=2), :] = wide
    for i in range(ROWS):
        o_ref[i] = it[i] + x_f[i] + wide_s[i // 2]


def planes_kernel(sources, planes, p_ref, o_ref):
    half = sources // 2
    lane = iota((half, LANES), 1)
    for q in range(planes):
        for a in range(4):
            even = p_ref[pl.ds(4 * q + a, half, stride=8 * planes), :]
            odd = p_ref[pl.ds(4 * (planes + q) + a, half, stride=8 * planes), :]
            to = (a * planes + q) * half
            o_ref[to:to + half] = jnp.where(lane < CLANES, even, roll(odd, CLANES, 1))
            to = ((a + 4) * planes + q) * half
            o_ref[to:to + half] = jnp.where(lane < CLANES, roll(even, CLANES, 1), odd)


def place():
    gx, gy = lax.axis_index("gx"), lax.axis_index("gy")
    n_gx, n_gy = lax.axis_size("gx"), lax.axis_size("gy")
    marks = [gx % 2, gx > 0, gx < n_gx - 1, gx > 1, gx < n_gx - 2, gy % 2, gy > 0, gy < n_gy - 1]
    return [m.astype(jnp.int32) for m in marks]


def call(kernel, outs, scratch, placed=False, operands=(), flops=1000000, copies=False):
    vmem = pl.BlockSpec(memory_space=pltpu.VMEM)
    specs = [pl.BlockSpec(memory_space=pltpu.HBM) if copies else vmem] * len(operands)
    size = sum(4 * x.size for x in operands) + sum(4 * o.size for o in outs)
    multiple = len(outs) > 1
    held = [pltpu.VMEM(s, F32) for s in scratch]
    out_specs = [vmem] * len(outs)
    if copies:
        out_specs[0] = pl.BlockSpec(memory_space=pltpu.HBM)
        held += [pltpu.VMEM(x.shape, x.dtype) for x in operands]
        held.append(pltpu.SemaphoreType.DMA((len(operands), PARTS)))
        held.append(pltpu.SemaphoreType.DMA((6,)))

    def body(*refs):
        if placed:
            kernel(place(), *refs)
        else:
            kernel(*refs)

    return pl.pallas_call(
        body,
        out_shape=outs if multiple else outs[0],
        in_specs=specs,
        out_specs=out_specs if multiple else out_specs[0],
        scratch_shapes=held,
        compiler_params=pltpu.CompilerParams(vmem_limit_bytes=(54900 if copies else 40960) * 1024),
        cost_estimate=pl.CostEstimate(flops=flops, bytes_accessed=size, transcendentals=0),
    )(*operands)


def shape(*dims):
    return jax.ShapeDtypeStruct(dims, F32)


def on_device(iterate, source, labels):
    n_gx, n_gy = lax.axis_size("gx"), lax.axis_size("gy")
    gx = lax.axis_index("gx")
    gy = lax.axis_index("gy")
    chips = [[i, i + 1] for i in range(0, n_gx, 2)]
    between = [[i, (i + 1) % n_gx] for i in range(1, n_gx, 2)]
    along = [
        [i * n_gy + j, i * n_gy + (j + 1) % n_gy] for i in range(n_gx) for j in range(i % 2, n_gy, 2)
    ]
    own = shape(ROWS, NZ, LANES)
    shared, near = call(
        residual_kernel,
        [shape(SHARED, LANES), shape(8 * NZ, LANES)],
        [(2, CROWS, NZ, LANES), own.shape, (SHARED, LANES)],
        True,
        (iterate, source, labels),
        copies=True,
    )
    pair = lax.all_gather(shared, "gx", axis_index_groups=chips)
    lower = (gx + gy) % 2 == 0
    strips = jnp.where(lower, pair[:, UP:DN], pair[:, DN:FACING]).reshape(2 * STRIP, LANES)
    strips = lax.all_gather(strips, ("gx", "gy"), axis_index_groups=along)
    strips = lax.all_gather(jnp.where(lower, strips[1], strips[0]), "gx", axis_index_groups=chips)
    chip = call(
        chip_kernel,
        [shape(2 * BLOCK + NEAR, LANES)],
        [(2, NZ, LANES)],
        True,
        (near, pair, strips),
    )
    beyond = lax.all_gather(chip, "gx", axis_index_groups=between)
    relay = call(relay_kernel, [shape(BLOCK + CZ, LANES)], [(2, NZ, LANES)], True, (beyond,))
    relay = lax.all_gather(relay, "gx", axis_index_groups=chips)
    rows, wide = (CEXT, CZ, LANES), (EXT, NZ, 2 * LANES)
    coarse_out, planes = call(
        coarse_kernel,
        [shape(CROWS, CZ, LANES), shape(4 * CZ, LANES)],
        [rows, rows, rows, (6, *rows)],
        True,
        (chip, beyond, relay),
    )
    per = CZ // n_gy
    planes = lax.all_to_all(planes.reshape(n_gy, 4 * per, LANES), "gy", split_axis=0, concat_axis=0, tiled=True)
    corrected = call(
        fine_kernel,
        [own],
        [own.shape, own.shape, own.shape, wide, wide, wide, (6, *wide), (CROWS, NZ, LANES)],
        True,
        (iterate, source, labels, pair, strips, beyond, coarse_out),
        flops=20000000,
    )
    owned = call(
        functools.partial(planes_kernel, n_gy, per),
        [shape(4 * CZ, LANES)],
        [],
        False,
        (planes.reshape(4 * CZ, LANES),),
    ).reshape(CROWS, per, CLANES * n_gy)
    return corrected, owned


def solution(mesh):
    spec = P("gx", None, "gy")
    return jax.shard_map(
        on_device, mesh=mesh, in_specs=(spec, spec, spec), out_specs=(spec, P("gx", "gy", None)), check_vma=False
    )
```
